32 devices in a mesh: dp: 16 (over z, x, core), seq: 2 (over y).
Axes of the slice: x: 2, y: 2, z: 4, core: 2. Of those that a mesh axis runs over, the one named last changes fastest.
Arguments:
- tokens: bfloat16 [16, 1024, 1024], P('dp', 'seq'), may hold values from -6 to 6
- time_index: int32 [16], P('dp'), may hold values from 0 to 999
- lengths: int32 [16], P('dp'), may hold values from 32 to 1024, as said below
- time_weight: bfloat16 [1024, 4096], replicated, may hold values from -0.09375 to 0.09375
- time_bias: float32 [4096], replicated, may hold values from -3 to 3
- attend_gain: float32 [1024], replicated, may hold values from 0.25 to 1.75
- query_key_value_weight: bfloat16 [1024, 3072], replicated, may hold values from -0.1875 to 0.1875
- attention_output_weight: bfloat16 [1024, 1024], replicated, may hold values from -1 to 1
- attend_bias: float32 [1024], replicated, may hold values from -3 to 3
- dense_gain: float32 [1024], replicated, may hold values from 0.25 to 1.75
- feedforward_up_matrix: bfloat16 [1024, 4096], replicated, may hold values from -0.1875 to 0.1875
- up_bias: float32 [4096], replicated, may hold values from -3 to 3
- feedforward_down_matrix: bfloat16 [4096, 1024], replicated, may hold values from -0.09375 to 0.09375
- down_bias: float32 [1024], replicated, may hold values from -3 to 3
- cotangent: bfloat16 [16, 1024, 1024], P('dp', 'seq'), may hold values from -6 to 6
Outputs:
- result: bfloat16 [16, 1024, 1024], P('dp', 'seq')
- gradient_tokens: bfloat16 [16, 1024, 1024], P('dp', 'seq')
- gradient_time_weight: float32 [1024, 4096], P('dp')
- gradient_time_bias: float32 [4096], P('dp')
- gradient_attend_gain: float32 [1024], P('dp')
- gradient_attend_in: float32 [1024, 3072], P('dp')
- gradient_attend_out: float32 [1024, 1024], P('dp')
- gradient_attend_bias: float32 [1024], P('dp')
- gradient_dense_gain: float32 [1024], P('dp')
- gradient_up_weight: float32 [1024, 4096], P('dp')
- gradient_up_bias: float32 [4096], P('dp')
- gradient_down_weight: float32 [4096, 1024], P('dp')
- gradient_down_bias: float32 [1024], P('dp')
The draws below stay inside these ranges and needn't reach their ends.
Inputs may be any that keep to these rules, and one draw needn't show every extreme that they name: A sequence's live tokens are its first lengths slots; in every draw some sequence has all 1024 slots live.
All inputs are finite; a program needn't handle non-finite values.
Results may differ from the reference program's by a relative error of at most 0.024.
Values may be sent and summed in bfloat16 or wider, within the bound.
No kernel may reach another device: no remote copies, remote signals or barrier semaphores. Data moves between devices by JAX's collectives and lax.ppermute only.
A program may use at most 256 MiB of HBM per device.

```python
import math
import jax
import jax.numpy as jnp
from jax import lax

D = 1024
H = 16
HD = 64
FF = 4096
L = 1024
LMIN = 32
NT = 1000
SEQS = 16


def draw_lengths(key, part):
    picks = jax.random.randint(key, (SEQS,), LMIN, L + 1)
    chosen = jax.random.randint(jax.random.fold_in(key, 7), (), 0, SEQS)
    return jnp.where(jnp.arange(SEQS) == chosen, L, picks).astype(jnp.int32)


def plant(result, key, least, top_value):
    longest = result.shape.index(max(result.shape))
    spots = []
    for shift in (0, 1):
        where = [jax.random.randint(jax.random.fold_in(key, axis), (), 0, length) for axis, length in enumerate(result.shape)]
        where[longest] = (where[longest] + shift) % result.shape[longest]
        spots.append(tuple(where))
    return result.at[spots[0]].set(least).at[spots[1]].set(top_value)


def spiked(drawn, key, source, target, shards_of, factor):
    owner, partner = [(jnp.arange(drawn.shape[dim]) // (drawn.shape[dim] // shards_of)).reshape([-1 if axis == dim else 1 for axis in range(drawn.ndim)]) for dim in (source, target)]
    chosen = jax.random.permutation(key, shards_of)[partner]
    strong = (owner == chosen) | (owner == (partner + shards_of // 2) % shards_of)
    return jnp.where(strong, factor * drawn, drawn)


def levels(stream_key, shape, cuts, low, top_value):
    factor_of, own = 1.0, jax.random.fold_in(stream_key, 6)
    for dim, shards_of in cuts:
        heights = jnp.exp(jax.random.uniform(jax.random.fold_in(own, dim), (shards_of,), jnp.float32, low / len(cuts), top_value / len(cuts)))
        factor_of = factor_of * jnp.repeat(heights, shape[dim] // shards_of).reshape([-1 if axis == dim else 1 for axis in range(len(shape))])
    return factor_of


def gaussian(own_key, shape, scale, bound, shards=(), kind=jnp.bfloat16):
    values = scale * jax.random.normal(own_key, shape, jnp.float32)
    if shards:
        values = values * levels(own_key, shape, shards, -0.22, 0.18)
    return jnp.clip(values, -bound, bound).astype(kind)


def noise_with(stream_key, dims, scale, reach, split, heavy, held_as=jnp.bfloat16):
    result = scale * jax.random.normal(stream_key, dims, jnp.float32)
    if split:
        result = result * levels(stream_key, dims, split, -0.22, 0.18)
    return jnp.clip(spiked(result, jax.random.fold_in(stream_key, 3), *heavy), -reach, reach).astype(held_as)


def setup_inputs(seed: int = 0) -> dict:
    keys = jax.random.split(jax.random.key(seed), 16)
    return {
        "tokens": gaussian(keys[0], (SEQS, L, D), 1.0, 6.0, ((0, 16), (1, 2))),
        "time_index": plant(jax.random.randint(keys[1], (SEQS,), 0, NT), jax.random.fold_in(keys[1], 1), 0, NT - 1).astype(jnp.int32),
        "lengths": draw_lengths(jax.random.fold_in(keys[15], 71), 0),
        "time_weight": gaussian(keys[3], (D, 4 * D), (4 * D) ** -0.5, 0.09375),
        "time_bias": gaussian(keys[4], (4 * D,), 0.5, 3.0, (), jnp.float32),
        "attend_gain": jnp.clip(1.0 + 0.15 * jax.random.normal(keys[5], (D,), jnp.float32), 0.25, 1.75),
        "query_key_value_weight": gaussian(keys[6], (D, 3 * D), D ** -0.5, 0.1875),
        "attention_output_weight": gaussian(keys[7], (D, D), (D // 32) ** -0.5, 1.0),
        "attend_bias": gaussian(keys[8], (D,), 0.5, 3.0, (), jnp.float32),
        "dense_gain": jnp.clip(1.0 + 0.15 * jax.random.normal(keys[9], (D,), jnp.float32), 0.25, 1.75),
        "feedforward_up_matrix": gaussian(keys[10], (D, FF), D ** -0.5, 0.1875),
        "up_bias": gaussian(keys[11], (FF,), 0.5, 3.0, (), jnp.float32),
        "feedforward_down_matrix": gaussian(keys[12], (FF, D), FF ** -0.5, 0.09375),
        "down_bias": gaussian(keys[13], (D,), 0.5, 3.0, (), jnp.float32),
        "cotangent": noise_with(keys[14], (SEQS, L, D), 1.0, 6.0, ((0, 16), (1, 2)), (0, 2, 16, 2.0)),
    }


epsilon = 1e-05
masked_score = -1e+30

@jax.custom_vjp
def low(v):
    return lax.optimization_barrier(v.astype(jnp.bfloat16)).astype(jnp.float32)

@jax.custom_vjp
def low_back(v):
    return v

def low_keep(v):
    return (low(v), None)

def low_pass(kept, grad):
    return (grad,)

def back_keep(v):
    return (v, None)

def back_low(kept, grad):
    return (low(grad),)
low.defvjp(low_keep, low_pass)
low_back.defvjp(back_keep, back_low)

def sinus_table(time_index, width):
    halfway = width // 2
    rates = jnp.exp(-math.log(10000.0) * jnp.arange(halfway, dtype=jnp.float32) / halfway)
    angles = time_index.astype(jnp.float32)[:, None] * rates[None, :]
    return jnp.concatenate([jnp.sin(angles), jnp.cos(angles)], axis=-1)

def normalize(values):
    centre = values - lax.optimization_barrier(jnp.mean(values, axis=-1, keepdims=True))
    return centre * lax.rsqrt(lax.optimization_barrier(jnp.mean(centre * centre, axis=-1, keepdims=True)) + epsilon)

def attend(packet):
    projected, length = packet
    queries = projected[:, 0:D].reshape(L, H, HD)
    keyset = projected[:, D:2 * D].reshape(L, H, HD)
    valueset = projected[:, 2 * D:3 * D].reshape(L, H, HD)
    scores = low_back(jnp.einsum('qhd,khd->hqk', queries, keyset, precision=lax.Precision.HIGHEST) * HD ** (-0.5))
    usable = jnp.arange(L) < length
    scores = jnp.where(usable[None, None, :], scores, masked_score)
    highest = lax.optimization_barrier(jnp.max(scores, axis=-1, keepdims=True))
    weights = jnp.exp(scores - highest)
    probability = low(weights / lax.optimization_barrier(jnp.sum(weights, axis=-1, keepdims=True)))
    attention_mixture = jnp.einsum('hqk,khd->qhd', probability, valueset, precision=lax.Precision.HIGHEST)
    return low(low_back(attention_mixture.reshape(L, D)))

def forward(features, table_low, live_rows, lengths, time_weight, time_bias, attend_gain, query_key_value_weight, attention_output_weight, attend_bias, dense_gain, feedforward_up_matrix, up_bias, feedforward_down_matrix, down_bias):
    highest = lax.Precision.HIGHEST
    condition = jnp.dot(table_low, time_weight, precision=highest) + time_bias
    scale_attend = condition[:, None, 0:D]
    shift_attend = condition[:, None, D:2 * D]
    scale_dense = condition[:, None, 2 * D:3 * D]
    shift_dense = condition[:, None, 3 * D:4 * D]
    attention_activation = low(normalize(features) * attend_gain * (1.0 + scale_attend) + shift_attend)
    projected = low(low_back(jnp.einsum('bld,de->ble', attention_activation, query_key_value_weight, precision=highest)))
    attention_mixture = lax.map(jax.checkpoint(attend), (projected, lengths))
    attended = low_back(jnp.einsum('bld,de->ble', attention_mixture, attention_output_weight, precision=highest) + attend_bias)
    residual = features + live_rows * attended
    dense_activation = low(normalize(residual) * dense_gain * (1.0 + scale_dense) + shift_dense)
    raised = low_back(jnp.einsum('bld,df->blf', dense_activation, feedforward_up_matrix, precision=highest) + up_bias)
    hidden_state = low(jax.nn.gelu(raised, approximate=False))
    branch = low_back(jnp.einsum('blf,fd->bld', hidden_state, feedforward_down_matrix, precision=highest) + down_bias)
    return residual + live_rows * branch

def reference(tokens, time_index, lengths, time_weight, time_bias, attend_gain, query_key_value_weight, attention_output_weight, attend_bias, dense_gain, feedforward_up_matrix, up_bias, feedforward_down_matrix, down_bias, cotangent):
    table_low = low(sinus_table(time_index, D))
    live_rows = (jnp.arange(L)[None, :] < lengths[:, None]).astype(jnp.float32)[:, :, None]

    def run(features, w_one, b_one, g_one, w_two, w_three, b_two, g_two, w_four, b_three, w_five, b_four):
        return forward(features, table_low, live_rows, lengths, w_one, b_one, g_one, w_two, w_three, b_two, g_two, w_four, b_three, w_five, b_four)
    output, pullback = jax.vjp(run, tokens.astype(jnp.float32), time_weight.astype(jnp.float32), time_bias.astype(jnp.float32), attend_gain.astype(jnp.float32), query_key_value_weight.astype(jnp.float32), attention_output_weight.astype(jnp.float32), attend_bias.astype(jnp.float32), dense_gain.astype(jnp.float32), feedforward_up_matrix.astype(jnp.float32), up_bias.astype(jnp.float32), feedforward_down_matrix.astype(jnp.float32), down_bias.astype(jnp.float32))
    grads = pullback(cotangent.astype(jnp.float32))
    return (output.astype(jnp.bfloat16), grads[0].astype(jnp.bfloat16), grads[1], grads[2], grads[3], grads[4], grads[5], grads[6], grads[7], grads[8], grads[9], grads[10], grads[11])
```

```python
import functools
import math

import jax
import jax.numpy as jnp
from jax import lax
from jax.experimental import pallas as pl
from jax.experimental.pallas import tpu as pltpu
from jax.sharding import PartitionSpec as P

HD = 64
EPS = 1e-05
MASKED = -1e30
EXP2_SCALE = math.log2(math.e) * HD ** (-0.5)
BF = jnp.bfloat16
F32 = jnp.float32
VMEM = 56 * 1024 * 1024


def sds(shape, dtype):
    return jax.ShapeDtypeStruct(shape, dtype)


def nt(a, b):
    return lax.dot_general(a, b, (((1,), (1,)), ((), ())), preferred_element_type=F32)


def nn(a, b):
    return jnp.dot(a, b, preferred_element_type=F32)


def tn_dot(a, b):
    return lax.dot_general(a, b, (((0,), (0,)), ((), ())), preferred_element_type=F32)


def call(kernel, name, scalars, grid, ins, in_specs, outs, out_specs, scratch=(), flops=0, aliases=None):
    size = lambda a: math.prod(a.shape) * a.dtype.itemsize
    return pl.pallas_call(
        kernel,
        name=name,
        grid_spec=pltpu.PrefetchScalarGridSpec(
            num_scalar_prefetch=len(scalars),
            grid=grid,
            in_specs=in_specs,
            out_specs=out_specs,
            scratch_shapes=list(scratch),
        ),
        out_shape=outs,
        input_output_aliases=aliases or {},
        compiler_params=pltpu.CompilerParams(
            vmem_limit_bytes=VMEM, dimension_semantics=("arbitrary",) * len(grid)
        ),
        cost_estimate=pl.CostEstimate(
            flops=int(flops),
            bytes_accessed=int(sum(map(size, ins)) + sum(map(size, jax.tree.leaves(outs)))),
            transcendentals=0,
        ),
    )(*scalars, *ins)


def norm_rows(v):
    centre = v - jnp.mean(v, axis=-1, keepdims=True)
    inverse = lax.rsqrt(jnp.mean(centre * centre, axis=-1, keepdims=True) + EPS)
    return centre * inverse, inverse


def live_column(rows, first, info_ref, local, total):
    r = first + lax.broadcasted_iota(jnp.int32, (rows, 1), 0)
    low = lax.rem(r, local)
    start = info_ref[1] - (r - low)
    slot = jnp.where(start < 0, start + total, start) + low
    return slot < info_ref[2]


def project_kernel(info_ref, x_ref, gain_ref, cond_ref, wq_ref, wk_ref, wv_ref, *rest):
    act_ref, qkv_ref = rest[-2:]
    normal, _ = norm_rows(x_ref[...].astype(F32))
    act = (normal * (gain_ref[...] * (1.0 + cond_ref[0:1, :])) + cond_ref[1:2, :]).astype(BF)
    act_ref[...] = act
    w = wq_ref.shape[1]
    for n, ref in enumerate((wq_ref, wk_ref, wv_ref)):
        qkv_ref[:, n * w : (n + 1) * w] = nn(act, ref[...]).astype(BF)


def project(info, x, first, total, gain, cond, weight, before=None):
    rows, width = x.shape
    block = min(256, rows)
    half = weight.shape[1] // 6
    skip = first // block
    weights = [pl.BlockSpec((width, half), lambda i, s, n=n: (0, 2 * n + s[0])) for n in range(3)]
    ins = [x, gain, cond, weight, weight, weight]
    specs = [
        pl.BlockSpec((block, width), lambda i, s: (i, 0)),
        pl.BlockSpec((1, width), lambda i, s: (0, 0)),
        pl.BlockSpec(cond.shape, lambda i, s: (0, 0)),
        *weights,
    ]
    aliases = {}
    if before is not None:
        ins += list(before)
        specs += [pl.BlockSpec(memory_space=pl.ANY)] * 2
        aliases = {7: 0, 8: 1}
    return call(
        project_kernel, "project", (info,), (rows // block,), ins, specs,
        (sds((total, width), BF), sds((total, 3 * half), BF)),
        (
            pl.BlockSpec((block, width), lambda i, s: (i + skip, 0)),
            pl.BlockSpec((block, 3 * half), lambda i, s: (i + skip, 0)),
        ),
        flops=2 * rows * width * 3 * half, aliases=aliases,
    )


def lanes_of(head, lane):
    return (lane < HD) if head == 0 else (lane >= HD), (HD if head == 0 else 0)


def put(lane, spare, inside, values, base):
    out = jnp.where(inside, base, jnp.zeros_like(base))
    for n, value in enumerate(values):
        out = jnp.where(lane == spare + n, value, out)
    return out


def attend_forward_kernel(local, info_ref, q_ref, k_ref, v_ref, o_ref, l_ref, ka, va):
    total = k_ref.shape[0]
    lane = lax.broadcasted_iota(jnp.int32, (1, 2 * HD), 1)

    @pl.when(pl.program_id(1) == 0)
    def _():
        live = live_column(total, 0, info_ref, local, total)
        bias = jnp.where(live, 0.0, MASKED)
        k = k_ref[...].astype(F32)
        v = v_ref[...].astype(F32)
        for head in range(2):
            inside, spare = lanes_of(head, lane)
            ka[head] = put(lane, spare, inside, (bias,), k).astype(BF)
            va[head] = put(lane, spare, inside, (1.0,), v).astype(BF)

    q = q_ref[...].astype(F32)
    results = []
    for head in range(2):
        inside, spare = lanes_of(head, lane)
        qa = put(lane, spare, inside, (1.0,), q).astype(BF)
        scores = nt(qa, ka[head])
        top = jnp.max(scores, axis=-1, keepdims=True)
        weights = jnp.exp2((scores - top) * EXP2_SCALE).astype(BF)
        mixed = nn(weights, va[head])
        sums = mixed[:, spare : spare + 1]
        results.append((mixed / sums, top + jnp.log(sums) * HD**0.5))
    (mixed0, log0), (mixed1, log1) = results
    first = lane < HD
    o_ref[...] = jnp.where(first, mixed0, mixed1).astype(BF)
    l_ref[...] = jnp.where(first, log1, log0)


def attend_forward(info, qkv, local):
    total = qkv.shape[0]
    half = qkv.shape[1] // 3
    pairs = half // (2 * HD)
    block = 256
    return call(
        functools.partial(attend_forward_kernel, local), "attend_forward", (info,), (pairs, total // block),
        [qkv, qkv, qkv],
        [
            pl.BlockSpec((block, 2 * HD), lambda j, i, s: (i, j)),
            pl.BlockSpec((total, 2 * HD), lambda j, i, s: (0, pairs + j)),
            pl.BlockSpec((total, 2 * HD), lambda j, i, s: (0, 2 * pairs + j)),
        ],
        (sds((total, half), BF), sds((total, half), F32)),
        (
            pl.BlockSpec((block, 2 * HD), lambda j, i, s: (i, j)),
            pl.BlockSpec((block, 2 * HD), lambda j, i, s: (i, j)),
        ),
        scratch=[pltpu.VMEM((2, total, 2 * HD), BF), pltpu.VMEM((2, total, 2 * HD), BF)],
        flops=16 * total * total * half,
    )


def attend_backward_kernel(
    local, info_ref, q_ref, g_ref, o_ref, l_ref, k_ref, v_ref, gq_ref, gk_ref, gv_ref, ka, va, kt, acck, accv
):
    total = k_ref.shape[0]
    lane = lax.broadcasted_iota(jnp.int32, (1, 2 * HD), 1)

    @pl.when(pl.program_id(1) == 0)
    def _():
        live = live_column(total, 0, info_ref, local, total)
        bias = jnp.where(live, 0.0, MASKED)
        k = k_ref[...].astype(F32)
        v = v_ref[...].astype(F32)
        for head in range(2):
            inside, spare = lanes_of(head, lane)
            ka[head] = put(lane, spare, inside, (bias, 1.0, 1.0, 1.0), k).astype(BF)
            va[head] = put(lane, spare, inside, (1.0, 1.0), v).astype(BF)
            kt[head] = jnp.where(inside, k, 0.0).astype(BF).T
        acck[...] = jnp.zeros_like(acck)
        accv[...] = jnp.zeros_like(accv)

    q = q_ref[...].astype(F32)
    g = g_ref[...].astype(F32)
    og = o_ref[...].astype(F32) * g
    logs = l_ref[...]
    log_hi = logs.astype(BF).astype(F32)
    log_mid = (logs - log_hi).astype(BF).astype(F32)
    log_low = logs - log_hi - log_mid
    gq_t = None
    for head in range(2):
        inside, spare = lanes_of(head, lane)
        qa = put(lane, spare, inside, (1.0, -log_hi, -log_mid, -log_low), q).astype(BF)
        inner = jnp.sum(jnp.where(inside, og, 0.0), axis=-1, keepdims=True)
        inner_hi = inner.astype(BF).astype(F32)
        ga = put(lane, spare, inside, (-inner_hi, inner_hi - inner), g).astype(BF)
        probability = jnp.exp2(nt(ka[head], qa) * EXP2_SCALE)
        g_scores = (probability * nt(va[head], ga)).astype(BF)
        qm = jnp.where(inside, q, 0.0).astype(BF)
        gm = jnp.where(inside, g, 0.0).astype(BF)
        acck[...] += nn(g_scores, qm)
        accv[...] += nn(probability.astype(BF), gm)
        term = nn(kt[head], g_scores)
        gq_t = term if gq_t is None else gq_t + term
    gq_ref[...] = (gq_t * HD**-0.5).T.astype(BF)

    @pl.when(pl.program_id(1) == pl.num_programs(1) - 1)
    def _():
        gk_ref[...] = (acck[...] * HD**-0.5).astype(BF)
        gv_ref[...] = accv[...].astype(BF)


def attend_backward(info, qkv, g, o, logs, local, first, count):
    total = qkv.shape[0]
    half = qkv.shape[1] // 3
    pairs = half // (2 * HD)
    block = 256
    part = lambda j, i, s: (i, first + j)
    return call(
        functools.partial(attend_backward_kernel, local), "attend_backward", (info,), (count, total // block),
        [qkv, g, o, logs, qkv, qkv],
        [
            pl.BlockSpec((block, 2 * HD), part),
            pl.BlockSpec((block, 2 * HD), part),
            pl.BlockSpec((block, 2 * HD), part),
            pl.BlockSpec((block, 2 * HD), part),
            pl.BlockSpec((total, 2 * HD), lambda j, i, s: (0, pairs + first + j)),
            pl.BlockSpec((total, 2 * HD), lambda j, i, s: (0, 2 * pairs + first + j)),
        ],
        (sds((total, count * 2 * HD), BF),) * 3,
        (
            pl.BlockSpec((block, 2 * HD), lambda j, i, s: (i, j)),
            pl.BlockSpec((total, 2 * HD), lambda j, i, s: (0, j)),
            pl.BlockSpec((total, 2 * HD), lambda j, i, s: (0, j)),
        ),
        scratch=[
            pltpu.VMEM((2, total, 2 * HD), BF),
            pltpu.VMEM((2, total, 2 * HD), BF),
            pltpu.VMEM((2, 2 * HD, total), BF),
            pltpu.VMEM((total, 2 * HD), F32),
            pltpu.VMEM((total, 2 * HD), F32),
        ],
        flops=40 * total * total * count * 2 * HD,
    )


def mix_out_kernel(local, total, info_ref, mine_ref, other_ref, w1_ref, w2_ref, bias_ref, x_ref, gain_ref, cond_ref, res_ref, act_ref):
    rows = x_ref.shape[0]
    live = live_column(rows, pl.program_id(0) * rows, info_ref, local, total).astype(F32)
    attended = nn(mine_ref[...], w1_ref[...]) + nn(other_ref[...], w2_ref[...]) + bias_ref[...]
    residual = x_ref[...].astype(F32) + live * attended
    res_ref[...] = residual
    normal, _ = norm_rows(residual)
    act_ref[...] = (normal * (gain_ref[...] * (1.0 + cond_ref[2:3, :])) + cond_ref[3:4, :]).astype(BF)


def mix_out(info, mine, other, weight, bias, x, gain, cond, local):
    total, width = x.shape
    half = mine.shape[1]
    block = 256
    row = lambda w: pl.BlockSpec((block, w), lambda i, s: (i, 0))
    vec = pl.BlockSpec((1, width), lambda i, s: (0, 0))
    return call(
        functools.partial(mix_out_kernel, local, total), "mix_out", (info,), (total // block,),
        [mine, other, weight, weight, bias, x, gain, cond],
        [
            row(half), row(half),
            pl.BlockSpec((half, width), lambda i, s: (s[0], 0)),
            pl.BlockSpec((half, width), lambda i, s: (1 - s[0], 0)),
            vec, row(width), vec, pl.BlockSpec(cond.shape, lambda i, s: (0, 0)),
        ],
        (sds((total, width), F32), sds((total, width), BF)),
        (row(width), row(width)),
        flops=4 * total * width * half,
    )


def raise_kernel(info_ref, act_ref, w_ref, bias_ref, hid_ref, der_ref):
    raised = nn(act_ref[...], w_ref[...]) + bias_ref[...]
    half = 0.5 * (1.0 + lax.erf(raised * (0.5**0.5)))
    hid_ref[...] = (raised * half).astype(BF)
    der_ref[...] = (half + raised * (jnp.exp(-0.5 * raised * raised) * (2.0 * math.pi) ** -0.5)).astype(BF)


def raise_up(info, act, weight, bias, fb, nb):
    total, width = act.shape
    col = pl.BlockSpec((total, fb), lambda j, s: (0, j))
    return call(
        raise_kernel, "raise_up", (info,), (nb,),
        [act, weight, bias],
        [
            pl.BlockSpec((total, width), lambda j, s: (0, 0)),
            pl.BlockSpec((width, fb), lambda j, s: (0, 2 * j + s[0])),
            pl.BlockSpec((1, fb), lambda j, s: (0, 2 * j + s[0])),
        ],
        (sds((total, fb * nb), BF),) * 2, (col, col),
        flops=2 * total * width * fb * nb,
    )


def weight_gradient_kernel(count, index_ref, lhs_ref, *refs):
    rhs, out_ref = refs[:count], refs[count]
    w = rhs[0].shape[1]
    lhs = lhs_ref[...]
    for n, ref in enumerate(rhs):
        out_ref[:, n * w : (n + 1) * w] = tn_dot(lhs, ref[...]).astype(BF)


def weight_gradient(lhs, rhss, rows, mb, col, w, name="weight_gradient"):
    total, height = lhs.shape
    if mb % 128:
        every = height // 128
        whole = weight_gradient(lhs, rhss, jnp.arange(every), 128, col, w, name)
        return whole.reshape(height // mb, mb, -1)[rows].reshape(rows.shape[0] * mb, -1)
    if w % 128:
        rhss = [lax.dynamic_slice_in_dim(r, col * w, w, 1) for r in rhss]
        col = 0
    n = rows.shape[0]
    index = jnp.concatenate([rows.astype(jnp.int32), jnp.full((1,), col, jnp.int32)])
    return call(
        functools.partial(weight_gradient_kernel, len(rhss)), name, (index,), (n,),
        [lhs, *rhss],
        [pl.BlockSpec((total, mb), lambda i, s: (0, s[i]))]
        + [pl.BlockSpec((total, w), lambda i, s: (0, s[n]))] * len(rhss),
        sds((n * mb, len(rhss) * w), BF),
        pl.BlockSpec((mb, len(rhss) * w), lambda i, s: (i, 0)),
        flops=2 * total * n * mb * len(rhss) * w,
    )


def raise_back_kernel(info_ref, g_ref, w_ref, der_ref, out_ref, sum_ref):
    back = (nt(g_ref[...], w_ref[...]) * der_ref[...].astype(F32)).astype(BF)
    out_ref[...] = back
    sum_ref[...] = jnp.sum(back.astype(F32), axis=0, keepdims=True)


def raise_back(info, g, weight, der, fb, nb):
    total, width = g.shape
    return call(
        raise_back_kernel, "raise_back", (info,), (nb,),
        [g, weight, der],
        [
            pl.BlockSpec((total, width), lambda j, s: (0, 0)),
            pl.BlockSpec((fb, width), lambda j, s: (2 * j + s[0], 0)),
            pl.BlockSpec((total, fb), lambda j, s: (0, j)),
        ],
        (sds((total, fb * nb), BF), sds((1, fb * nb), F32)),
        (pl.BlockSpec((total, fb), lambda j, s: (0, j)), pl.BlockSpec((1, fb), lambda j, s: (0, j))),
        flops=2 * total * width * fb * nb,
    )


def rows_product_kernel(count, transposed, index_ref, *refs):
    lhs, rhs, out_ref = refs[0], refs[1 : 1 + count], refs[1 + count]
    w = rhs[0].shape[1] if transposed else rhs[0].shape[0]
    total = None
    for n, ref in enumerate(rhs):
        term = (nt if transposed else nn)(lhs[:, n * w : (n + 1) * w], ref[...])
        total = term if total is None else total + term
    out_ref[...] = total.astype(BF)


def rows_product(lhs, weight, rows, block, core, fb, nb, transposed, name):
    depth = lhs.shape[1]
    width = weight.shape[0] if transposed else weight.shape[1]
    n = rows.shape[0]
    index = jnp.concatenate([rows.astype(jnp.int32), jnp.full((1,), core, jnp.int32)])
    if transposed:
        specs = [pl.BlockSpec((width, fb), lambda i, s, j=j: (0, 2 * j + s[n])) for j in range(nb)]
    else:
        specs = [pl.BlockSpec((fb, width), lambda i, s, j=j: (2 * j + s[n], 0)) for j in range(nb)]
    return call(
        functools.partial(rows_product_kernel, nb, transposed), name, (index,), (n,),
        [lhs] + [weight] * nb,
        [pl.BlockSpec((block, depth), lambda i, s: (s[i], 0)), *specs],
        sds((n * block, width), BF),
        pl.BlockSpec((block, width), lambda i, s: (i, 0)),
        flops=2 * n * block * depth * width,
    )


def norm_back(g, v, gain, scale):
    normal, inverse = norm_rows(v)
    e = g * (gain * (1.0 + scale))
    grad = inverse * (
        e - jnp.mean(e, axis=-1, keepdims=True) - normal * jnp.mean(e * normal, axis=-1, keepdims=True)
    )
    return grad, jnp.sum(g * normal, axis=0, keepdims=True), jnp.sum(g, axis=0, keepdims=True)


def accumulate(sum_ref, parts):
    block = jnp.concatenate(parts, axis=0)

    @pl.when(pl.program_id(0) == 0)
    def _():
        sum_ref[...] = block

    @pl.when(pl.program_id(0) > 0)
    def _():
        sum_ref[...] += block


def dense_norm_back_kernel(local, total, info_ref, a_ref, b_ref, res_ref, cot_ref, gain_ref, cond_ref, w_ref, gres_ref, gatt_ref, gmix_ref, sum_ref):
    rows = res_ref.shape[0]
    live = live_column(rows, pl.program_id(0) * rows, info_ref, local, total).astype(F32)
    g = a_ref[...].astype(F32) + b_ref[...].astype(F32)
    grad, by_normal, plain = norm_back(g, res_ref[...], gain_ref[...], cond_ref[2:3, :])
    g_residual = cot_ref[...].astype(F32) + grad
    gres_ref[...] = g_residual
    g_attend = (live * g_residual).astype(BF)
    gatt_ref[...] = g_attend
    gmix_ref[...] = nt(g_attend, w_ref[...]).astype(BF)
    bias = jnp.sum(g_attend.astype(F32), axis=0, keepdims=True)
    accumulate(sum_ref, [by_normal, plain, bias, jnp.zeros((5, bias.shape[1]), F32)])


def dense_norm_back(info, a, b, residual, cot, gain, cond, weight, local):
    total, width = residual.shape
    half = weight.shape[0] // 2
    block = 256
    row = lambda w: pl.BlockSpec((block, w), lambda i, s: (i, 0))
    return call(
        functools.partial(dense_norm_back_kernel, local, total), "dense_norm_back", (info,), (total // block,),
        [a, b, residual, cot, gain, cond, weight],
        [
            row(width), row(width), row(width), row(width),
            pl.BlockSpec((1, width), lambda i, s: (0, 0)),
            pl.BlockSpec(cond.shape, lambda i, s: (0, 0)),
            pl.BlockSpec((half, width), lambda i, s: (s[0], 0)),
        ],
        (sds((total, width), F32), sds((total, width), BF), sds((total, half), BF), sds((8, width), F32)),
        (row(width), row(width), row(half), pl.BlockSpec((8, width), lambda i, s: (0, 0))),
        flops=2 * total * width * half,
    )


def project_back_kernel(count, index_ref, *refs):
    lhs, rhs, out_ref = refs[: 3 * count], refs[3 * count : 3 * count + 3], refs[-1]
    total = None
    for n in range(3):
        for m in range(count):
            ref = lhs[n * count + m]
            w = ref.shape[1]
            term = nt(ref[...], rhs[n][:, m * w : (m + 1) * w])
            total = term if total is None else total + term
    out_ref[...] = total.astype(BF)


def project_back(parts, weight, rows, block, core):
    width = weight.shape[0]
    half = weight.shape[1] // 6
    count = len(parts)
    n = rows.shape[0]
    index = jnp.concatenate([rows.astype(jnp.int32), jnp.full((1,), core, jnp.int32)])
    lhs = [part[m] for m in range(3) for part in parts]
    return call(
        functools.partial(project_back_kernel, count), "project_back", (index,), (n,),
        lhs + [weight] * 3,
        [pl.BlockSpec((block, a.shape[1]), lambda i, s: (s[i], 0)) for a in lhs]
        + [pl.BlockSpec((width, half), lambda i, s, m=m: (0, 2 * m + s[n])) for m in range(3)],
        sds((n * block, width), BF),
        pl.BlockSpec((block, width), lambda i, s: (i, 0)),
        flops=6 * n * block * half * width,
    )


def attend_norm_back_kernel(index_ref, a_ref, b_ref, x_ref, gres_ref, gain_ref, cond_ref, out_ref, sum_ref):
    g = a_ref[...].astype(F32) + b_ref[...].astype(F32)
    grad, by_normal, plain = norm_back(g, x_ref[...].astype(F32), gain_ref[...], cond_ref[0:1, :])
    out_ref[...] = (gres_ref[...] + grad).astype(BF)
    accumulate(sum_ref, [by_normal, plain, jnp.zeros((6, plain.shape[1]), F32)])


def attend_norm_back(rows, a, b, x, g_residual, gain, cond, block):
    width = x.shape[1]
    n = rows.shape[0]
    plain = pl.BlockSpec((block, width), lambda i, s: (i, 0))
    picked = pl.BlockSpec((block, width), lambda i, s: (s[i], 0))
    return call(
        attend_norm_back_kernel, "attend_norm_back", (rows.astype(jnp.int32),), (n,),
        [a, b, x, g_residual, gain, cond],
        [
            plain, plain, picked, picked,
            pl.BlockSpec((1, width), lambda i, s: (0, 0)),
            pl.BlockSpec(cond.shape, lambda i, s: (0, 0)),
        ],
        (sds((n * block, width), BF), sds((8, width), F32)),
        (plain, pl.BlockSpec((8, width), lambda i, s: (0, 0))),
        flops=0,
    )


def sinus_angles(time, features, width):
    halfway = width // 2
    rates = jnp.exp(-math.log(10000.0) * (features % halfway).astype(F32) / halfway)
    angles = time[:, None] * rates[None, :]
    return jnp.where((features < halfway)[None, :], jnp.sin(angles), jnp.cos(angles))


def body(
    dp, seq,
    tokens, time_index, lengths, time_weight, time_bias, attend_gain, query_key_value_weight,
    attention_output_weight, attend_bias, dense_gain, feedforward_up_matrix, up_bias,
    feedforward_down_matrix, down_bias, cotangent,
):
    nl, tl, d = tokens.shape
    ff = feedforward_up_matrix.shape[1]
    total = tl * seq
    chips = dp // 2
    nz = dp // 4
    i = lax.axis_index("dp")
    y = lax.axis_index("seq")
    core = i % 2
    x = (i // 2) % 2
    z = i // 4
    h = tl // 2
    half = d // 2
    fb, nb = ff // dp, dp // 2


    core_swap = lambda a: lax.ppermute(a, "dp", [(n, n ^ 1) for n in range(dp)])
    x_swap = lambda a: lax.ppermute(a, "dp", [(n, n ^ 2) for n in range(dp)])

    def z_shift(a, k):
        return lax.ppermute(a, "dp", [(n, (n // 4 + k) % nz * 4 + n % 4) for n in range(dp)])

    def y_shift(a, k):
        return lax.ppermute(a, "seq", [(n, (n + k) % seq) for n in range(seq)])

    def travel(k, q):
        pairs = []
        for chip in range(chips):
            for s in range(seq):
                target = (s + k) % seq
                pairs.append(((chip * 2 + target // nl) * seq + s, (chip * 2 + q) * seq + target))
        return pairs

    def pick(a, index):
        return lax.dynamic_index_in_dim(a, index, 0, keepdims=False)

    def in_core_order(mine, other):
        return jnp.where(core == 0, mine, other), jnp.where(core == 0, other, mine)

    def fetch(a):
        mine = pick(a, y % nl)
        local = jnp.where(core == y // nl, mine, core_swap(mine))
        far = []
        for k in range(1, seq):
            piece = pick(a, (y + k) % seq % nl)
            got = [
                lax.ppermute(piece[q * h : (q + 1) * h], ("dp", "seq"), travel(k, q)) for q in range(2)
            ]
            own = jnp.where(core == 0, got[0], got[1])
            far += in_core_order(own, core_swap(own))
        return local, jnp.concatenate(far, axis=0)

    def give_back(a):
        got = [jnp.concatenate(in_core_order(a[0], core_swap(a[0])), axis=0)]
        for k in range(1, seq):
            halves = [
                lax.ppermute(a[k], ("dp", "seq"), [(t, s) for s, t in travel(k, q)]) for q in range(2)
            ]
            got.append(jnp.concatenate(halves, axis=0))
        got = jnp.stack(got)
        return jnp.stack([pick(got, (core * nl + j - y) % seq) for j in range(nl)])

    def add(*terms):
        return sum(t.astype(F32) for t in terms).astype(BF)

    def z_sum(a):
        return add(pick(a, z), *[z_shift(pick(a, (z + k) % nz), k) for k in range(1, nz)])

    def y_sum(a):
        got = [y_shift(a, k).astype(F32) for k in range(1, seq)]
        return sum(got, a.astype(F32))

    def y_gather(a):
        got = jnp.stack([a] + [y_shift(a, k) for k in range(1, seq)])
        return jnp.stack([pick(got, (y - n) % seq) for n in range(seq)])

    def reduce_x_first(send, keep, rows):
        mine = add(keep, x_swap(send)).reshape(nz, rows, -1)
        return y_sum(z_sum(mine))

    def reduce_y_first(sends, keep, rows):
        mine = add(keep, *[y_shift(s, k + 1) for k, s in enumerate(sends)])
        mine = mine.reshape(nz, 2, rows, -1)
        mine = add(
            lax.dynamic_index_in_dim(mine, x, 1, keepdims=False),
            x_swap(lax.dynamic_index_in_dim(mine, 1 - x, 1, keepdims=False)),
        )
        return y_gather(z_sum(mine))

    zs = jnp.arange(nz)

    def reduced(lhs, early, late, rows, name):
        w_early = early[0].shape[1]
        first = reduce_x_first(
            weight_gradient(lhs, early, zs * 2 + 1 - x, rows, 0, w_early, name),
            weight_gradient(lhs, early, zs * 2 + x, rows, 0, w_early, name),
            rows,
        )
        w = late[0].shape[1] // seq
        every = jnp.arange(chips)
        parts = [weight_gradient(lhs, late, every, rows, (y + k) % seq, w, name) for k in range(1, seq)]
        kept = weight_gradient(lhs, late, every, rows, y, w, name)
        second = reduce_y_first(parts, kept, rows)
        second = second.reshape(seq, rows, len(late), w).transpose(1, 2, 0, 3)
        return first, second.reshape(rows, -1).astype(F32)


    both = jnp.stack([time_index, lengths])
    every = jnp.stack(in_core_order(both, core_swap(both)), axis=1).reshape(2, 2 * nl)
    time = lax.dynamic_slice_in_dim(every[0], y, 1).astype(F32)
    length = lax.dynamic_slice_in_dim(every[1], y, 1)
    info = jnp.concatenate([core[None], (y * tl)[None], length]).astype(jnp.int32)
    slot_of = (y * tl - jnp.arange(total) // tl * tl) % total + jnp.arange(total) % tl
    live = slot_of < length[0]

    near, far = fetch(tokens)
    near_cot, far_cot = fetch(cotangent)
    table = sinus_angles(time, jnp.arange(d), d).astype(BF)
    cond = (jnp.dot(table, time_weight, preferred_element_type=F32) + time_bias).reshape(4, d)
    gain1, gain2 = attend_gain[None, :], dense_gain[None, :]

    act1, qkv = project(info, near, 0, total, gain1, cond, query_key_value_weight)
    act1, qkv = project(info, far, tl, total, gain1, cond, query_key_value_weight, (act1, qkv))
    full = jnp.concatenate([near, far], axis=0)
    mixture, logs = attend_forward(info, qkv, tl)
    other_mixture = core_swap(mixture)
    residual, act2 = mix_out(
        info, mixture, other_mixture, attention_output_weight, attend_bias[None, :], full, gain2, cond, tl
    )
    hidden, slope = raise_up(info, act2, feedforward_up_matrix, up_bias[None, :], fb, nb)

    cot = jnp.concatenate([near_cot, far_cot], axis=0)
    g_dense = jnp.where(live[:, None], cot, jnp.zeros_like(cot))
    g_down_bias = jnp.sum(g_dense.astype(F32), axis=0)
    down_early, down_late = reduced(hidden, [g_dense[:, :half]], [g_dense[:, half:]], fb, "down_gradient")
    gradient_down = jnp.concatenate([down_early, down_late], axis=1)

    g_raised, g_up_bias = raise_back(info, g_dense, feedforward_down_matrix, slope, fb, nb)
    g_act2 = rows_product(
        g_raised, feedforward_up_matrix, jnp.arange(total // 256), 256, core, fb, nb, True, "raise_input_back"
    )
    up_half = fb * nb // 2
    up_early, up_late = reduced(act2, [g_raised[:, :up_half]], [g_raised[:, up_half:]], d // chips, "up_gradient")

    g_residual, g_attend, g_mixture, sums2 = dense_norm_back(
        info, g_act2, core_swap(g_act2), residual, cot, gain2, cond, attention_output_weight, tl
    )

    rb = d // dp
    g_out = weight_gradient(mixture, [g_attend], jnp.arange(half // 128), 128, 0, d, "out_gradient")
    g_out = g_out.reshape(chips // 2, 2, rb, d)
    mine = lax.dynamic_index_in_dim(g_out, core, 1, keepdims=False)
    yours = core_swap(lax.dynamic_index_in_dim(g_out, 1 - core, 1, keepdims=False))
    g_out = jnp.concatenate(in_core_order(mine, yours), axis=0).reshape(nz, 2, rb, d)
    gradient_out = reduce_x_first(
        lax.dynamic_index_in_dim(g_out, 1 - x, 1, keepdims=False).reshape(nz * rb, d),
        lax.dynamic_index_in_dim(g_out, x, 1, keepdims=False).reshape(nz * rb, d),
        rb,
    )

    pairs = half // (2 * HD)
    parts = [
        attend_backward(info, qkv, g_mixture, mixture, logs, tl, n * pairs // 2, pairs // 2) for n in range(2)
    ]
    in_early, in_late = reduced(act1, list(parts[0]), list(parts[1]), d // chips, "in_gradient")

    own_rows, their_rows = jnp.arange(seq) * 2 + core, jnp.arange(seq) * 2 + 1 - core
    g_act1_theirs = core_swap(project_back(parts, query_key_value_weight, their_rows, h, core))
    g_act1 = project_back(parts, query_key_value_weight, own_rows, h, core)
    g_tokens, sums1 = attend_norm_back(own_rows, g_act1, g_act1_theirs, full, g_residual, gain1, cond, h)
    gradient_tokens = give_back(g_tokens.reshape(seq, h, d))

    down_args = (h, core, fb, nb, False, "lower")
    branch_theirs = core_swap(rows_product(hidden, feedforward_down_matrix, their_rows, *down_args))
    branch = rows_product(hidden, feedforward_down_matrix, own_rows, *down_args)
    pieces = lambda a: lax.dynamic_index_in_dim(a.reshape(seq, 2, h, -1), core, 1, keepdims=False)
    live_half = pieces(live[:, None])
    branch = (branch.astype(F32) + branch_theirs.astype(F32)).reshape(seq, h, d) + down_bias
    result = give_back((pieces(residual) + jnp.where(live_half, branch, 0.0)).astype(BF))

    def finish(early, late, blocks, inner):
        whole = jnp.concatenate(
            [a.astype(BF).reshape(2, d // dp, blocks, inner) for a in (early, late)], axis=3
        )
        got = core_swap(lax.dynamic_index_in_dim(whole, 1 - core, 0, keepdims=False))
        mine = lax.dynamic_index_in_dim(whole, core, 0, keepdims=False)
        return in_core_order(mine.astype(F32), got.astype(F32))

    first, second = finish(up_early, up_late, 1, up_half)
    gradient_up = jnp.stack([a.reshape(d // dp, nb, fb) for a in (first, second)], axis=2).reshape(d // dp, ff)
    first, second = finish(in_early, in_late, 3, half // 2)
    gradient_in = jnp.stack([first, second], axis=2).reshape(d // dp, 3 * d)

    once = jnp.where(core == 0, 1.0, 0.0)
    scales = 1.0 + cond
    up_sum = g_up_bias.reshape(nb, 1, fb)
    up_sum = jnp.concatenate(in_core_order(up_sum, jnp.zeros_like(up_sum)), axis=1).reshape(ff // d, d)
    pack = jnp.concatenate(
        [
            sums1[0:1] * gain1,
            sums1[1:2],
            once * sums2[0:1] * gain2,
            once * sums2[1:2],
            sums1[0:1] * scales[0:1],
            once * sums2[0:1] * scales[2:3],
            once * sums2[2:3],
            once * g_down_bias[None, :],
            once * jnp.broadcast_to(time[:, None], (1, d)),
            up_sum,
        ]
    )
    pack = pack + core_swap(pack)
    all_packs = jnp.stack([pack, x_swap(pack)])
    all_packs = jnp.concatenate([all_packs] + [y_shift(all_packs, k) for k in range(1, seq)])
    all_packs = jnp.concatenate([all_packs] + [z_shift(all_packs, k) for k in range(1, nz)])
    g_cond = all_packs[:, 0:4].reshape(-1, 4 * d)
    own_features = i * (d // dp) + jnp.arange(d // dp)
    features = sinus_angles(all_packs[:, 8, 0], own_features, d).astype(BF)
    gradient_time = lax.dot_general(
        features.astype(F32), g_cond, (((0,), (0,)), ((), ())), precision=lax.Precision.HIGHEST
    )
    sums = jnp.sum(all_packs, axis=0)
    part = lambda v: lax.dynamic_index_in_dim(v.reshape(dp, -1), i, 0, keepdims=False)
    return (
        result,
        gradient_tokens,
        gradient_time,
        part(sums[0:4]),
        part(sums[4]),
        gradient_in,
        gradient_out,
        part(sums[6]),
        part(sums[5]),
        gradient_up,
        part(sums[9:]),
        gradient_down,
        part(sums[7]),
    )


def solution(mesh):
    whole = P()
    rows = P("dp", "seq", None)
    return jax.shard_map(
        functools.partial(body, mesh.shape["dp"], mesh.shape["seq"]),
        mesh=mesh,
        in_specs=(rows, P("dp"), P("dp"), *(whole,) * 11, rows),
        out_specs=(
            rows, rows, P("dp", None), P("dp"), P("dp"), P("dp", None), P("dp", None),
            P("dp"), P("dp"), P("dp", None), P("dp"), P("dp", None), P("dp"),
        ),
        check_vma=False,
    )
```

```python
import functools
import math

import jax
import jax.numpy as jnp
from jax import lax
from jax.experimental import pallas as pl
from jax.experimental.pallas import tpu as pltpu
from jax.sharding import PartitionSpec as P

HD = 64
CORE, OFFSET, LENGTH, NEAR, FAR, X, Z, HALF, Y = range(9)
EPS = 1e-05
COST = 1
MASKED = -1e30
EXP2_SCALE = math.log2(math.e) * HD ** (-0.5)
BF = jnp.bfloat16
F32 = jnp.float32
VMEM = 20 * 1024 * 1024
ROOM = 56 * 1024 * 1024


class Order:
    def __init__(self, info):
        self.info = info

    def run(self, kernel, *args):
        return self.after(kernel(self.info, *args))

    def after(self, values):
        values, self.info = lax.optimization_barrier((values, self.info))
        return values


def sds(shape, dtype):
    return jax.ShapeDtypeStruct(shape, dtype)


def nt(a, b):
    return lax.dot_general(a, b, (((1,), (1,)), ((), ())), preferred_element_type=F32)


def nn(a, b):
    return jnp.dot(a, b, preferred_element_type=F32)


def tn_dot(a, b):
    return lax.dot_general(a, b, (((0,), (0,)), ((), ())), preferred_element_type=F32)


def call(kernel, name, scalars, grid, ins, in_specs, outs, out_specs, scratch=(), flops=0, aliases=None, room=VMEM):
    return pl.pallas_call(
        kernel,
        name=name,
        grid_spec=pltpu.PrefetchScalarGridSpec(
            num_scalar_prefetch=len(scalars),
            grid=grid,
            in_specs=in_specs,
            out_specs=out_specs,
            scratch_shapes=list(scratch),
        ),
        out_shape=outs,
        input_output_aliases=aliases or {},
        compiler_params=pltpu.CompilerParams(
            vmem_limit_bytes=room, dimension_semantics=("arbitrary",) * len(grid)
        ),
        cost_estimate=pl.CostEstimate(flops=COST, bytes_accessed=1, transcendentals=0),
    )(*scalars, *ins)


def norm_rows(v):
    centre = v - jnp.mean(v, axis=-1, keepdims=True)
    inverse = lax.rsqrt(jnp.mean(centre * centre, axis=-1, keepdims=True) + EPS)
    return centre * inverse, inverse


def live_column(rows, first, info_ref, local, total):
    r = first + lax.broadcasted_iota(jnp.int32, (rows, 1), 0)
    low = lax.rem(r, local)
    start = info_ref[OFFSET] - (r - low)
    slot = jnp.where(start < 0, start + total, start) + low
    return slot < info_ref[LENGTH]


def own_projection_kernel(info_ref, q_ref, k_ref, v_ref, out_ref):
    w = q_ref.shape[1]
    for n, ref in enumerate((q_ref, k_ref, v_ref)):
        out_ref[:, n * w : (n + 1) * w] = ref[...]


def own_projection(info, weight):
    d, half = weight.shape[0], weight.shape[1] // 6
    block = min(256, d)
    return call(
        own_projection_kernel, "own_projection", (info,), (d // block,), [weight] * 3,
        [pl.BlockSpec((block, half), lambda i, s, n=n: (i, 2 * n + s[CORE])) for n in range(3)],
        sds((d, 3 * half), BF), pl.BlockSpec((block, 3 * half), lambda i, s: (i, 0)), flops=d * d, room=ROOM,
    )


def own_units_kernel(fb, info_ref, *refs):
    up, down, (up_out, down_out) = refs[:-2:2], refs[1:-2:2], refs[-2:]
    for n, (u, w) in enumerate(zip(up, down, strict=True)):
        up_out[:, n * fb : (n + 1) * fb] = u[...]
        down_out[n * fb : (n + 1) * fb, :] = w[...]


def own_units(info, up, down, fb):
    d, ff = up.shape
    each = 2
    specs = []
    for n in range(each):
        specs.append(pl.BlockSpec((d, fb), lambda i, s, n=n: (0, 2 * (each * i + n) + s[CORE])))
        specs.append(pl.BlockSpec((fb, d), lambda i, s, n=n: (2 * (each * i + n) + s[CORE], 0)))
    return call(
        functools.partial(own_units_kernel, fb), "own_units", (info,), (ff // (2 * fb * each),), [up, down] * each, specs,
        (sds((d, ff // 2), BF), sds((ff // 2, d), BF)),
        (pl.BlockSpec((d, each * fb), lambda i, s: (0, i)), pl.BlockSpec((each * fb, d), lambda i, s: (i, 0))),
        flops=d * ff, room=ROOM,
    )


def choose(flag, a, b):
    return jnp.where(flag == 1, a, b)


def project_kernel(flag, info_ref, a_ref, b_ref, gain_ref, cond_ref, w_ref, *rest):
    full_ref, act_ref, qkv_ref = rest[-3:]
    x = choose(info_ref[flag], a_ref[...].astype(F32), b_ref[...].astype(F32))
    full_ref[...] = x.astype(BF)
    normal, _ = norm_rows(x)
    act = (normal * (gain_ref[...] * (1.0 + cond_ref[0:1, :])) + cond_ref[1:2, :]).astype(BF)
    act_ref[...] = act
    qkv_ref[...] = nn(act, w_ref[...]).astype(BF)


def project(info, flag, a, b, first, total, gain, cond, weight, before=None):
    rows, width = a.shape
    block = min(256, rows)
    skip = first // block
    row = pl.BlockSpec((block, width), lambda i, s: (i, 0))
    ins = [a, b, gain, cond, weight]
    specs = [
        row, row,
        pl.BlockSpec((1, width), lambda i, s: (0, 0)),
        pl.BlockSpec(cond.shape, lambda i, s: (0, 0)),
        pl.BlockSpec(weight.shape, lambda i, s: (0, 0)),
    ]
    aliases = {}
    if before is not None:
        ins += list(before)
        specs += [pl.BlockSpec(memory_space=pl.ANY)] * 3
        aliases = {6: 0, 7: 1, 8: 2}
    out = pl.BlockSpec((block, width), lambda i, s: (i + skip, 0))
    return call(
        functools.partial(project_kernel, flag), "project", (info,), (rows // block,), ins, specs,
        (sds((total, width), BF), sds((total, width), BF), sds((total, weight.shape[1]), BF)),
        (out, out, pl.BlockSpec((block, weight.shape[1]), lambda i, s: (i + skip, 0))),
        flops=2 * rows * width * weight.shape[1], aliases=aliases,
    )


def assemble_kernel(local, total, info_ref, n1_ref, n2_ref, f1_ref, f2_ref, cot_ref, g_ref, sum_ref):
    near = choose(info_ref[NEAR], n1_ref[...].astype(F32), n2_ref[...].astype(F32))
    far = choose(info_ref[FAR], f1_ref[...].astype(F32), f2_ref[...].astype(F32))
    sums = jnp.zeros((1, near.shape[1]), F32)
    for first, piece in ((0, near), (near.shape[0], far)):
        rows = slice(first, first + piece.shape[0])
        live = live_column(piece.shape[0], first, info_ref, local, total)
        masked = jnp.where(live, piece, 0.0)
        cot_ref[rows, :] = piece.astype(BF)
        g_ref[rows, :] = masked.astype(BF)
        sums += jnp.sum(masked, axis=0, keepdims=True)
    sum_ref[...] = jnp.broadcast_to(sums, sum_ref.shape)


def assemble(info, near, far, local):
    total, width = near[0].shape[0] + far[0].shape[0], near[0].shape[1]
    whole = lambda a: pl.BlockSpec(a.shape, lambda i, s: (0, 0))
    ins = [*near, *far]
    outs = (sds((total, width), BF), sds((total, width), BF), sds((8, width), F32))
    return call(
        functools.partial(assemble_kernel, local, total), "assemble", (info,), (1,),
        ins, [whole(a) for a in ins], outs, tuple(whole(a) for a in outs), flops=total * width,
    )


def augment(main, rows, values):
    lane = lax.broadcasted_iota(jnp.int32, (1, 2 * HD), 1)
    extra = jnp.zeros((rows, 2 * HD), F32)
    for n, value in enumerate(values):
        extra = jnp.where(lane == n, value, extra)
    return jnp.concatenate([main.astype(BF), extra.astype(BF)], axis=1)


def stack_heads(pair):
    first = lax.broadcasted_iota(jnp.int32, (1, 2 * HD), 1) < HD
    zero = jnp.zeros_like(pair)
    return jnp.concatenate([jnp.where(first, pair, zero), jnp.where(first, zero, pair)], axis=0)


def merge_heads(stacked):
    rows = stacked.shape[0] // 2
    first = lax.broadcasted_iota(jnp.int32, (1, 2 * HD), 1) < HD
    return jnp.where(first, stacked[:rows], stacked[rows:])


TILE = 256


def attend_forward_kernel(local, info_ref, q_ref, k_ref, v_ref, o_ref, l_ref, ka, va):
    total = k_ref.shape[0]
    pair = pl.program_id(0)
    live = live_column(total, 0, info_ref, local, total)
    ka[...] = augment(k_ref[...], total, (jnp.where(live, 0.0, MASKED),))
    va[...] = augment(v_ref[...], total, (1.0,))

    def scores_of(start):
        return nt(augment(stack_heads(q_ref[start : start + TILE, :]), 2 * TILE, (1.0,)), ka[...])

    def mix(start, top, weights):
        rows = slice(start, start + TILE)
        mixed = nn(weights, va[...])
        sums = mixed[:, 2 * HD : 2 * HD + 1]
        o_ref[rows, :] = merge_heads(mixed[:, : 2 * HD] / sums).astype(BF)
        logs = top + jnp.log(sums) * HD**0.5
        column = lax.broadcasted_iota(jnp.int32, (1, 2 * HD), 1) - 2 * pair
        held = jnp.where(pair == 0, 0.0, l_ref[rows, :])
        l_ref[rows, :] = jnp.where(column == 0, logs[:TILE], jnp.where(column == 1, logs[TILE:], held))

    scores, waiting = scores_of(0), None
    for start in range(0, total, TILE):
        ahead = scores_of(start + TILE) if start + TILE < total else None
        top = jnp.max(scores, axis=-1, keepdims=True)
        weights = jnp.exp2((scores - top) * EXP2_SCALE).astype(BF)
        if waiting is not None:
            mix(*waiting)
        scores, waiting = ahead, (start, top, weights)
    mix(*waiting)


def attend_forward(info, qkv, local, first, count):
    total = qkv.shape[0]
    pairs = qkv.shape[1] // (6 * HD)
    out = pl.BlockSpec((total, 2 * HD), lambda j, s: (0, j))
    return call(
        functools.partial(attend_forward_kernel, local), "attend_forward", (info,), (count,),
        [qkv, qkv, qkv],
        [pl.BlockSpec((total, 2 * HD), lambda j, s, m=m: (0, m * pairs + first + j)) for m in range(3)],
        (sds((total, count * 2 * HD), BF), sds((total, 2 * HD), F32)),
        (out, pl.BlockSpec((total, 2 * HD), lambda j, s: (0, 0))),
        scratch=[pltpu.VMEM((total, 4 * HD), BF), pltpu.VMEM((total, 4 * HD), BF)],
        flops=32 * total * total * count * HD,
    )


def attend_backward_kernel(
    local, info_ref, q_ref, g_ref, o_ref, l_ref, k_ref, v_ref, gq_ref, gk_ref, gv_ref, ka, va, acck, accv
):
    total = k_ref.shape[0]

    @pl.when(pl.program_id(1) == 0)
    def _():
        live = live_column(total, 0, info_ref, local, total)
        ka[...] = augment(k_ref[...], total, (jnp.where(live, 0.0, MASKED), 1.0, 1.0, 1.0))
        va[...] = augment(v_ref[...], total, (1.0, 1.0))
        acck[...] = jnp.zeros_like(acck)
        accv[...] = jnp.zeros_like(accv)

    for start in range(0, q_ref.shape[0], TILE):
        rows = slice(start, start + TILE)
        q = stack_heads(q_ref[rows, :])
        g = stack_heads(g_ref[rows, :])
        o = o_ref[rows, :].astype(F32)
        inner = jnp.sum(g.astype(F32) * jnp.concatenate([o, o], axis=0), axis=-1, keepdims=True)
        column = lax.broadcasted_iota(jnp.int32, (1, 2 * HD), 1) - 2 * pl.program_id(0)
        logs = [jnp.sum(jnp.where(column == k, l_ref[rows, :], 0.0), axis=-1, keepdims=True) for k in range(2)]
        logs = jnp.concatenate(logs, axis=0)
        high = logs.astype(BF).astype(F32)
        middle = (logs - high).astype(BF).astype(F32)
        inner_high = inner.astype(BF).astype(F32)
        qa = augment(q, 2 * TILE, (1.0, -high, -middle, high + middle - logs))
        ga = augment(g, 2 * TILE, (-inner_high, inner_high - inner))
        probability = jnp.exp2(nt(ka[...], qa) * EXP2_SCALE)
        g_scores = (probability * nt(va[...], ga)).astype(BF)
        acck[...] += nn(g_scores, q)
        accv[...] += nn(probability.astype(BF), g)
        gq_ref[rows, :] = merge_heads(tn_dot(g_scores, k_ref[...]) * HD**-0.5).astype(BF)

    @pl.when(pl.program_id(1) == pl.num_programs(1) - 1)
    def _():
        gk_ref[...] = (acck[...] * HD**-0.5).astype(BF)
        gv_ref[...] = accv[...].astype(BF)


def attend_backward(info, qkv, g, o, logs, local, first, count):
    total = qkv.shape[0]
    pairs = qkv.shape[1] // (6 * HD)
    block = total
    part = pl.BlockSpec((block, 2 * HD), lambda j, i, s: (i, first + j))
    own = pl.BlockSpec((block, 2 * HD), lambda j, i, s: (i, j))
    return call(
        functools.partial(attend_backward_kernel, local), "attend_backward", (info,), (count, total // block),
        [qkv, g, o, logs, qkv, qkv],
        [
            part, part, own, pl.BlockSpec((total, 2 * HD), lambda j, i, s: (i, 0)),
            pl.BlockSpec((total, 2 * HD), lambda j, i, s: (0, pairs + first + j)),
            pl.BlockSpec((total, 2 * HD), lambda j, i, s: (0, 2 * pairs + first + j)),
        ],
        (sds((total, count * 2 * HD), BF),) * 3,
        (
            own,
            pl.BlockSpec((total, 2 * HD), lambda j, i, s: (0, j)),
            pl.BlockSpec((total, 2 * HD), lambda j, i, s: (0, j)),
        ),
        scratch=[
            pltpu.VMEM((total, 4 * HD), BF),
            pltpu.VMEM((total, 4 * HD), BF),
            pltpu.VMEM((total, 2 * HD), F32),
            pltpu.VMEM((total, 2 * HD), F32),
        ],
        flops=80 * total * total * count * HD,
    )


def mix_out_kernel(local, total, info_ref, *refs):
    mine, other = refs[:2], refs[2:4]
    w_ref, bias_ref, x_ref, gain_ref, cond_ref, mix_ref, res_ref, act_ref = refs[4:]
    rows = x_ref.shape[0]
    live = live_column(rows, pl.program_id(0) * rows, info_ref, local, total).astype(F32)
    mine, other = [jnp.concatenate([r[...] for r in side], axis=1) for side in (mine, other)]
    first = info_ref[CORE] == 0
    mixture = jnp.concatenate([jnp.where(first, mine, other), jnp.where(first, other, mine)], axis=1)
    mix_ref[...] = mixture
    residual = x_ref[...].astype(F32) + live * (nn(mixture, w_ref[...]) + bias_ref[...])
    res_ref[...] = residual.astype(BF)
    normal, _ = norm_rows(residual)
    act_ref[...] = (normal * (gain_ref[...] * (1.0 + cond_ref[2:3, :])) + cond_ref[3:4, :]).astype(BF)


def mix_out(info, mine, other, weight, bias, x, gain, cond, local):
    total, width = x.shape
    block = 256
    row = lambda w: pl.BlockSpec((block, w), lambda i, s: (i, 0))
    vec = pl.BlockSpec((1, width), lambda i, s: (0, 0))
    parts = [*mine, *other]
    return call(
        functools.partial(mix_out_kernel, local, total), "mix_out", (info,), (total // block,),
        [*parts, weight, bias, x, gain, cond],
        [row(a.shape[1]) for a in parts]
        + [
            pl.BlockSpec(weight.shape, lambda i, s: (0, 0)),
            vec, row(width), vec, pl.BlockSpec(cond.shape, lambda i, s: (0, 0)),
        ],
        (sds((total, width), BF),) * 3, (row(width),) * 3,
        flops=2 * total * width * width,
    )


def raise_kernel(info_ref, act_ref, w_ref, bias_ref, hid_ref, der_ref):
    raised = nn(act_ref[...], w_ref[...]) + bias_ref[...]
    scaled = raised * 0.5**0.5
    half = 0.5 * lax.erf(scaled) + 0.5
    hid_ref[...] = (raised * half).astype(BF)
    slope = half + (raised * (2.0 * math.pi) ** -0.5) * jnp.exp2(scaled * scaled * -math.log2(math.e))
    der_ref[...] = slope.astype(BF)


def raise_up(info, act, weight, bias, block):
    total, width = act.shape
    units = weight.shape[1]
    col = pl.BlockSpec((total, block), lambda j, s: (0, j))
    return call(
        raise_kernel, "raise_up", (info,), (units // block,),
        [act, weight, bias],
        [
            pl.BlockSpec((total, width), lambda j, s: (0, 0)),
            pl.BlockSpec((width, block), lambda j, s: (0, j)),
            pl.BlockSpec((1, block), lambda j, s: (0, j)),
        ],
        (sds((total, units), BF),) * 2, (col, col),
        flops=2 * total * width * units,
    )


def weight_gradient_kernel(which, n, info_ref, *refs):
    lhs, refs = refs[: max(which) + 1], refs[max(which) + 1 :]
    rhs, outs = refs[: len(which)], refs[len(which) :]
    for group, out in enumerate(outs):

        @pl.when(pl.program_id(0) // n == group)
        def _():
            first = 0
            for k, ref in zip(which, rhs, strict=True):
                w = ref.shape[1]
                out[:, first : first + w] = tn_dot(lhs[k][...], ref[...]).astype(BF)
                first += w


def weight_gradient(info, parts, n, mb, row, col, groups, name):
    total, height = parts[0][0].shape
    width = sum(part[3] for part in parts)
    if mb % 128 or any(part[3] % 128 for part in parts):
        results = []
        for g in range(groups):
            sliced = [
                (l, lax.dynamic_slice_in_dim(r, (f(info) + col(g, info)) * w, w, 1), lambda s: 0, w)
                for l, r, f, w in parts
            ]
            every = height // 128
            (whole,) = weight_gradient(info, sliced, every, 128, lambda k, g, s: k, lambda g, s: 0, 1, name)
            rows = jnp.stack([jnp.asarray(row(k, g, info), jnp.int32) for k in range(n)])
            results.append(whole.reshape(height // mb, mb, width)[rows].reshape(n * mb, width))
        return results
    lhs = []
    for part in parts:
        if not any(part[0] is a for a in lhs):
            lhs.append(part[0])
    which = [next(k for k, a in enumerate(lhs) if a is part[0]) for part in parts]
    return call(
        functools.partial(weight_gradient_kernel, which, n), name, (info,), (n * groups,),
        [*lhs, *[part[1] for part in parts]],
        [pl.BlockSpec((total, mb), lambda i, s: (0, row(i % n, i // n, s)))] * len(lhs)
        + [
            pl.BlockSpec((total, part[3]), lambda i, s, f=part[2]: (0, f(s) + col(i // n, s))) for part in parts
        ],
        (sds((n * mb, width), BF),) * groups,
        tuple(
            pl.BlockSpec((mb, width), lambda i, s, g=g: (jnp.clip(i - g * n, 0, n - 1), 0)) for g in range(groups)
        ),
        flops=2 * total * n * mb * width * groups,
    )


def add_split_kernel(info_ref, a1_ref, b1_ref, a2_ref, b2_ref, send_ref, keep_ref):
    send_ref[...] = (a1_ref[...].astype(F32) + b1_ref[...].astype(F32)).astype(BF)
    keep_ref[...] = (a2_ref[...].astype(F32) + b2_ref[...].astype(F32)).astype(BF)


def add_split(info, a, b, bit):
    rows, width = a.shape[0] // 2, a.shape[1]
    give = pl.BlockSpec((rows, width), lambda i, s: (1 - bit(s), 0))
    keep = pl.BlockSpec((rows, width), lambda i, s: (bit(s), 0))
    out = pl.BlockSpec((rows, width), lambda i, s: (0, 0))
    return call(
        add_split_kernel, "add_split", (info,), (1,), [a, b, a, b], [give, give, keep, keep],
        (sds((rows, width), BF),) * 2, (out, out), flops=rows * width,
    )


def raise_back_kernel(info_ref, g_ref, w_ref, der_ref, out_ref, sum_ref):
    back = (nt(g_ref[...], w_ref[...]) * der_ref[...].astype(F32)).astype(BF)
    out_ref[...] = back
    sum_ref[...] = jnp.sum(back.astype(F32), axis=0, keepdims=True)


def raise_back(info, g, weight, der, block):
    total, width = g.shape
    units = weight.shape[0]
    col = pl.BlockSpec((total, block), lambda j, s: (0, j))
    return call(
        raise_back_kernel, "raise_back", (info,), (units // block,),
        [g, weight, der],
        [pl.BlockSpec((total, width), lambda j, s: (0, 0)), pl.BlockSpec((block, width), lambda j, s: (j, 0)), col],
        (sds((total, units), BF), sds((1, units), F32)),
        (col, pl.BlockSpec((1, block), lambda j, s: (0, j))),
        flops=2 * total * width * units,
    )


def rows_product_kernel(transposed, index_ref, lhs_ref, w_ref, out_ref):
    out_ref[...] = (nt if transposed else nn)(lhs_ref[...], w_ref[...]).astype(BF)


def rows_product(info, lhs, weight, n, block, row, transposed, name):
    depth = lhs.shape[1]
    width = weight.shape[0] if transposed else weight.shape[1]
    return call(
        functools.partial(rows_product_kernel, transposed), name, (info,), (n,),
        [lhs, weight],
        [pl.BlockSpec((block, depth), lambda i, s: (row(i, s), 0)), pl.BlockSpec(weight.shape, lambda i, s: (0, 0))],
        sds((n * block, width), BF),
        pl.BlockSpec((block, width), lambda i, s: (i, 0)),
        flops=2 * n * block * depth * width,
    )


def lower_kernel(local, total, info_ref, a_ref, b_ref, res_ref, bias_ref, out_ref):
    rows = out_ref.shape[0]
    first = (info_ref[HALF] * pl.num_programs(0) + pl.program_id(0)) * rows
    live = live_column(rows, first, info_ref, local, total)
    branch = a_ref[...].astype(F32) + b_ref[...].astype(F32) + bias_ref[...]
    out_ref[...] = (res_ref[...].astype(F32) + jnp.where(live, branch, 0.0)).astype(BF)


def add_branch(info, a, b, residual, bias, local):
    total, width = residual.shape
    block = 256
    n = total // 2 // block
    row = pl.BlockSpec((block, width), lambda i, s: (i, 0))
    return call(
        functools.partial(lower_kernel, local, total), "add_branch", (info,), (n,),
        [a, b, residual, bias],
        [row, row, pl.BlockSpec((block, width), lambda i, s: (s[HALF] * n + i, 0)), pl.BlockSpec((1, width), lambda i, s: (0, 0))],
        sds((total // 2, width), BF), row, flops=total * width,
    )


def norm_back(g, v, gain, scale):
    normal, inverse = norm_rows(v)
    e = g * (gain * (1.0 + scale))
    grad = inverse * (
        e - jnp.mean(e, axis=-1, keepdims=True) - normal * jnp.mean(e * normal, axis=-1, keepdims=True)
    )
    return grad, jnp.sum(g * normal, axis=0, keepdims=True), jnp.sum(g, axis=0, keepdims=True)


def accumulate(sum_ref, parts):
    block = jnp.concatenate(parts, axis=0)

    @pl.when(pl.program_id(0) == 0)
    def _():
        sum_ref[...] = block

    @pl.when(pl.program_id(0) > 0)
    def _():
        sum_ref[...] += block


def dense_norm_back_kernel(local, total, info_ref, a1_ref, a2_ref, b1_ref, b2_ref, res_ref, cot_ref, gain_ref, cond_ref, w_ref, gres_ref, gatt_ref, gmix_ref, sum_ref):
    rows = res_ref.shape[0]
    live = live_column(rows, pl.program_id(0) * rows, info_ref, local, total).astype(F32)
    early = pl.program_id(0) < pl.num_programs(0) // 2
    g = jnp.where(early, a1_ref[...].astype(F32) + b1_ref[...].astype(F32), a2_ref[...].astype(F32) + b2_ref[...].astype(F32))
    grad, by_normal, plain = norm_back(g, res_ref[...].astype(F32), gain_ref[...], cond_ref[2:3, :])
    g_residual = cot_ref[...].astype(F32) + grad
    gres_ref[...] = g_residual.astype(BF)
    g_attend = (live * g_residual).astype(BF)
    gatt_ref[...] = g_attend
    gmix_ref[...] = nt(g_attend, w_ref[...]).astype(BF)
    bias = jnp.sum(g_attend.astype(F32), axis=0, keepdims=True)
    accumulate(sum_ref, [by_normal, plain, bias, jnp.zeros((5, bias.shape[1]), F32)])


def dense_norm_back(info, a, b, residual, cot, gain, cond, weight, local):
    total, width = residual.shape
    half = weight.shape[0] // 2
    block = 256
    row = lambda w: pl.BlockSpec((block, w), lambda i, s: (i, 0))
    n = total // block // 2
    first = pl.BlockSpec((block, width), lambda i, s: (jnp.minimum(i, n - 1), 0))
    second = pl.BlockSpec((block, width), lambda i, s: (jnp.maximum(i - n, 0), 0))
    return call(
        functools.partial(dense_norm_back_kernel, local, total), "dense_norm_back", (info,), (total // block,),
        [*a, *b, residual, cot, gain, cond, weight],
        [
            first, second, first, second, row(width), row(width),
            pl.BlockSpec((1, width), lambda i, s: (0, 0)),
            pl.BlockSpec(cond.shape, lambda i, s: (0, 0)),
            pl.BlockSpec((half, width), lambda i, s: (s[CORE], 0)),
        ],
        (sds((total, width), BF), sds((total, width), BF), sds((total, half), BF), sds((8, width), F32)),
        (row(width), row(width), row(half), pl.BlockSpec((8, width), lambda i, s: (0, 0))),
        flops=2 * total * width * half,
    )


def project_back_kernel(count, index_ref, *refs):
    lhs, w_ref, out_ref = refs[:-2], refs[-2], refs[-1]
    first, total = 0, None
    for n in range(3):
        for m in range(count):
            ref = lhs[n * count + m]
            w = ref.shape[1]
            term = nt(ref[...], w_ref[:, first : first + w])
            total = term if total is None else total + term
            first += w
    out_ref[...] = total.astype(BF)


def project_back(info, parts, weight, n, block, row):
    width = weight.shape[0]
    lhs = [part[m] for m in range(3) for part in parts]
    return call(
        functools.partial(project_back_kernel, len(parts)), "project_back", (info,), (n,),
        lhs + [weight],
        [pl.BlockSpec((block, a.shape[1]), lambda i, s: (row(i, s), 0)) for a in lhs]
        + [pl.BlockSpec(weight.shape, lambda i, s: (0, 0))],
        sds((n * block, width), BF),
        pl.BlockSpec((block, width), lambda i, s: (i, 0)),
        flops=2 * n * block * weight.shape[1] * width,
    )


def attend_norm_back_kernel(info_ref, a_ref, b1_ref, b2_ref, x_ref, gres_ref, gain_ref, cond_ref, out_ref, sum_ref):
    early = pl.program_id(0) < pl.num_programs(0) // 2
    g = a_ref[...].astype(F32) + jnp.where(early, b1_ref[...].astype(F32), b2_ref[...].astype(F32))
    grad, by_normal, plain = norm_back(g, x_ref[...].astype(F32), gain_ref[...], cond_ref[0:1, :])
    out_ref[...] = (gres_ref[...].astype(F32) + grad).astype(BF)
    accumulate(sum_ref, [by_normal, plain, jnp.zeros((6, plain.shape[1]), F32)])


def attend_norm_back(info, a, b, x, g_residual, gain, cond):
    width = x.shape[1]
    block = 256
    n = a.shape[0] // block
    plain = pl.BlockSpec((block, width), lambda i, s: (i, 0))
    first = pl.BlockSpec((block, width), lambda i, s: (jnp.minimum(i, n // 2 - 1), 0))
    second = pl.BlockSpec((block, width), lambda i, s: (jnp.maximum(i - n // 2, 0), 0))
    picked = pl.BlockSpec((block, width), lambda i, s: (s[HALF] * n + i, 0))
    return call(
        attend_norm_back_kernel, "attend_norm_back", (info,), (n,),
        [a, *b, x, g_residual, gain, cond],
        [
            plain, first, second, picked, picked,
            pl.BlockSpec((1, width), lambda i, s: (0, 0)),
            pl.BlockSpec(cond.shape, lambda i, s: (0, 0)),
        ],
        (sds((n * block, width), BF), sds((8, width), F32)),
        (plain, pl.BlockSpec((8, width), lambda i, s: (0, 0))),
        flops=n * block * width,
    )


def finish_kernel(places, counts, info_ref, *refs):
    outs = refs[sum(counts) :]
    groups, at = [], 0
    for count in counts:
        groups.append(refs[at : at + count])
        at += count
    first = info_ref[CORE] == 0
    for out, group, source, width, target, stride in places:
        refs_ = groups[group]
        columns = slice(source, source + width)
        mine, other = [sum(r[side, :, columns].astype(F32) for r in refs_) for side in range(2)]
        outs[out][:, target : target + width] = jnp.where(first, mine, other)
        outs[out][:, target + stride : target + stride + width] = jnp.where(first, other, mine)


def finish(info, groups, places, widths):
    r = groups[0][0].shape[1]
    ins = [a for group in groups for a in group]
    outs = tuple(sds((r, w), F32) for w in widths)
    return call(
        functools.partial(finish_kernel, places, [len(g) for g in groups]), "finish", (info,), (1,),
        ins, [pl.BlockSpec(a.shape, lambda i, s: (0, 0, 0)) for a in ins],
        outs, tuple(pl.BlockSpec(a.shape, lambda i, s: (0, 0)) for a in outs), flops=r * sum(widths),
    )


def sinus_angles(time, features, width):
    halfway = width // 2
    rates = jnp.exp(-math.log(10000.0) * (features % halfway).astype(F32) / halfway)
    angles = time[:, None] * rates[None, :]
    return jnp.where((features < halfway)[None, :], jnp.sin(angles), jnp.cos(angles))


def body(
    dp, seq,
    tokens, time_index, lengths, time_weight, time_bias, attend_gain, query_key_value_weight,
    attention_output_weight, attend_bias, dense_gain, feedforward_up_matrix, up_bias,
    feedforward_down_matrix, down_bias, cotangent,
):
    nl, tl, d = tokens.shape
    ff = feedforward_up_matrix.shape[1]
    total = tl * seq
    chips = dp // 2
    nz = dp // 4
    i = lax.axis_index("dp")
    y = lax.axis_index("seq")
    core = i % 2
    x = (i // 2) % 2
    z = i // 4
    h = tl // 2
    half = d // 2
    fb, nb = ff // dp, dp // 2

    entry = lax.broadcasted_iota(jnp.int32, (16,), 0)
    places = {CORE: core, OFFSET: y * tl, NEAR: core == y // nl, FAR: core == 0, X: x, Z: z, HALF: core != y // nl, Y: y}
    info = jnp.zeros((16,), jnp.int32)
    for n, v in places.items():
        info = jnp.where(entry == n, jnp.asarray(v, jnp.int32), info)
    order = Order(info)
    run = order.run


    core_swap = lambda a: lax.ppermute(a, "dp", [(n, n ^ 1) for n in range(dp)])
    x_swap = lambda a: lax.ppermute(a, "dp", [(n, n ^ 2) for n in range(dp)])

    def y_shift(a, k):
        return lax.ppermute(a, "seq", [(n, (n + k) % seq) for n in range(seq)])

    def travel(k):
        pairs = []
        for chip in range(chips):
            for s in range(seq):
                target = (s + k) % seq
                pairs.append(((chip * 2 + target // nl) * seq + s, chip * 2 * seq + target))
        return pairs


    def take(a, axis, n):
        return lax.dynamic_index_in_dim(a, n, axis, keepdims=False)

    def pick(a, index):
        return lax.dynamic_index_in_dim(a, index, 0, keepdims=False)

    def in_core_order(mine, other):
        return jnp.where(core == 0, mine, other), jnp.where(core == 0, other, mine)

    def fetch_near(a):
        mine = pick(a, y % nl)
        return mine, core_swap(mine)

    def fetch_far(a):
        got = [lax.ppermute(pick(a, (y + k) % seq % nl), ("dp", "seq"), travel(k)) for k in range(1, seq)]
        return got[0] if len(got) == 1 else jnp.concatenate(got, axis=0)

    def give_back(a):
        got = [a[0]]
        for k in range(1, seq):
            pairs = []
            for chip in range(chips):
                for s in range(seq):
                    owner = s // nl
                    source = owner if k < seq // 2 else 1 - owner
                    pairs.append(((chip * 2 + source) * seq + s, (chip * 2 + owner) * seq + (s - k) % seq))
            got.append(lax.ppermute(a[k % (seq // 2)], ("dp", "seq"), pairs))
        if nl == 1 and seq == 2:
            return lambda: jnp.where(core == y, *got)[None]
        return lambda: jnp.stack([pick(jnp.stack(got), (core * nl + j - y) % seq) for j in range(nl)])

    steps = nz.bit_length() - 1

    def z_swap(a, j):
        return lax.ppermute(a, "dp", [(n, n ^ (4 << j)) for n in range(dp)])

    z_way = lambda j: (lambda s: (s[Z] >> j) & 1, 2 << j, functools.partial(z_swap, j=j))
    x_way = (lambda s: s[X], 1, x_swap)

    class Chain:
        def __init__(self, parts, mb, name, ways, along=False):
            free = ways if along else ways[1:]
            n = 2 ** len(free)

            def row(k, group, s):
                place = 0
                for t, (_, weight, _) in enumerate(free):
                    place = place + ((k >> (len(free) - 1 - t)) & 1) * weight
                if not along:
                    bit = ways[0][0](s)
                    place = place + (bit + (1 - group) * (1 - 2 * bit)) * ways[0][1]
                return place

            if along:
                parts = [(l, r, lambda s, f=f: f(s) * seq, w // seq) for l, r, f, w in parts]
                col = lambda group, s: lax.rem(s[Y] + group + 1, seq)
                out = run(weight_gradient, parts, n, mb, row, col, seq, name)
                self.came = [y_shift(a, k + 1) for k, a in enumerate(out[:-1])]
            else:
                out = run(weight_gradient, parts, n, mb, row, lambda group, s: 0, 2, name)
                self.came = [ways[0][2](out[0])]
            self.kept = out[-1]
            self.ways = list(free)

        def other(self):
            if len(self.came) == 1:
                return self.came[0]
            return sum(a.astype(F32) for a in self.came).astype(BF)

        def hop(self):
            bit, _, swap = self.ways.pop(0)
            send, self.kept = run(add_split, self.kept, self.other(), bit)
            self.came = [swap(send)]

        def last(self):
            return run(add_split, self.kept, self.other(), lambda s: s[CORE])


    far = fetch_far(tokens)
    mine = jnp.stack([pick(time_index, y % nl), pick(lengths, y % nl)])
    time, length = jnp.where(core == y // nl, mine, core_swap(mine))
    near = fetch_near(tokens)
    weight_qkv = run(own_projection, query_key_value_weight)
    own_up_bias = take(up_bias.reshape(nb, 2, fb), 1, core).reshape(1, nb * fb)
    order.info = jnp.where(entry == LENGTH, length, order.info)
    time = time.astype(F32)[None]
    table = sinus_angles(order.after(time), jnp.arange(d), d).astype(BF)
    cond = order.after((jnp.dot(table, time_weight, preferred_element_type=F32) + time_bias).reshape(4, d))
    gain1, gain2 = attend_gain[None, :], dense_gain[None, :]

    before = run(project, NEAR, *near, 0, total, gain1, cond, weight_qkv)
    cotangent = order.after(cotangent)
    near_cot = fetch_near(cotangent)
    far_cot = fetch_far(cotangent)
    weight_up, weight_down = run(own_units, feedforward_up_matrix, feedforward_down_matrix, fb)
    far = order.after(far)
    full, act1, qkv = run(project, FAR, far, core_swap(far), tl, total, gain1, cond, weight_qkv, before)
    pairs = half // (2 * HD)
    share = pairs // 2
    attended, swapped = [], []
    for n in range(2):
        attended.append(run(attend_forward, qkv, tl, n * share, share))
        swapped.append(core_swap(attended[n][0]))
        far_cot = order.after(far_cot) if n == 0 else far_cot
    cot, g_dense, g_down_bias = run(assemble, near_cot, (far_cot, core_swap(far_cot)), tl)
    mixture, residual, act2 = run(
        mix_out, [a[0] for a in attended], swapped, attention_output_weight, attend_bias[None, :],
        full, gain2, cond, tl,
    )
    hidden, slope = run(raise_up, act2, weight_up, own_up_bias, 2 * fb)

    rows_of = d // chips
    zero = lambda s: 0
    zs = [z_way(j) for j in range(steps)]
    down = Chain([(hidden, g_dense, zero, d)], fb, "down_gradient", [*zs, x_way], along=True)
    g_raised, g_up_bias = run(raise_back, g_dense, weight_down, slope, 2 * fb)
    up = Chain([(act2, g_raised, zero, fb * nb)], rows_of, "up_gradient", [x_way, *zs])
    quarters = max(2, total // 256)
    g_act2, g_act2_other = [], []
    for n in range(2):
        place = lambda i, s, n=n: n * (quarters // 2) + i
        g_act2.append(run(rows_product, g_raised, weight_up, quarters // 2, total // quarters, place, True, "raise_input_back"))
        g_act2_other.append(core_swap(g_act2[n]))

    n = max(1, total // 2 // 256)
    own_half = (n, total // 2 // n, lambda i, s: s[HALF] * n + i)
    their_half = (n, total // 2 // n, lambda i, s: (1 - s[HALF]) * n + i)
    branch_theirs = core_swap(run(rows_product, hidden, weight_down, *their_half, False, "lower"))
    branch = run(rows_product, hidden, weight_down, *own_half, False, "lower")
    g_residual, g_attend, g_mixture, sums2 = run(
        dense_norm_back, g_act2, g_act2_other, residual, cot, gain2, cond, attention_output_weight, tl
    )

    def input_gradients(n):
        back = run(attend_backward, qkv, g_mixture, *attended[n], tl, n * share, share)
        return back, [(act1, a, zero, a.shape[1]) for a in back]

    back1, in1 = input_gradients(0)
    in1 = Chain(in1 + [(mixture, g_attend, lambda s: s[CORE], half)], rows_of, "in_gradient", [zs[0], x_way, *zs[1:]])
    down.hop()
    back2, in2 = input_gradients(1)
    parts = [back1, back2]
    g_act1_theirs = []
    few = max(1, n // 2)
    for m in range(2):
        place = lambda i, s, m=m: ((1 - s[HALF]) * 2 + m) * few + i
        g_act1_theirs.append(core_swap(run(project_back, parts, weight_qkv, few, total // 4 // few, place)))
    in2 = Chain(in2, rows_of, "in_gradient", [x_way, *zs])
    up.hop()
    g_act1 = run(project_back, parts, weight_qkv, *own_half)
    result = give_back(run(add_branch, branch, branch_theirs, residual, down_bias[None, :], tl).reshape(-1, tl, d))
    down.hop()
    g_tokens, sums1 = run(attend_norm_back, g_act1, g_act1_theirs, full, g_residual, gain1, cond)
    gradient_tokens = give_back(g_tokens.reshape(-1, tl, d))
    in1.hop()

    once = jnp.where(core == 0, 1.0, 0.0)
    scales = 1.0 + cond
    up_sum = g_up_bias.reshape(nb, 1, fb)
    up_sum = jnp.concatenate(in_core_order(up_sum, jnp.zeros_like(up_sum)), axis=1).reshape(ff // d, d)
    level = jnp.where(lax.broadcasted_iota(jnp.int32, (1, d), 1) == 0, time // 256.0, time % 256.0)
    pack = jnp.concatenate(
        [
            sums1[0:1] * gain1,
            sums1[1:2],
            once * sums2[0:1] * gain2,
            once * sums2[1:2],
            once * level,
            sums1[0:1] * scales[0:1],
            once * sums2[0:1] * scales[2:3],
            once * sums2[2:3],
            once * g_down_bias[0:1],
            up_sum,
        ]
    )
    pack = order.after(pack + core_swap(pack))
    rows_each, sums = pack[:5].astype(BF), pack[5:]

    def pack_hop(rows_each, sums, swaps):
        sums = sums.astype(BF)
        packs = [swap(jnp.concatenate([rows_each, sums])) for swap in swaps]
        count = rows_each.shape[0]

        def arrive():
            rows = jnp.concatenate([rows_each] + [p[:count] for p in packs])
            return order.after((rows, sum([p[count:].astype(F32) for p in packs], sums.astype(F32))))

        return arrive

    packed = pack_hop(rows_each, sums, [x_swap])
    up.hop()
    in2.hop()
    packed = pack_hop(*packed(), [functools.partial(y_shift, k=k) for k in range(1, seq)])
    result = order.after(result())
    for _ in range(steps - 1):
        down.hop()
    packed = pack_hop(*packed(), [functools.partial(z_swap, j=0)])
    for _ in range(steps - 1):
        in1.hop()
    for _ in range(steps - 2):
        up.hop()
    down_mine = order.after((down.kept.astype(F32) + down.other().astype(F32)).astype(BF))
    down_all = jnp.stack([down_mine] + [y_shift(down_mine, k) for k in range(1, seq)])
    for j in range(1, steps):
        packed = pack_hop(*packed(), [functools.partial(z_swap, j=j)])

    def shared(chain):
        theirs, mine = chain.last()
        both = jnp.stack([mine, core_swap(theirs)])
        return [both] + [y_shift(both, k) for k in range(1, seq)]

    up_all, in1_all = shared(up), shared(in1)
    rows_each, sums = packed()
    for _ in range(steps - 1):
        in2.hop()
    gradient_tokens = order.after(gradient_tokens())
    in2_all = shared(in2)
    gradient_down = jnp.concatenate([pick(down_all, (y - n) % seq) for n in range(seq)], axis=1).astype(F32)
    (gradient_up,) = run(finish, [up_all], [(0, 0, n * fb, fb, 2 * n * fb, fb) for n in range(nb)], [ff])
    w = share * 2 * HD
    spots = [(0, n, t * w, w, (2 * t * 2 + n) * w, 2 * w) for t in range(3) for n in range(2)]
    gradient_in, gradient_out = run(
        finish, [in1_all, in2_all], spots + [(1, 0, 3 * w, half, 0, half)], [3 * d, d]
    )
    gathered = rows_each.reshape(-1, 5, d).astype(F32)
    g_cond = gathered[:, 0:4].reshape(-1, 4 * d)
    own_features = i * (d // dp) + jnp.arange(d // dp)
    times = gathered[:, 4, 0] * 256.0 + gathered[:, 4, 1]
    features = sinus_angles(times, own_features, d).astype(BF)
    gradient_time = lax.dot_general(
        features.astype(F32), g_cond, (((0,), (0,)), ((), ())), precision=lax.Precision.HIGHEST
    )
    g_time_bias = jnp.sum(g_cond, axis=0)
    part = lambda v: lax.dynamic_index_in_dim(v.reshape(dp, -1), i, 0, keepdims=False)
    return (
        result,
        gradient_tokens,
        gradient_time,
        part(g_time_bias),
        part(sums[0]),
        gradient_in,
        gradient_out,
        part(sums[2]),
        part(sums[1]),
        gradient_up,
        part(sums[4:]),
        gradient_down,
        part(sums[3]),
    )


def solution(mesh):
    whole = P()
    rows = P("dp", "seq", None)
    return jax.shard_map(
        functools.partial(body, mesh.shape["dp"], mesh.shape["seq"]),
        mesh=mesh,
        in_specs=(rows, P("dp"), P("dp"), *(whole,) * 11, rows),
        out_specs=(
            rows, rows, P("dp", None), P("dp"), P("dp"), P("dp", None), P("dp", None),
            P("dp"), P("dp"), P("dp", None), P("dp"), P("dp", None), P("dp"),
        ),
        check_vma=False,
    )
```

```python
import functools
import math

import jax
import jax.numpy as jnp
from jax import lax
from jax.experimental import pallas as pl
from jax.experimental.pallas import tpu as pltpu
from jax.sharding import PartitionSpec as P

HD = 64
CORE, OFFSET, LENGTH, NEAR, FAR, X, Z, HALF, Y, FIRST = range(10)
EPS = 1e-05
COST = 10**9
MASKED = -1e30
EXP2_SCALE = math.log2(math.e) * HD ** (-0.5)
BF = jnp.bfloat16
F32 = jnp.float32
VMEM = 20 * 1024 * 1024
ROOM = 56 * 1024 * 1024


class Order:
    def __init__(self, info):
        self.info = info
        self.open = False

    def run(self, kernel, *args):
        return self.after(kernel(self.info, *args))

    def after(self, values):
        if not self.open:
            values, self.info = lax.optimization_barrier((values, self.info))
        return values


def sds(shape, dtype):
    return jax.ShapeDtypeStruct(shape, dtype)


def nt(a, b):
    return lax.dot_general(a, b, (((1,), (1,)), ((), ())), preferred_element_type=F32)


def nn(a, b):
    return jnp.dot(a, b, preferred_element_type=F32)


def tn_dot(a, b):
    return lax.dot_general(a, b, (((0,), (0,)), ((), ())), preferred_element_type=F32)


def call(kernel, name, scalars, grid, ins, in_specs, outs, out_specs, scratch=(), flops=0, aliases=None, room=VMEM):
    return pl.pallas_call(
        kernel,
        name=name,
        grid_spec=pltpu.PrefetchScalarGridSpec(
            num_scalar_prefetch=len(scalars),
            grid=grid,
            in_specs=in_specs,
            out_specs=out_specs,
            scratch_shapes=list(scratch),
        ),
        out_shape=outs,
        input_output_aliases=aliases or {},
        compiler_params=pltpu.CompilerParams(
            vmem_limit_bytes=room, dimension_semantics=("arbitrary",) * len(grid)
        ),
        cost_estimate=pl.CostEstimate(flops=COST, bytes_accessed=1, transcendentals=0),
    )(*scalars, *ins)


def norm_rows(v):
    centre = v - jnp.mean(v, axis=-1, keepdims=True)
    inverse = lax.rsqrt(jnp.mean(centre * centre, axis=-1, keepdims=True) + EPS)
    return centre * inverse, inverse


def live_column(rows, first, info_ref, local, total):
    r = first + lax.broadcasted_iota(jnp.int32, (rows, 1), 0)
    low = lax.rem(r, local)
    start = info_ref[OFFSET] - (r - low)
    slot = jnp.where(start < 0, start + total, start) + low
    return slot < info_ref[LENGTH]


def own_units_kernel(fb, info_ref, *refs):
    up, down, (up_out, down_out) = refs[:-2:2], refs[1:-2:2], refs[-2:]
    for n, (u, w) in enumerate(zip(up, down, strict=True)):
        up_out[:, n * fb : (n + 1) * fb] = u[...]
        down_out[n * fb : (n + 1) * fb, :] = w[...]


def own_units(info, up, down, fb):
    d, ff = up.shape
    each = 2
    specs = []
    for n in range(each):
        specs.append(pl.BlockSpec((d, fb), lambda i, s, n=n: (0, 2 * (each * i + n) + s[CORE])))
        specs.append(pl.BlockSpec((fb, d), lambda i, s, n=n: (2 * (each * i + n) + s[CORE], 0)))
    return call(
        functools.partial(own_units_kernel, fb), "own_units", (info,), (ff // (2 * fb * each),), [up, down] * each, specs,
        (sds((d, ff // 2), BF), sds((ff // 2, d), BF)),
        (pl.BlockSpec((d, each * fb), lambda i, s: (0, i)), pl.BlockSpec((each * fb, d), lambda i, s: (i, 0))),
        flops=d * ff, room=ROOM,
    )


def choose(flag, a, b):
    return jnp.where(flag == 1, a, b)


def project_kernel(info_ref, n1_ref, n2_ref, f1_ref, f2_ref, gain_ref, cond_ref, wq_ref, wk_ref, wv_ref, full_ref, act_ref, qkv_ref):
    near = choose(info_ref[NEAR], n1_ref[...].astype(F32), n2_ref[...].astype(F32))
    far = choose(info_ref[FAR], f1_ref[...].astype(F32), f2_ref[...].astype(F32))
    x = jnp.where(pl.program_id(0) < info_ref[FIRST], near, far)
    full_ref[...] = x.astype(BF)
    normal, _ = norm_rows(x)
    act = (normal * (gain_ref[...] * (1.0 + cond_ref[0:1, :])) + cond_ref[1:2, :]).astype(BF)
    act_ref[...] = act
    w = wq_ref.shape[1]
    for n, ref in enumerate((wq_ref, wk_ref, wv_ref)):
        qkv_ref[:, n * w : (n + 1) * w] = nn(act, ref[...]).astype(BF)


def project(info, near, far, gain, cond, weight):
    width = near[0].shape[1]
    total = near[0].shape[0] + far[0].shape[0]
    half = weight.shape[1] // 6
    block = min(256, near[0].shape[0])
    n = near[0].shape[0] // block
    head = pl.BlockSpec((block, width), lambda i, s: (jnp.minimum(i, n - 1), 0))
    tail = pl.BlockSpec((block, width), lambda i, s: (jnp.maximum(i - n, 0), 0))
    row = lambda w: pl.BlockSpec((block, w), lambda i, s: (i, 0))
    return call(
        project_kernel, "project", (jnp.where(jnp.arange(16) == FIRST, n, info),), (total // block,),
        [*near, *far, gain, cond, weight, weight, weight],
        [
            head, head, tail, tail,
            pl.BlockSpec((1, width), lambda i, s: (0, 0)),
            pl.BlockSpec(cond.shape, lambda i, s: (0, 0)),
            *[pl.BlockSpec((width, half), lambda i, s, n=n: (0, 2 * n + s[CORE])) for n in range(3)],
        ],
        (sds((total, width), BF), sds((total, width), BF), sds((total, 3 * half), BF)),
        (row(width), row(width), row(3 * half)),
        flops=6 * total * width * half, room=ROOM,
    )


def assemble_kernel(local, total, info_ref, n1_ref, n2_ref, f1_ref, f2_ref, cot_ref, g_ref, sum_ref):
    near = choose(info_ref[NEAR], n1_ref[...].astype(F32), n2_ref[...].astype(F32))
    far = choose(info_ref[FAR], f1_ref[...].astype(F32), f2_ref[...].astype(F32))
    sums = jnp.zeros((1, near.shape[1]), F32)
    for first, piece in ((0, near), (near.shape[0], far)):
        rows = slice(first, first + piece.shape[0])
        live = live_column(piece.shape[0], first, info_ref, local, total)
        masked = jnp.where(live, piece, 0.0)
        cot_ref[rows, :] = piece.astype(BF)
        g_ref[rows, :] = masked.astype(BF)
        sums += jnp.sum(masked, axis=0, keepdims=True)
    sum_ref[...] = jnp.broadcast_to(sums, sum_ref.shape)


def assemble(info, near, far, local):
    total, width = near[0].shape[0] + far[0].shape[0], near[0].shape[1]
    whole = lambda a: pl.BlockSpec(a.shape, lambda i, s: (0, 0))
    ins = [*near, *far]
    outs = (sds((total, width), BF), sds((total, width), BF), sds((8, width), F32))
    return call(
        functools.partial(assemble_kernel, local, total), "assemble", (info,), (1,),
        ins, [whole(a) for a in ins], outs, tuple(whole(a) for a in outs), flops=total * width,
    )


def augment(main, rows, values):
    lane = lax.broadcasted_iota(jnp.int32, (1, 2 * HD), 1)
    extra = jnp.zeros((rows, 2 * HD), F32)
    for n, value in enumerate(values):
        extra = jnp.where(lane == n, value, extra)
    return jnp.concatenate([main.astype(BF), extra.astype(BF)], axis=1)


def stack_heads(pair):
    first = lax.broadcasted_iota(jnp.int32, (1, 2 * HD), 1) < HD
    zero = jnp.zeros_like(pair)
    return jnp.concatenate([jnp.where(first, pair, zero), jnp.where(first, zero, pair)], axis=0)


def merge_heads(stacked):
    rows = stacked.shape[0] // 2
    first = lax.broadcasted_iota(jnp.int32, (1, 2 * HD), 1) < HD
    return jnp.where(first, stacked[:rows], stacked[rows:])


TILE = 256


def attend_forward_kernel(local, info_ref, q_ref, k_ref, v_ref, o_ref, l_ref, ka, va):
    total = k_ref.shape[0]
    pair = pl.program_id(0)
    live = live_column(total, 0, info_ref, local, total)
    ka[...] = augment(k_ref[...], total, (jnp.where(live, 0.0, MASKED),))
    va[...] = augment(v_ref[...], total, (1.0,))

    def scores_of(start):
        return nt(augment(stack_heads(q_ref[start : start + TILE, :]), 2 * TILE, (1.0,)), ka[...])

    def mix(start, top, weights):
        rows = slice(start, start + TILE)
        mixed = nn(weights, va[...])
        sums = mixed[:, 2 * HD : 2 * HD + 1]
        o_ref[rows, :] = merge_heads(mixed[:, : 2 * HD] / sums).astype(BF)
        logs = top + jnp.log(sums) * HD**0.5
        column = lax.broadcasted_iota(jnp.int32, (1, 2 * HD), 1) - 2 * pair
        held = jnp.where(pair == 0, 0.0, l_ref[rows, :])
        l_ref[rows, :] = jnp.where(column == 0, logs[:TILE], jnp.where(column == 1, logs[TILE:], held))

    scores, waiting = scores_of(0), None
    for start in range(0, total, TILE):
        ahead = scores_of(start + TILE) if start + TILE < total else None
        top = jnp.max(scores, axis=-1, keepdims=True)
        weights = jnp.exp2((scores - top) * EXP2_SCALE).astype(BF)
        if waiting is not None:
            mix(*waiting)
        scores, waiting = ahead, (start, top, weights)
    mix(*waiting)


def attend_forward(info, qkv, local, first, count):
    total = qkv.shape[0]
    pairs = qkv.shape[1] // (6 * HD)
    out = pl.BlockSpec((total, 2 * HD), lambda j, s: (0, j))
    return call(
        functools.partial(attend_forward_kernel, local), "attend_forward", (info,), (count,),
        [qkv, qkv, qkv],
        [pl.BlockSpec((total, 2 * HD), lambda j, s, m=m: (0, m * pairs + first + j)) for m in range(3)],
        (sds((total, count * 2 * HD), BF), sds((total, 2 * HD), F32)),
        (out, pl.BlockSpec((total, 2 * HD), lambda j, s: (0, 0))),
        scratch=[pltpu.VMEM((total, 4 * HD), BF), pltpu.VMEM((total, 4 * HD), BF)],
        flops=32 * total * total * count * HD,
    )


def attend_backward_kernel(
    local, info_ref, q_ref, g_ref, o_ref, l_ref, k_ref, v_ref, gq_ref, gk_ref, gv_ref, ka, va, acck, accv
):
    total = k_ref.shape[0]

    @pl.when(pl.program_id(1) == 0)
    def _():
        live = live_column(total, 0, info_ref, local, total)
        ka[...] = augment(k_ref[...], total, (jnp.where(live, 0.0, MASKED), 1.0, 1.0, 1.0))
        va[...] = augment(v_ref[...], total, (1.0, 1.0))
        acck[...] = jnp.zeros_like(acck)
        accv[...] = jnp.zeros_like(accv)

    for start in range(0, q_ref.shape[0], TILE):
        rows = slice(start, start + TILE)
        q = stack_heads(q_ref[rows, :])
        g = stack_heads(g_ref[rows, :])
        o = o_ref[rows, :].astype(F32)
        inner = jnp.sum(g.astype(F32) * jnp.concatenate([o, o], axis=0), axis=-1, keepdims=True)
        column = lax.broadcasted_iota(jnp.int32, (1, 2 * HD), 1) - 2 * pl.program_id(0)
        logs = [jnp.sum(jnp.where(column == k, l_ref[rows, :], 0.0), axis=-1, keepdims=True) for k in range(2)]
        logs = jnp.concatenate(logs, axis=0)
        high = logs.astype(BF).astype(F32)
        middle = (logs - high).astype(BF).astype(F32)
        inner_high = inner.astype(BF).astype(F32)
        qa = augment(q, 2 * TILE, (1.0, -high, -middle, high + middle - logs))
        ga = augment(g, 2 * TILE, (-inner_high, inner_high - inner))
        probability = jnp.exp2(nt(ka[...], qa) * EXP2_SCALE)
        g_scores = (probability * nt(va[...], ga)).astype(BF)
        acck[...] += nn(g_scores, q)
        accv[...] += nn(probability.astype(BF), g)
        gq_ref[rows, :] = merge_heads(tn_dot(g_scores, k_ref[...]) * HD**-0.5).astype(BF)

    @pl.when(pl.program_id(1) == pl.num_programs(1) - 1)
    def _():
        gk_ref[...] = (acck[...] * HD**-0.5).astype(BF)
        gv_ref[...] = accv[...].astype(BF)


def attend_backward(info, qkv, g, o, logs, local, first, count):
    total = qkv.shape[0]
    pairs = qkv.shape[1] // (6 * HD)
    block = total
    part = pl.BlockSpec((block, 2 * HD), lambda j, i, s: (i, first + j))
    own = pl.BlockSpec((block, 2 * HD), lambda j, i, s: (i, j))
    return call(
        functools.partial(attend_backward_kernel, local), "attend_backward", (info,), (count, total // block),
        [qkv, g, o, logs, qkv, qkv],
        [
            part, part, own, pl.BlockSpec((total, 2 * HD), lambda j, i, s: (i, 0)),
            pl.BlockSpec((total, 2 * HD), lambda j, i, s: (0, pairs + first + j)),
            pl.BlockSpec((total, 2 * HD), lambda j, i, s: (0, 2 * pairs + first + j)),
        ],
        (sds((total, count * 2 * HD), BF),) * 3,
        (
            own,
            pl.BlockSpec((total, 2 * HD), lambda j, i, s: (0, j)),
            pl.BlockSpec((total, 2 * HD), lambda j, i, s: (0, j)),
        ),
        scratch=[
            pltpu.VMEM((total, 4 * HD), BF),
            pltpu.VMEM((total, 4 * HD), BF),
            pltpu.VMEM((total, 2 * HD), F32),
            pltpu.VMEM((total, 2 * HD), F32),
        ],
        flops=80 * total * total * count * HD,
    )


def mix_out_kernel(local, total, info_ref, *refs):
    mine, other = refs[:2], refs[2:4]
    w_ref, bias_ref, x_ref, gain_ref, cond_ref, mix_ref, res_ref, act_ref = refs[4:]
    rows = x_ref.shape[0]
    live = live_column(rows, pl.program_id(0) * rows, info_ref, local, total).astype(F32)
    mine, other = [jnp.concatenate([r[...] for r in side], axis=1) for side in (mine, other)]
    first = info_ref[CORE] == 0
    mixture = jnp.concatenate([jnp.where(first, mine, other), jnp.where(first, other, mine)], axis=1)
    mix_ref[...] = mixture
    residual = x_ref[...].astype(F32) + live * (nn(mixture, w_ref[...]) + bias_ref[...])
    res_ref[...] = residual.astype(BF)
    normal, _ = norm_rows(residual)
    act_ref[...] = (normal * (gain_ref[...] * (1.0 + cond_ref[2:3, :])) + cond_ref[3:4, :]).astype(BF)


def mix_out(info, mine, other, weight, bias, x, gain, cond, local):
    total, width = x.shape
    block = 256
    row = lambda w: pl.BlockSpec((block, w), lambda i, s: (i, 0))
    vec = pl.BlockSpec((1, width), lambda i, s: (0, 0))
    parts = [*mine, *other]
    return call(
        functools.partial(mix_out_kernel, local, total), "mix_out", (info,), (total // block,),
        [*parts, weight, bias, x, gain, cond],
        [row(a.shape[1]) for a in parts]
        + [
            pl.BlockSpec(weight.shape, lambda i, s: (0, 0)),
            vec, row(width), vec, pl.BlockSpec(cond.shape, lambda i, s: (0, 0)),
        ],
        (sds((total, width), BF),) * 3, (row(width),) * 3,
        flops=2 * total * width * width,
    )


def raise_kernel(info_ref, act_ref, w_ref, bias_ref, hid_ref, der_ref):
    raised = nn(act_ref[...], w_ref[...]) + bias_ref[...]
    scaled = raised * 0.5**0.5
    half = 0.5 * lax.erf(scaled) + 0.5
    hid_ref[...] = (raised * half).astype(BF)
    slope = half + (raised * (2.0 * math.pi) ** -0.5) * jnp.exp2(scaled * scaled * -math.log2(math.e))
    der_ref[...] = slope.astype(BF)


def raise_up(info, act, weight, bias, block):
    total, width = act.shape
    units = weight.shape[1]
    col = pl.BlockSpec((total, block), lambda j, s: (0, j))
    return call(
        raise_kernel, "raise_up", (info,), (units // block,),
        [act, weight, bias],
        [
            pl.BlockSpec((total, width), lambda j, s: (0, 0)),
            pl.BlockSpec((width, block), lambda j, s: (0, j)),
            pl.BlockSpec((1, block), lambda j, s: (0, j)),
        ],
        (sds((total, units), BF),) * 2, (col, col),
        flops=2 * total * width * units,
    )


def weight_gradient_kernel(which, per, n, wide, info_ref, *refs):
    count = max(which) + 1
    lhs, refs = refs[: count * per], refs[count * per :]
    rhs, outs = refs[: len(which) * wide], refs[len(which) * wide :]

    def left(k):
        blocks = [ref[...] for ref in lhs[k * per : (k + 1) * per]]
        return blocks[0] if per == 1 else jnp.concatenate(blocks, axis=1)

    def write(out, rhs):
        first = 0
        for k, ref in zip(which, rhs, strict=True):
            w = ref.shape[1]
            out[:, first : first + w] = tn_dot(left(k), ref[...]).astype(BF)
            first += w

    for group, out in enumerate(outs):
        if wide > 1:
            write(out, rhs[group::wide])
        else:
            pl.when(pl.program_id(0) // n == group)(lambda out=out: write(out, rhs))


def weight_gradient(info, parts, n, mb, row, col, groups, wide, name):
    total, height = parts[0][0].shape
    width = sum(part[3] for part in parts)
    if mb % 128 or any(part[3] % 128 for part in parts):
        results = []
        for g in range(groups):
            sliced = [
                (l, lax.dynamic_slice_in_dim(r, (f(info) + col(g, info)) * w, w, 1), lambda s: 0, w)
                for l, r, f, w in parts
            ]
            every = height // 128
            (whole,) = weight_gradient(info, sliced, every, 128, lambda k, g, s: k, lambda g, s: 0, 1, False, name)
            rows = jnp.stack([jnp.asarray(row(k, g, info), jnp.int32) for k in range(n)])
            results.append(whole.reshape(height // mb, mb, width)[rows].reshape(n * mb, width))
        return results
    lhs = []
    for part in parts:
        if not any(part[0] is a for a in lhs):
            lhs.append(part[0])
    which = [next(k for k, a in enumerate(lhs) if a is part[0]) for part in parts]
    per = 2 if mb < 256 and n % 2 == 0 else 1
    steps = n // per
    together = groups if wide else 1
    group = (lambda i: 0) if wide else (lambda i: i // steps)
    return call(
        functools.partial(weight_gradient_kernel, which, per, steps, together), name, (info,),
        (steps * groups // together,),
        [a for a in lhs for _ in range(per)] + [part[1] for part in parts for _ in range(together)],
        [
            pl.BlockSpec((total, mb), lambda i, s, p=p: (0, row(i % steps * per + p, group(i), s)))
            for _ in lhs
            for p in range(per)
        ]
        + [
            pl.BlockSpec(
                (total, part[3]), lambda i, s, f=part[2], g=g: (0, f(s) + col(g if wide else group(i), s))
            )
            for part in parts
            for g in range(together)
        ],
        (sds((n * mb, width), BF),) * groups,
        tuple(
            pl.BlockSpec((per * mb, width), lambda i, s, g=g: (i if wide else jnp.clip(i - g * steps, 0, steps - 1), 0))
            for g in range(groups)
        ),
        flops=2 * total * n * mb * width * groups,
    )


def add_pick_kernel(count, info_ref, *refs):
    outs = refs[-(len(refs) // (count + 1)) :]
    for k, out in enumerate(outs):
        out[...] = sum(ref[...].astype(F32) for ref in refs[k * count : (k + 1) * count]).astype(BF)


def add_pick(info, arrays, parts, picks):
    rows, width = arrays[0].shape[0] // parts, arrays[0].shape[1]
    out = pl.BlockSpec((rows, width), lambda i, s: (0, 0))
    return call(
        functools.partial(add_pick_kernel, len(arrays)), "add_pick", (info,), (1,), [*arrays] * len(picks),
        [pl.BlockSpec((rows, width), lambda i, s, f=f: (f(s), 0)) for f in picks for _ in arrays],
        (sds((rows, width), BF),) * len(picks), (out,) * len(picks), flops=rows * width,
    )


def raise_back_kernel(info_ref, g_ref, w_ref, der_ref, out_ref, sum_ref):
    back = (nt(g_ref[...], w_ref[...]) * der_ref[...].astype(F32)).astype(BF)
    out_ref[...] = back
    sum_ref[...] = jnp.sum(back.astype(F32), axis=0, keepdims=True)


def raise_back(info, g, weight, der, block):
    total, width = g.shape
    units = weight.shape[0]
    col = pl.BlockSpec((total, block), lambda j, s: (0, j))
    return call(
        raise_back_kernel, "raise_back", (info,), (units // block,),
        [g, weight, der],
        [pl.BlockSpec((total, width), lambda j, s: (0, 0)), pl.BlockSpec((block, width), lambda j, s: (j, 0)), col],
        (sds((total, units), BF), sds((1, units), F32)),
        (col, pl.BlockSpec((1, block), lambda j, s: (0, j))),
        flops=2 * total * width * units,
    )


def rows_product_kernel(transposed, index_ref, lhs_ref, w_ref, out_ref):
    out_ref[...] = (nt if transposed else nn)(lhs_ref[...], w_ref[...]).astype(BF)


def rows_product(info, lhs, weight, n, block, row, transposed, name):
    depth = lhs.shape[1]
    width = weight.shape[0] if transposed else weight.shape[1]
    return call(
        functools.partial(rows_product_kernel, transposed), name, (info,), (n,),
        [lhs, weight],
        [pl.BlockSpec((block, depth), lambda i, s: (row(i, s), 0)), pl.BlockSpec(weight.shape, lambda i, s: (0, 0))],
        sds((n * block, width), BF),
        pl.BlockSpec((block, width), lambda i, s: (i, 0)),
        flops=2 * n * block * depth * width,
    )


def lower_kernel(local, total, info_ref, a_ref, b_ref, res_ref, bias_ref, out_ref):
    rows = out_ref.shape[0]
    first = (info_ref[HALF] * pl.num_programs(0) + pl.program_id(0)) * rows
    live = live_column(rows, first, info_ref, local, total)
    branch = a_ref[...].astype(F32) + b_ref[...].astype(F32) + bias_ref[...]
    out_ref[...] = (res_ref[...].astype(F32) + jnp.where(live, branch, 0.0)).astype(BF)


def add_branch(info, a, b, residual, bias, local):
    total, width = residual.shape
    block = 256
    n = total // 2 // block
    row = pl.BlockSpec((block, width), lambda i, s: (i, 0))
    return call(
        functools.partial(lower_kernel, local, total), "add_branch", (info,), (n,),
        [a, b, residual, bias],
        [row, row, pl.BlockSpec((block, width), lambda i, s: (s[HALF] * n + i, 0)), pl.BlockSpec((1, width), lambda i, s: (0, 0))],
        sds((total // 2, width), BF), row, flops=total * width, room=ROOM,
    )


def norm_back(g, v, gain, scale):
    normal, inverse = norm_rows(v)
    e = g * (gain * (1.0 + scale))
    grad = inverse * (
        e - jnp.mean(e, axis=-1, keepdims=True) - normal * jnp.mean(e * normal, axis=-1, keepdims=True)
    )
    return grad, jnp.sum(g * normal, axis=0, keepdims=True), jnp.sum(g, axis=0, keepdims=True)


def accumulate(sum_ref, parts):
    block = jnp.concatenate(parts, axis=0)

    @pl.when(pl.program_id(0) == 0)
    def _():
        sum_ref[...] = block

    @pl.when(pl.program_id(0) > 0)
    def _():
        sum_ref[...] += block


def dense_norm_back_kernel(local, total, info_ref, a1_ref, a2_ref, b1_ref, b2_ref, res_ref, cot_ref, gain_ref, cond_ref, w_ref, gres_ref, gatt_ref, gmix_ref, sum_ref):
    rows = res_ref.shape[0]
    live = live_column(rows, pl.program_id(0) * rows, info_ref, local, total).astype(F32)
    early = pl.program_id(0) < pl.num_programs(0) // 2
    g = jnp.where(early, a1_ref[...].astype(F32) + b1_ref[...].astype(F32), a2_ref[...].astype(F32) + b2_ref[...].astype(F32))
    grad, by_normal, plain = norm_back(g, res_ref[...].astype(F32), gain_ref[...], cond_ref[2:3, :])
    g_residual = cot_ref[...].astype(F32) + grad
    gres_ref[...] = g_residual.astype(BF)
    g_attend = (live * g_residual).astype(BF)
    gatt_ref[...] = g_attend
    gmix_ref[...] = nt(g_attend, w_ref[...]).astype(BF)
    bias = jnp.sum(g_attend.astype(F32), axis=0, keepdims=True)
    accumulate(sum_ref, [by_normal, plain, bias, jnp.zeros((5, bias.shape[1]), F32)])


def dense_norm_back(info, a, b, residual, cot, gain, cond, weight, local):
    total, width = residual.shape
    half = weight.shape[0] // 2
    block = 256
    row = lambda w: pl.BlockSpec((block, w), lambda i, s: (i, 0))
    n = total // block // 2
    first = pl.BlockSpec((block, width), lambda i, s: (jnp.minimum(i, n - 1), 0))
    second = pl.BlockSpec((block, width), lambda i, s: (jnp.maximum(i - n, 0), 0))
    return call(
        functools.partial(dense_norm_back_kernel, local, total), "dense_norm_back", (info,), (total // block,),
        [*a, *b, residual, cot, gain, cond, weight],
        [
            first, second, first, second, row(width), row(width),
            pl.BlockSpec((1, width), lambda i, s: (0, 0)),
            pl.BlockSpec(cond.shape, lambda i, s: (0, 0)),
            pl.BlockSpec((half, width), lambda i, s: (s[CORE], 0)),
        ],
        (sds((total, width), BF), sds((total, width), BF), sds((total, half), BF), sds((8, width), F32)),
        (row(width), row(width), row(half), pl.BlockSpec((8, width), lambda i, s: (0, 0))),
        flops=2 * total * width * half, room=ROOM,
    )


def project_back_kernel(count, n, info_ref, *refs):
    lhs, weights, outs = refs[:-5], refs[-5:-2], refs[-2:]
    total = None
    for k in range(3):
        first = 0
        for m in range(count):
            ref = lhs[k * count + m]
            w = ref.shape[1]
            term = nt(ref[...], weights[k][:, first : first + w])
            total = term if total is None else total + term
            first += w
    for half, out in enumerate(outs):

        @pl.when(pl.program_id(0) // n == half)
        def _():
            out[...] = total.astype(BF)


def project_back(info, parts, weight):
    width, half = weight.shape[0], weight.shape[1] // 6
    total = parts[0][0].shape[0]
    block = 256
    n = total // block // 2
    lhs = [part[m] for m in range(3) for part in parts]
    return call(
        functools.partial(project_back_kernel, len(parts), n), "project_back", (info,), (2 * n,),
        lhs + [weight] * 3,
        [
            pl.BlockSpec((block, a.shape[1]), lambda i, s: (lax.rem(s[HALF] + 1 + i // n, 2) * n + i % n, 0))
            for a in lhs
        ]
        + [pl.BlockSpec((width, half), lambda i, s, m=m: (0, 2 * m + s[CORE])) for m in range(3)],
        (sds((n * block, width), BF),) * 2,
        tuple(pl.BlockSpec((block, width), lambda i, s, g=g: (jnp.clip(i - g * n, 0, n - 1), 0)) for g in range(2)),
        flops=6 * total * half * width, room=ROOM,
    )


def attend_norm_back_kernel(info_ref, a_ref, b_ref, x_ref, gres_ref, gain_ref, cond_ref, out_ref, sum_ref):
    g = a_ref[...].astype(F32) + b_ref[...].astype(F32)
    grad, by_normal, plain = norm_back(g, x_ref[...].astype(F32), gain_ref[...], cond_ref[0:1, :])
    out_ref[...] = (gres_ref[...].astype(F32) + grad).astype(BF)
    accumulate(sum_ref, [by_normal, plain, jnp.zeros((6, plain.shape[1]), F32)])


def attend_norm_back(info, a, b, x, g_residual, gain, cond):
    width = x.shape[1]
    block = 256
    n = a.shape[0] // block
    plain = pl.BlockSpec((block, width), lambda i, s: (i, 0))
    picked = pl.BlockSpec((block, width), lambda i, s: (s[HALF] * n + i, 0))
    return call(
        attend_norm_back_kernel, "attend_norm_back", (info,), (n,),
        [a, b, x, g_residual, gain, cond],
        [
            plain, plain, picked, picked,
            pl.BlockSpec((1, width), lambda i, s: (0, 0)),
            pl.BlockSpec(cond.shape, lambda i, s: (0, 0)),
        ],
        (sds((n * block, width), BF), sds((8, width), F32)),
        (plain, pl.BlockSpec((8, width), lambda i, s: (0, 0))),
        flops=n * block * width, room=ROOM,
    )


def finish_kernel(places, counts, info_ref, *refs):
    outs = refs[sum(counts) :]
    groups, at = [], 0
    for count in counts:
        groups.append(refs[at : at + count])
        at += count
    first = info_ref[CORE] == 0
    for out, group, source, width, target, stride in places:
        refs_ = groups[group]
        columns = slice(source, source + width)
        mine, other = [sum(r[side, :, columns].astype(F32) for r in refs_) for side in range(2)]
        outs[out][:, target : target + width] = jnp.where(first, mine, other)
        outs[out][:, target + stride : target + stride + width] = jnp.where(first, other, mine)


def finish(info, groups, places, widths):
    r = groups[0][0].shape[1]
    ins = [a for group in groups for a in group]
    outs = tuple(sds((r, w), F32) for w in widths)
    return call(
        functools.partial(finish_kernel, places, [len(g) for g in groups]), "finish", (info,), (1,),
        ins, [pl.BlockSpec(a.shape, lambda i, s: (0, 0, 0)) for a in ins],
        outs, tuple(pl.BlockSpec(a.shape, lambda i, s: (0, 0)) for a in outs), flops=r * sum(widths),
    )


def sinus_angles(time, features, width):
    halfway = width // 2
    rates = jnp.exp(-math.log(10000.0) * (features % halfway).astype(F32) / halfway)
    angles = time[:, None] * rates[None, :]
    return jnp.where((features < halfway)[None, :], jnp.sin(angles), jnp.cos(angles))


def body(
    dp, seq,
    tokens, time_index, lengths, time_weight, time_bias, attend_gain, query_key_value_weight,
    attention_output_weight, attend_bias, dense_gain, feedforward_up_matrix, up_bias,
    feedforward_down_matrix, down_bias, cotangent,
):
    nl, tl, d = tokens.shape
    ff = feedforward_up_matrix.shape[1]
    total = tl * seq
    chips = dp // 2
    nz = dp // 4
    i = lax.axis_index("dp")
    y = lax.axis_index("seq")
    core = i % 2
    x = (i // 2) % 2
    z = i // 4
    h = tl // 2
    half = d // 2
    fb, nb = ff // dp, dp // 2

    entry = lax.broadcasted_iota(jnp.int32, (16,), 0)
    places = {CORE: core, OFFSET: y * tl, NEAR: core == y // nl, FAR: core == 0, X: x, Z: z, HALF: core != y // nl, Y: y}
    info = jnp.zeros((16,), jnp.int32)
    for n, v in places.items():
        info = jnp.where(entry == n, jnp.asarray(v, jnp.int32), info)
    order = Order(info)
    run = order.run


    core_swap = lambda a: lax.ppermute(a, "dp", [(n, n ^ 1) for n in range(dp)])
    x_swap = lambda a: lax.ppermute(a, "dp", [(n, n ^ 2) for n in range(dp)])

    def y_shift(a, k):
        return lax.ppermute(a, "seq", [(n, (n + k) % seq) for n in range(seq)])

    def travel(k):
        pairs = []
        for chip in range(chips):
            for s in range(seq):
                target = (s + k) % seq
                pairs.append(((chip * 2 + target // nl) * seq + s, chip * 2 * seq + target))
        return pairs


    def take(a, axis, n):
        return lax.dynamic_index_in_dim(a, n, axis, keepdims=False)

    def pick(a, index):
        return lax.dynamic_index_in_dim(a, index, 0, keepdims=False)

    def in_core_order(mine, other):
        return jnp.where(core == 0, mine, other), jnp.where(core == 0, other, mine)

    def fetch_near(a):
        mine = pick(a, y % nl)
        return mine, core_swap(mine)

    def fetch_far(a):
        got = [lax.ppermute(pick(a, (y + k) % seq % nl), ("dp", "seq"), travel(k)) for k in range(1, seq)]
        return got[0] if len(got) == 1 else jnp.concatenate(got, axis=0)

    def give_back(a):
        got = [a[0]]
        for k in range(1, seq):
            pairs = []
            for chip in range(chips):
                for s in range(seq):
                    owner = s // nl
                    source = owner if k < seq // 2 else 1 - owner
                    pairs.append(((chip * 2 + source) * seq + s, (chip * 2 + owner) * seq + (s - k) % seq))
            got.append(lax.ppermute(a[k % (seq // 2)], ("dp", "seq"), pairs))
        if nl == 1 and seq == 2:
            return lambda: jnp.where(core == y, *got)[None]
        return lambda: jnp.stack([pick(jnp.stack(got), (core * nl + j - y) % seq) for j in range(nl)])

    steps = nz.bit_length() - 1

    def z_swap(a, j):
        return lax.ppermute(a, "dp", [(n, n ^ (4 << j)) for n in range(dp)])

    def two_way(own, weight, swap):
        return (2, weight, own, [lambda s: 1 - own(s)], [swap])

    def z_way(j):
        return two_way(lambda s: (s[Z] >> j) & 1, 2 << j, functools.partial(z_swap, j=j))

    def z_shift(a, k):
        return lax.ppermute(a, "dp", [(n, (n // 4 + k) % nz * 4 + n % 4) for n in range(dp)])

    x_way = two_way(lambda s: s[X], 1, x_swap)
    z_all = (
        nz, 2, lambda s: s[Z],
        [lambda s, k=k: lax.rem(s[Z] + k, nz) for k in range(1, nz)],
        [functools.partial(z_shift, k=k) for k in range(1, nz)],
    )

    class Chain:
        def __init__(self, parts, mb, name, ways, along=False):
            free = ways if along else ways[1:]
            n = math.prod(way[0] for way in free)

            def row(k, group, s):
                place = 0
                for count, weight, _, _, _ in reversed(free):
                    place = place + k % count * weight
                    k = k // count
                if not along:
                    _, weight, own, _, _ = ways[0]
                    bit = own(s)
                    place = place + (bit + (1 - group) * (1 - 2 * bit)) * weight
                return place

            if along:
                parts = [(l, r, lambda s, f=f: f(s) * seq, w // seq) for l, r, f, w in parts]
                col = lambda group, s: lax.rem(s[Y] + group + 1, seq)
                out = run(weight_gradient, parts, n, mb, row, col, seq, True, name)
                self.came = [y_shift(a, k + 1) for k, a in enumerate(out[:-1])]
            else:
                out = run(weight_gradient, parts, n, mb, row, lambda group, s: 0, 2, False, name)
                self.came = [ways[0][4][0](out[0])]
            self.kept = out[-1]
            self.ways = list(free)

        def hop(self):
            count, _, own, away, sends = self.ways.pop(0)
            out = run(add_pick, [self.kept, *self.came], count, [*away, own])
            self.came = [send(a) for send, a in zip(sends, out, strict=False)]
            self.kept = out[-1]

        def last(self):
            return run(add_pick, [self.kept, *self.came], 2, [lambda s: 1 - s[CORE], lambda s: s[CORE]])


    far = fetch_far(tokens)
    mine = jnp.stack([pick(time_index, y % nl), pick(lengths, y % nl)])
    time, length = jnp.where(core == y // nl, mine, core_swap(mine))
    near = fetch_near(tokens)
    own_up_bias = take(up_bias.reshape(nb, 2, fb), 1, core).reshape(1, nb * fb)
    order.info = jnp.where(entry == LENGTH, length, order.info)
    time = time.astype(F32)[None]
    table = sinus_angles(order.after(time), jnp.arange(d), d).astype(BF)
    cond = order.after((jnp.dot(table, time_weight, preferred_element_type=F32) + time_bias).reshape(4, d))
    gain1, gain2 = attend_gain[None, :], dense_gain[None, :]

    weight_up, weight_down = run(own_units, feedforward_up_matrix, feedforward_down_matrix, fb)
    far = order.after(far)
    far_other = core_swap(far)
    cotangent = order.after(cotangent)
    near_cot = fetch_near(cotangent)
    far_cot = fetch_far(cotangent)
    full, act1, qkv = run(project, near, (far, far_other), gain1, cond, query_key_value_weight)
    pairs = half // (2 * HD)
    share = pairs // 2
    attended, swapped = [], []
    for n in range(2):
        attended.append(run(attend_forward, qkv, tl, n * share, share))
        swapped.append(core_swap(attended[n][0]))
        far_cot = order.after(far_cot) if n == 0 else far_cot
    cot, g_dense, g_down_bias = run(assemble, near_cot, (far_cot, core_swap(far_cot)), tl)
    mixture, residual, act2 = run(
        mix_out, [a[0] for a in attended], swapped, attention_output_weight, attend_bias[None, :],
        full, gain2, cond, tl,
    )
    hidden, slope = run(raise_up, act2, weight_up, own_up_bias, 2 * fb)

    rows_of = d // chips
    zero = lambda s: 0
    zs = [z_way(j) for j in range(steps)]
    down = Chain([(hidden, g_dense, zero, d)], fb, "down_gradient", [x_way, *zs], along=True)
    g_raised, g_up_bias = run(raise_back, g_dense, weight_down, slope, 2 * fb)
    quarters = max(2, total // 256)
    g_act2, g_act2_other = [], []
    for n in range(2):
        place = lambda i, s, n=n: n * (quarters // 2) + i
        g_act2.append(run(rows_product, g_raised, weight_up, quarters // 2, total // quarters, place, True, "raise_input_back"))
        g_act2_other.append(core_swap(g_act2[n]))
    up = Chain([(act2, g_raised, zero, fb * nb)], rows_of, "up_gradient", [x_way, *zs])
    g_residual, g_attend, g_mixture, sums2 = run(
        dense_norm_back, g_act2, g_act2_other, residual, cot, gain2, cond, attention_output_weight, tl
    )

    def input_gradients(n):
        back = run(attend_backward, qkv, g_mixture, *attended[n], tl, n * share, share)
        return back, [(act1, a, zero, a.shape[1]) for a in back]

    back1, in1 = input_gradients(0)
    in1 = Chain(in1 + [(mixture, g_attend, lambda s: s[CORE], half)], rows_of, "in_gradient", [zs[0], x_way, *zs[1:]])
    down.hop()
    back2, in2 = input_gradients(1)
    g_act1_theirs, g_act1 = run(project_back, [back1, back2], query_key_value_weight)
    g_act1_theirs = core_swap(g_act1_theirs)
    in2 = Chain(in2, rows_of, "in_gradient", [x_way, z_all])
    up.hop()
    down.hop()
    g_tokens, sums1 = run(attend_norm_back, g_act1, g_act1_theirs, full, g_residual, gain1, cond)
    gradient_tokens = give_back(g_tokens.reshape(-1, tl, d))
    in1.hop()

    once = jnp.where(core == 0, 1.0, 0.0)
    scales = 1.0 + cond
    up_sum = g_up_bias.reshape(nb, 1, fb)
    up_sum = jnp.concatenate(in_core_order(up_sum, jnp.zeros_like(up_sum)), axis=1).reshape(ff // d, d)
    level = jnp.where(lax.broadcasted_iota(jnp.int32, (1, d), 1) == 0, time // 256.0, time % 256.0)
    pack = jnp.concatenate(
        [
            sums1[0:1] * gain1,
            sums1[1:2],
            once * sums2[0:1] * gain2,
            once * sums2[1:2],
            once * level,
            sums1[0:1] * scales[0:1],
            once * sums2[0:1] * scales[2:3],
            once * sums2[2:3],
            once * g_down_bias[0:1],
            up_sum,
        ]
    )
    pack = order.after(pack + core_swap(pack))
    rows_each, sums = pack[:5].astype(BF), pack[5:]

    def pack_hop(rows_each, sums, swaps):
        sums = sums.astype(BF)
        packs = [swap(jnp.concatenate([rows_each, sums])) for swap in swaps]
        count = rows_each.shape[0]

        def arrive():
            rows = jnp.concatenate([rows_each] + [p[:count] for p in packs])
            return order.after((rows, sum([p[count:].astype(F32) for p in packs], sums.astype(F32))))

        return arrive

    packed = pack_hop(rows_each, sums, [x_swap])
    n = max(1, total // 2 // 256)
    own_half = (n, total // 2 // n, lambda i, s: s[HALF] * n + i)
    their_half = (n, total // 2 // n, lambda i, s: (1 - s[HALF]) * n + i)
    branch_theirs = core_swap(run(rows_product, hidden, weight_down, *their_half, False, "lower"))
    branch = run(rows_product, hidden, weight_down, *own_half, False, "lower")
    packed = pack_hop(*packed(), [functools.partial(y_shift, k=k) for k in range(1, seq)])
    in2.hop()
    order.open = True
    result = give_back(run(add_branch, branch, branch_theirs, residual, down_bias[None, :], tl).reshape(-1, tl, d))
    packed = pack_hop(*packed(), [functools.partial(z_swap, j=0)])
    up.hop()
    for _ in range(steps - 1):
        down.hop()
        in1.hop()
    for _ in range(steps - 2):
        up.hop()
    for j in range(1, steps):
        packed = pack_hop(*packed(), [functools.partial(z_swap, j=j)])
    down_mine = order.after(sum(a.astype(F32) for a in [down.kept, *down.came]).astype(BF))
    down_all = jnp.stack([down_mine] + [y_shift(down_mine, k) for k in range(1, seq)])

    def shared(chain):
        theirs, mine = chain.last()
        both = jnp.stack([mine, core_swap(theirs)])
        return [both] + [y_shift(both, k) for k in range(1, seq)]

    up_all = shared(up)
    result = order.after(result())
    gradient_tokens = order.after(gradient_tokens())
    in2_all = shared(in2)
    rows_each, sums = packed()
    in1_all = shared(in1)
    gradient_down = jnp.concatenate([pick(down_all, (y - n) % seq) for n in range(seq)], axis=1).astype(F32)
    (gradient_up,) = run(finish, [up_all], [(0, 0, n * fb, fb, 2 * n * fb, fb) for n in range(nb)], [ff])
    w = share * 2 * HD
    spots = [(0, n, t * w, w, (2 * t * 2 + n) * w, 2 * w) for t in range(3) for n in range(2)]
    gradient_in, gradient_out = run(
        finish, [in1_all, in2_all], spots + [(1, 0, 3 * w, half, 0, half)], [3 * d, d]
    )
    gathered = rows_each.reshape(-1, 5, d).astype(F32)
    g_cond = gathered[:, 0:4].reshape(-1, 4 * d)
    own_features = i * (d // dp) + jnp.arange(d // dp)
    times = gathered[:, 4, 0] * 256.0 + gathered[:, 4, 1]
    features = sinus_angles(times, own_features, d).astype(BF)
    gradient_time = lax.dot_general(
        features.astype(F32), g_cond, (((0,), (0,)), ((), ())), precision=lax.Precision.HIGHEST
    )
    g_time_bias = jnp.sum(g_cond, axis=0)
    part = lambda v: lax.dynamic_index_in_dim(v.reshape(dp, -1), i, 0, keepdims=False)
    return (
        result,
        gradient_tokens,
        gradient_time,
        part(g_time_bias),
        part(sums[0]),
        gradient_in,
        gradient_out,
        part(sums[2]),
        part(sums[1]),
        gradient_up,
        part(sums[4:]),
        gradient_down,
        part(sums[3]),
    )


def solution(mesh):
    whole = P()
    rows = P("dp", "seq", None)
    return jax.shard_map(
        functools.partial(body, mesh.shape["dp"], mesh.shape["seq"]),
        mesh=mesh,
        in_specs=(rows, P("dp"), P("dp"), *(whole,) * 11, rows),
        out_specs=(
            rows, rows, P("dp", None), P("dp"), P("dp"), P("dp", None), P("dp", None),
            P("dp"), P("dp"), P("dp", None), P("dp"), P("dp", None), P("dp"),
        ),
        check_vma=False,
    )
```

```python
import functools
import math

import jax
import jax.numpy as jnp
from jax import lax
from jax.experimental import pallas as pl
from jax.experimental.pallas import tpu as pltpu
from jax.sharding import PartitionSpec as P

HD = 64
CORE, OFFSET, LENGTH, NEAR, FAR, X, Z, HALF, Y, FIRST = range(10)
EPS = 1e-05
COST = 10**9
MASKED = -1e30
EXP2_SCALE = math.log2(math.e) * HD ** (-0.5)
BF = jnp.bfloat16
F32 = jnp.float32
VMEM = 20 * 1024 * 1024
ROOM = 56 * 1024 * 1024


class Order:
    def __init__(self, info):
        self.info = info
        self.open = False

    def run(self, kernel, *args):
        return self.after(kernel(self.info, *args))

    def after(self, values):
        if not self.open:
            values, self.info = lax.optimization_barrier((values, self.info))
        return values


def sds(shape, dtype):
    return jax.ShapeDtypeStruct(shape, dtype)


def nt(a, b):
    return lax.dot_general(a, b, (((1,), (1,)), ((), ())), preferred_element_type=F32)


def nn(a, b):
    return jnp.dot(a, b, preferred_element_type=F32)


def tn_dot(a, b):
    return lax.dot_general(a, b, (((0,), (0,)), ((), ())), preferred_element_type=F32)


def call(kernel, name, scalars, grid, ins, in_specs, outs, out_specs, scratch=(), flops=0, aliases=None, room=VMEM):
    return pl.pallas_call(
        kernel,
        name=name,
        grid_spec=pltpu.PrefetchScalarGridSpec(
            num_scalar_prefetch=len(scalars),
            grid=grid,
            in_specs=in_specs,
            out_specs=out_specs,
            scratch_shapes=list(scratch),
        ),
        out_shape=outs,
        input_output_aliases=aliases or {},
        compiler_params=pltpu.CompilerParams(
            vmem_limit_bytes=room, dimension_semantics=("arbitrary",) * len(grid)
        ),
        cost_estimate=pl.CostEstimate(flops=COST, bytes_accessed=1, transcendentals=0),
    )(*scalars, *ins)


def norm_rows(v):
    centre = v - jnp.mean(v, axis=-1, keepdims=True)
    inverse = lax.rsqrt(jnp.mean(centre * centre, axis=-1, keepdims=True) + EPS)
    return centre * inverse, inverse


def live_column(rows, first, info_ref, local, total):
    r = first + lax.broadcasted_iota(jnp.int32, (rows, 1), 0)
    low = lax.rem(r, local)
    start = info_ref[OFFSET] - (r - low)
    slot = jnp.where(start < 0, start + total, start) + low
    return slot < info_ref[LENGTH]


def own_units_kernel(fb, info_ref, *refs):
    up, down, (up_out, down_out) = refs[:-2:2], refs[1:-2:2], refs[-2:]
    for n, (u, w) in enumerate(zip(up, down, strict=True)):
        up_out[:, n * fb : (n + 1) * fb] = u[...]
        down_out[n * fb : (n + 1) * fb, :] = w[...]


def own_units(info, up, down, fb):
    d, ff = up.shape
    each = 2
    specs = []
    for n in range(each):
        specs.append(pl.BlockSpec((d, fb), lambda i, s, n=n: (0, 2 * (each * i + n) + s[CORE])))
        specs.append(pl.BlockSpec((fb, d), lambda i, s, n=n: (2 * (each * i + n) + s[CORE], 0)))
    return call(
        functools.partial(own_units_kernel, fb), "own_units", (info,), (ff // (2 * fb * each),), [up, down] * each, specs,
        (sds((d, ff // 2), BF), sds((ff // 2, d), BF)),
        (pl.BlockSpec((d, each * fb), lambda i, s: (0, i)), pl.BlockSpec((each * fb, d), lambda i, s: (i, 0))),
        flops=d * ff, room=ROOM,
    )


def choose(flag, a, b):
    return jnp.where(flag == 1, a, b)


def project_kernel(info_ref, n1_ref, n2_ref, f1_ref, f2_ref, gain_ref, cond_ref, wq_ref, wk_ref, wv_ref, full_ref, act_ref, qkv_ref):
    near = choose(info_ref[NEAR], n1_ref[...].astype(F32), n2_ref[...].astype(F32))
    far = choose(info_ref[FAR], f1_ref[...].astype(F32), f2_ref[...].astype(F32))
    x = jnp.where(pl.program_id(0) < info_ref[FIRST], near, far)
    full_ref[...] = x.astype(BF)
    normal, _ = norm_rows(x)
    act = (normal * (gain_ref[...] * (1.0 + cond_ref[0:1, :])) + cond_ref[1:2, :]).astype(BF)
    act_ref[...] = act
    w = wq_ref.shape[1]
    for n, ref in enumerate((wq_ref, wk_ref, wv_ref)):
        qkv_ref[:, n * w : (n + 1) * w] = nn(act, ref[...]).astype(BF)


def project(info, near, far, gain, cond, weight):
    width = near[0].shape[1]
    total = near[0].shape[0] + far[0].shape[0]
    half = weight.shape[1] // 6
    block = min(256, near[0].shape[0])
    n = near[0].shape[0] // block
    head = pl.BlockSpec((block, width), lambda i, s: (jnp.minimum(i, n - 1), 0))
    tail = pl.BlockSpec((block, width), lambda i, s: (jnp.maximum(i - n, 0), 0))
    row = lambda w: pl.BlockSpec((block, w), lambda i, s: (i, 0))
    return call(
        project_kernel, "project", (jnp.where(jnp.arange(16) == FIRST, n, info),), (total // block,),
        [*near, *far, gain, cond, weight, weight, weight],
        [
            head, head, tail, tail,
            pl.BlockSpec((1, width), lambda i, s: (0, 0)),
            pl.BlockSpec(cond.shape, lambda i, s: (0, 0)),
            *[pl.BlockSpec((width, half), lambda i, s, n=n: (0, 2 * n + s[CORE])) for n in range(3)],
        ],
        (sds((total, width), BF), sds((total, width), BF), sds((total, 3 * half), BF)),
        (row(width), row(width), row(3 * half)),
        flops=6 * total * width * half, room=ROOM,
    )


def assemble_kernel(local, total, info_ref, n1_ref, n2_ref, f1_ref, f2_ref, cot_ref, g_ref, sum_ref):
    near = choose(info_ref[NEAR], n1_ref[...].astype(F32), n2_ref[...].astype(F32))
    far = choose(info_ref[FAR], f1_ref[...].astype(F32), f2_ref[...].astype(F32))
    sums = jnp.zeros((1, near.shape[1]), F32)
    for first, piece in ((0, near), (near.shape[0], far)):
        rows = slice(first, first + piece.shape[0])
        live = live_column(piece.shape[0], first, info_ref, local, total)
        masked = jnp.where(live, piece, 0.0)
        cot_ref[rows, :] = piece.astype(BF)
        g_ref[rows, :] = masked.astype(BF)
        sums += jnp.sum(masked, axis=0, keepdims=True)
    sum_ref[...] = jnp.broadcast_to(sums, sum_ref.shape)


def assemble(info, near, far, local):
    total, width = near[0].shape[0] + far[0].shape[0], near[0].shape[1]
    whole = lambda a: pl.BlockSpec(a.shape, lambda i, s: (0, 0))
    ins = [*near, *far]
    outs = (sds((total, width), BF), sds((total, width), BF), sds((8, width), F32))
    return call(
        functools.partial(assemble_kernel, local, total), "assemble", (info,), (1,),
        ins, [whole(a) for a in ins], outs, tuple(whole(a) for a in outs), flops=total * width,
    )


def augment(main, rows, values):
    lane = lax.broadcasted_iota(jnp.int32, (1, 2 * HD), 1)
    extra = jnp.zeros((rows, 2 * HD), F32)
    for n, value in enumerate(values):
        extra = jnp.where(lane == n, value, extra)
    return jnp.concatenate([main.astype(BF), extra.astype(BF)], axis=1)


def stack_heads(pair):
    first = lax.broadcasted_iota(jnp.int32, (1, 2 * HD), 1) < HD
    zero = jnp.zeros_like(pair)
    return jnp.concatenate([jnp.where(first, pair, zero), jnp.where(first, zero, pair)], axis=0)


def merge_heads(stacked):
    rows = stacked.shape[0] // 2
    first = lax.broadcasted_iota(jnp.int32, (1, 2 * HD), 1) < HD
    return jnp.where(first, stacked[:rows], stacked[rows:])


TILE = 256


def attend_forward_kernel(local, info_ref, q_ref, k_ref, v_ref, o_ref, l_ref, ka, va):
    total = k_ref.shape[0]
    pair = pl.program_id(0)
    live = live_column(total, 0, info_ref, local, total)
    ka[...] = augment(k_ref[...], total, (jnp.where(live, 0.0, MASKED),))
    va[...] = augment(v_ref[...], total, (1.0,))

    def scores_of(start):
        return nt(augment(stack_heads(q_ref[start : start + TILE, :]), 2 * TILE, (1.0,)), ka[...])

    def mix(start, top, weights):
        rows = slice(start, start + TILE)
        mixed = nn(weights, va[...])
        sums = mixed[:, 2 * HD : 2 * HD + 1]
        o_ref[rows, :] = merge_heads(mixed[:, : 2 * HD] / sums).astype(BF)
        logs = top + jnp.log(sums) * HD**0.5
        column = lax.broadcasted_iota(jnp.int32, (1, 2 * HD), 1) - 2 * pair
        held = jnp.where(pair == 0, 0.0, l_ref[rows, :])
        l_ref[rows, :] = jnp.where(column == 0, logs[:TILE], jnp.where(column == 1, logs[TILE:], held))

    scores, waiting = scores_of(0), None
    for start in range(0, total, TILE):
        ahead = scores_of(start + TILE) if start + TILE < total else None
        top = jnp.max(scores, axis=-1, keepdims=True)
        weights = jnp.exp2((scores - top) * EXP2_SCALE).astype(BF)
        if waiting is not None:
            mix(*waiting)
        scores, waiting = ahead, (start, top, weights)
    mix(*waiting)


def attend_forward(info, qkv, local, first, count):
    total = qkv.shape[0]
    pairs = qkv.shape[1] // (6 * HD)
    out = pl.BlockSpec((total, 2 * HD), lambda j, s: (0, j))
    return call(
        functools.partial(attend_forward_kernel, local), "attend_forward", (info,), (count,),
        [qkv, qkv, qkv],
        [pl.BlockSpec((total, 2 * HD), lambda j, s, m=m: (0, m * pairs + first + j)) for m in range(3)],
        (sds((total, count * 2 * HD), BF), sds((total, 2 * HD), F32)),
        (out, pl.BlockSpec((total, 2 * HD), lambda j, s: (0, 0))),
        scratch=[pltpu.VMEM((total, 4 * HD), BF), pltpu.VMEM((total, 4 * HD), BF)],
        flops=32 * total * total * count * HD,
    )


def attend_backward_kernel(
    local, info_ref, q_ref, g_ref, o_ref, l_ref, k_ref, v_ref, gq_ref, gk_ref, gv_ref, ka, va, acck, accv
):
    total = k_ref.shape[0]

    @pl.when(pl.program_id(1) == 0)
    def _():
        live = live_column(total, 0, info_ref, local, total)
        ka[...] = augment(k_ref[...], total, (jnp.where(live, 0.0, MASKED), 1.0, 1.0, 1.0))
        va[...] = augment(v_ref[...], total, (1.0, 1.0))
        acck[...] = jnp.zeros_like(acck)
        accv[...] = jnp.zeros_like(accv)

    for start in range(0, q_ref.shape[0], TILE):
        rows = slice(start, start + TILE)
        q = stack_heads(q_ref[rows, :])
        g = stack_heads(g_ref[rows, :])
        o = o_ref[rows, :].astype(F32)
        inner = jnp.sum(g.astype(F32) * jnp.concatenate([o, o], axis=0), axis=-1, keepdims=True)
        column = lax.broadcasted_iota(jnp.int32, (1, 2 * HD), 1) - 2 * pl.program_id(0)
        logs = [jnp.sum(jnp.where(column == k, l_ref[rows, :], 0.0), axis=-1, keepdims=True) for k in range(2)]
        logs = jnp.concatenate(logs, axis=0)
        high = logs.astype(BF).astype(F32)
        middle = (logs - high).astype(BF).astype(F32)
        inner_high = inner.astype(BF).astype(F32)
        qa = augment(q, 2 * TILE, (1.0, -high, -middle, high + middle - logs))
        ga = augment(g, 2 * TILE, (-inner_high, inner_high - inner))
        probability = jnp.exp2(nt(ka[...], qa) * EXP2_SCALE)
        g_scores = (probability * nt(va[...], ga)).astype(BF)
        acck[...] += nn(g_scores, q)
        accv[...] += nn(probability.astype(BF), g)
        gq_ref[rows, :] = merge_heads(tn_dot(g_scores, k_ref[...]) * HD**-0.5).astype(BF)

    @pl.when(pl.program_id(1) == pl.num_programs(1) - 1)
    def _():
        gk_ref[...] = (acck[...] * HD**-0.5).astype(BF)
        gv_ref[...] = accv[...].astype(BF)


def attend_backward(info, qkv, g, o, logs, local, first, count):
    total = qkv.shape[0]
    pairs = qkv.shape[1] // (6 * HD)
    block = total
    part = pl.BlockSpec((block, 2 * HD), lambda j, i, s: (i, first + j))
    own = pl.BlockSpec((block, 2 * HD), lambda j, i, s: (i, j))
    return call(
        functools.partial(attend_backward_kernel, local), "attend_backward", (info,), (count, total // block),
        [qkv, g, o, logs, qkv, qkv],
        [
            part, part, own, pl.BlockSpec((total, 2 * HD), lambda j, i, s: (i, 0)),
            pl.BlockSpec((total, 2 * HD), lambda j, i, s: (0, pairs + first + j)),
            pl.BlockSpec((total, 2 * HD), lambda j, i, s: (0, 2 * pairs + first + j)),
        ],
        (sds((total, count * 2 * HD), BF),) * 3,
        (
            own,
            pl.BlockSpec((total, 2 * HD), lambda j, i, s: (0, j)),
            pl.BlockSpec((total, 2 * HD), lambda j, i, s: (0, j)),
        ),
        scratch=[
            pltpu.VMEM((total, 4 * HD), BF),
            pltpu.VMEM((total, 4 * HD), BF),
            pltpu.VMEM((total, 2 * HD), F32),
            pltpu.VMEM((total, 2 * HD), F32),
        ],
        flops=80 * total * total * count * HD,
    )


def mix_out_kernel(local, total, info_ref, *refs):
    mine, other = refs[:2], refs[2:4]
    w_ref, bias_ref, x_ref, gain_ref, cond_ref, mix_ref, res_ref, act_ref = refs[4:]
    rows = x_ref.shape[0]
    live = live_column(rows, pl.program_id(0) * rows, info_ref, local, total).astype(F32)
    mine, other = [jnp.concatenate([r[...] for r in side], axis=1) for side in (mine, other)]
    first = info_ref[CORE] == 0
    mixture = jnp.concatenate([jnp.where(first, mine, other), jnp.where(first, other, mine)], axis=1)
    mix_ref[...] = mixture
    residual = x_ref[...].astype(F32) + live * (nn(mixture, w_ref[...]) + bias_ref[...])
    res_ref[...] = residual.astype(BF)
    normal, _ = norm_rows(residual)
    act_ref[...] = (normal * (gain_ref[...] * (1.0 + cond_ref[2:3, :])) + cond_ref[3:4, :]).astype(BF)


def mix_out(info, mine, other, weight, bias, x, gain, cond, local):
    total, width = x.shape
    block = 256
    row = lambda w: pl.BlockSpec((block, w), lambda i, s: (i, 0))
    vec = pl.BlockSpec((1, width), lambda i, s: (0, 0))
    parts = [*mine, *other]
    return call(
        functools.partial(mix_out_kernel, local, total), "mix_out", (info,), (total // block,),
        [*parts, weight, bias, x, gain, cond],
        [row(a.shape[1]) for a in parts]
        + [
            pl.BlockSpec(weight.shape, lambda i, s: (0, 0)),
            vec, row(width), vec, pl.BlockSpec(cond.shape, lambda i, s: (0, 0)),
        ],
        (sds((total, width), BF),) * 3, (row(width),) * 3,
        flops=2 * total * width * width,
    )


def raise_kernel(info_ref, act_ref, w_ref, bias_ref, hid_ref, der_ref):
    raised = nn(act_ref[...], w_ref[...]) + bias_ref[...]
    scaled = raised * 0.5**0.5
    half = 0.5 * lax.erf(scaled) + 0.5
    hid_ref[...] = (raised * half).astype(BF)
    slope = half + (raised * (2.0 * math.pi) ** -0.5) * jnp.exp2(scaled * scaled * -math.log2(math.e))
    der_ref[...] = slope.astype(BF)


def raise_up(info, act, weight, bias, block):
    total, width = act.shape
    units = weight.shape[1]
    col = pl.BlockSpec((total, block), lambda j, s: (0, j))
    return call(
        raise_kernel, "raise_up", (info,), (units // block,),
        [act, weight, bias],
        [
            pl.BlockSpec((total, width), lambda j, s: (0, 0)),
            pl.BlockSpec((width, block), lambda j, s: (0, j)),
            pl.BlockSpec((1, block), lambda j, s: (0, j)),
        ],
        (sds((total, units), BF),) * 2, (col, col),
        flops=2 * total * width * units,
    )


def weight_gradient_kernel(which, per, n, wide, info_ref, *refs):
    count = max(which) + 1
    lhs, refs = refs[: count * per], refs[count * per :]
    rhs, outs = refs[: len(which) * wide], refs[len(which) * wide :]

    def left(k):
        blocks = [ref[...] for ref in lhs[k * per : (k + 1) * per]]
        return blocks[0] if per == 1 else jnp.concatenate(blocks, axis=1)

    def write(out, rhs):
        first = 0
        for k, ref in zip(which, rhs, strict=True):
            w = ref.shape[1]
            out[:, first : first + w] = tn_dot(left(k), ref[...]).astype(BF)
            first += w

    for group, out in enumerate(outs):
        if wide > 1:
            write(out, rhs[group::wide])
        else:
            pl.when(pl.program_id(0) // n == group)(lambda out=out: write(out, rhs))


def weight_gradient(info, parts, n, mb, row, col, groups, wide, name):
    total, height = parts[0][0].shape
    width = sum(part[3] for part in parts)
    if mb % 128 or any(part[3] % 128 for part in parts):
        results = []
        for g in range(groups):
            sliced = [
                (l, lax.dynamic_slice_in_dim(r, (f(info) + col(g, info)) * w, w, 1), lambda s: 0, w)
                for l, r, f, w in parts
            ]
            every = height // 128
            (whole,) = weight_gradient(info, sliced, every, 128, lambda k, g, s: k, lambda g, s: 0, 1, False, name)
            rows = jnp.stack([jnp.asarray(row(k, g, info), jnp.int32) for k in range(n)])
            results.append(whole.reshape(height // mb, mb, width)[rows].reshape(n * mb, width))
        return results
    lhs = []
    for part in parts:
        if not any(part[0] is a for a in lhs):
            lhs.append(part[0])
    which = [next(k for k, a in enumerate(lhs) if a is part[0]) for part in parts]
    per = 2 if mb < 256 and n % 2 == 0 else 1
    steps = n // per
    together = groups if wide else 1
    group = (lambda i: 0) if wide else (lambda i: i // steps)
    return call(
        functools.partial(weight_gradient_kernel, which, per, steps, together), name, (info,),
        (steps * groups // together,),
        [a for a in lhs for _ in range(per)] + [part[1] for part in parts for _ in range(together)],
        [
            pl.BlockSpec((total, mb), lambda i, s, p=p: (0, row(i % steps * per + p, group(i), s)))
            for _ in lhs
            for p in range(per)
        ]
        + [
            pl.BlockSpec(
                (total, part[3]), lambda i, s, f=part[2], g=g: (0, f(s) + col(g if wide else group(i), s))
            )
            for part in parts
            for g in range(together)
        ],
        (sds((n * mb, width), BF),) * groups,
        tuple(
            pl.BlockSpec((per * mb, width), lambda i, s, g=g: (i if wide else jnp.clip(i - g * steps, 0, steps - 1), 0))
            for g in range(groups)
        ),
        flops=2 * total * n * mb * width * groups,
    )


def add_pick_kernel(count, info_ref, *refs):
    outs = refs[-(len(refs) // (count + 1)) :]
    for k, out in enumerate(outs):
        out[...] = sum(ref[...].astype(F32) for ref in refs[k * count : (k + 1) * count]).astype(BF)


def add_pick(info, arrays, parts, picks, columns=False):
    rows, width = arrays[0].shape
    rows, width = (rows, width // parts) if columns else (rows // parts, width)
    place = (lambda k: (0, k)) if columns else (lambda k: (k, 0))
    out = pl.BlockSpec((rows, width), lambda i, s: (0, 0))
    return call(
        functools.partial(add_pick_kernel, len(arrays)), "add_pick", (info,), (1,), [*arrays] * len(picks),
        [pl.BlockSpec((rows, width), lambda i, s, f=f: place(f(s))) for f in picks for _ in arrays],
        (sds((rows, width), BF),) * len(picks), (out,) * len(picks), flops=rows * width,
    )


def raise_back_kernel(info_ref, g_ref, w_ref, der_ref, out_ref, sum_ref):
    back = (nt(g_ref[...], w_ref[...]) * der_ref[...].astype(F32)).astype(BF)
    out_ref[...] = back
    sum_ref[...] = jnp.sum(back.astype(F32), axis=0, keepdims=True)


def raise_back(info, g, weight, der, block):
    total, width = g.shape
    units = weight.shape[0]
    col = pl.BlockSpec((total, block), lambda j, s: (0, j))
    return call(
        raise_back_kernel, "raise_back", (info,), (units // block,),
        [g, weight, der],
        [pl.BlockSpec((total, width), lambda j, s: (0, 0)), pl.BlockSpec((block, width), lambda j, s: (j, 0)), col],
        (sds((total, units), BF), sds((1, units), F32)),
        (col, pl.BlockSpec((1, block), lambda j, s: (0, j))),
        flops=2 * total * width * units,
    )


def rows_product_kernel(transposed, index_ref, lhs_ref, w_ref, out_ref):
    out_ref[...] = (nt if transposed else nn)(lhs_ref[...], w_ref[...]).astype(BF)


def rows_product(info, lhs, weight, n, block, row, transposed, name):
    depth = lhs.shape[1]
    width = weight.shape[0] if transposed else weight.shape[1]
    return call(
        functools.partial(rows_product_kernel, transposed), name, (info,), (n,),
        [lhs, weight],
        [pl.BlockSpec((block, depth), lambda i, s: (row(i, s), 0)), pl.BlockSpec(weight.shape, lambda i, s: (0, 0))],
        sds((n * block, width), BF),
        pl.BlockSpec((block, width), lambda i, s: (i, 0)),
        flops=2 * n * block * depth * width,
    )


def lower_kernel(local, total, info_ref, a_ref, b_ref, res_ref, bias_ref, out_ref):
    rows = out_ref.shape[0]
    first = (info_ref[HALF] * pl.num_programs(0) + pl.program_id(0)) * rows
    live = live_column(rows, first, info_ref, local, total)
    branch = a_ref[...].astype(F32) + b_ref[...].astype(F32) + bias_ref[...]
    out_ref[...] = (res_ref[...].astype(F32) + jnp.where(live, branch, 0.0)).astype(BF)


def add_branch(info, a, b, residual, bias, local):
    total, width = residual.shape
    block = 256
    n = total // 2 // block
    row = pl.BlockSpec((block, width), lambda i, s: (i, 0))
    return call(
        functools.partial(lower_kernel, local, total), "add_branch", (info,), (n,),
        [a, b, residual, bias],
        [row, row, pl.BlockSpec((block, width), lambda i, s: (s[HALF] * n + i, 0)), pl.BlockSpec((1, width), lambda i, s: (0, 0))],
        sds((total // 2, width), BF), row, flops=total * width, room=ROOM,
    )


def norm_back(g, v, gain, scale):
    normal, inverse = norm_rows(v)
    e = g * (gain * (1.0 + scale))
    grad = inverse * (
        e - jnp.mean(e, axis=-1, keepdims=True) - normal * jnp.mean(e * normal, axis=-1, keepdims=True)
    )
    return grad, jnp.sum(g * normal, axis=0, keepdims=True), jnp.sum(g, axis=0, keepdims=True)


def accumulate(sum_ref, parts):
    block = jnp.concatenate(parts, axis=0)

    @pl.when(pl.program_id(0) == 0)
    def _():
        sum_ref[...] = block

    @pl.when(pl.program_id(0) > 0)
    def _():
        sum_ref[...] += block


def dense_norm_back_kernel(local, total, info_ref, a1_ref, a2_ref, b1_ref, b2_ref, res_ref, cot_ref, gain_ref, cond_ref, w_ref, gres_ref, gatt_ref, gmix_ref, sum_ref):
    rows = res_ref.shape[0]
    live = live_column(rows, pl.program_id(0) * rows, info_ref, local, total).astype(F32)
    early = pl.program_id(0) < pl.num_programs(0) // 2
    g = jnp.where(early, a1_ref[...].astype(F32) + b1_ref[...].astype(F32), a2_ref[...].astype(F32) + b2_ref[...].astype(F32))
    grad, by_normal, plain = norm_back(g, res_ref[...].astype(F32), gain_ref[...], cond_ref[2:3, :])
    g_residual = cot_ref[...].astype(F32) + grad
    gres_ref[...] = g_residual.astype(BF)
    g_attend = (live * g_residual).astype(BF)
    gatt_ref[...] = g_attend
    gmix_ref[...] = nt(g_attend, w_ref[...]).astype(BF)
    bias = jnp.sum(g_attend.astype(F32), axis=0, keepdims=True)
    accumulate(sum_ref, [by_normal, plain, bias, jnp.zeros((5, bias.shape[1]), F32)])


def dense_norm_back(info, a, b, residual, cot, gain, cond, weight, local):
    total, width = residual.shape
    half = weight.shape[0] // 2
    block = 256
    row = lambda w: pl.BlockSpec((block, w), lambda i, s: (i, 0))
    n = total // block // 2
    first = pl.BlockSpec((block, width), lambda i, s: (jnp.minimum(i, n - 1), 0))
    second = pl.BlockSpec((block, width), lambda i, s: (jnp.maximum(i - n, 0), 0))
    return call(
        functools.partial(dense_norm_back_kernel, local, total), "dense_norm_back", (info,), (total // block,),
        [*a, *b, residual, cot, gain, cond, weight],
        [
            first, second, first, second, row(width), row(width),
            pl.BlockSpec((1, width), lambda i, s: (0, 0)),
            pl.BlockSpec(cond.shape, lambda i, s: (0, 0)),
            pl.BlockSpec((half, width), lambda i, s: (s[CORE], 0)),
        ],
        (sds((total, width), BF), sds((total, width), BF), sds((total, half), BF), sds((8, width), F32)),
        (row(width), row(width), row(half), pl.BlockSpec((8, width), lambda i, s: (0, 0))),
        flops=2 * total * width * half, room=ROOM,
    )


def project_back_kernel(count, n, info_ref, *refs):
    lhs, weights, outs = refs[:-5], refs[-5:-2], refs[-2:]
    total = None
    for k in range(3):
        first = 0
        for m in range(count):
            ref = lhs[k * count + m]
            w = ref.shape[1]
            term = nt(ref[...], weights[k][:, first : first + w])
            total = term if total is None else total + term
            first += w
    for half, out in enumerate(outs):

        @pl.when(pl.program_id(0) // n == half)
        def _():
            out[...] = total.astype(BF)


def project_back(info, parts, weight):
    width, half = weight.shape[0], weight.shape[1] // 6
    total = parts[0][0].shape[0]
    block = 256
    n = total // block // 2
    lhs = [part[m] for m in range(3) for part in parts]
    return call(
        functools.partial(project_back_kernel, len(parts), n), "project_back", (info,), (2 * n,),
        lhs + [weight] * 3,
        [
            pl.BlockSpec((block, a.shape[1]), lambda i, s: (lax.rem(s[HALF] + 1 + i // n, 2) * n + i % n, 0))
            for a in lhs
        ]
        + [pl.BlockSpec((width, half), lambda i, s, m=m: (0, 2 * m + s[CORE])) for m in range(3)],
        (sds((n * block, width), BF),) * 2,
        tuple(pl.BlockSpec((block, width), lambda i, s, g=g: (jnp.clip(i - g * n, 0, n - 1), 0)) for g in range(2)),
        flops=6 * total * half * width, room=ROOM,
    )


def attend_norm_back_kernel(info_ref, a_ref, b_ref, x_ref, gres_ref, gain_ref, cond_ref, out_ref, sum_ref):
    g = a_ref[...].astype(F32) + b_ref[...].astype(F32)
    grad, by_normal, plain = norm_back(g, x_ref[...].astype(F32), gain_ref[...], cond_ref[0:1, :])
    out_ref[...] = (gres_ref[...].astype(F32) + grad).astype(BF)
    accumulate(sum_ref, [by_normal, plain, jnp.zeros((6, plain.shape[1]), F32)])


def attend_norm_back(info, a, b, x, g_residual, gain, cond):
    width = x.shape[1]
    block = 256
    n = a.shape[0] // block
    plain = pl.BlockSpec((block, width), lambda i, s: (i, 0))
    picked = pl.BlockSpec((block, width), lambda i, s: (s[HALF] * n + i, 0))
    return call(
        attend_norm_back_kernel, "attend_norm_back", (info,), (n,),
        [a, b, x, g_residual, gain, cond],
        [
            plain, plain, picked, picked,
            pl.BlockSpec((1, width), lambda i, s: (0, 0)),
            pl.BlockSpec(cond.shape, lambda i, s: (0, 0)),
        ],
        (sds((n * block, width), BF), sds((8, width), F32)),
        (plain, pl.BlockSpec((8, width), lambda i, s: (0, 0))),
        flops=n * block * width, room=ROOM,
    )


def finish_kernel(places, counts, info_ref, *refs):
    outs = refs[sum(counts) :]
    groups, at = [], 0
    for count in counts:
        groups.append(refs[at : at + count])
        at += count
    first = info_ref[CORE] == 0
    for out, group, source, width, target, stride in places:
        refs_ = groups[group]
        columns = slice(source, source + width)
        mine, other = [sum(r[side, :, columns].astype(F32) for r in refs_) for side in range(2)]
        outs[out][:, target : target + width] = jnp.where(first, mine, other)
        outs[out][:, target + stride : target + stride + width] = jnp.where(first, other, mine)


def finish(info, groups, places, widths):
    r = groups[0][0].shape[1]
    ins = [a for group in groups for a in group]
    outs = tuple(sds((r, w), F32) for w in widths)
    return call(
        functools.partial(finish_kernel, places, [len(g) for g in groups]), "finish", (info,), (1,),
        ins, [pl.BlockSpec(a.shape, lambda i, s: (0, 0, 0)) for a in ins],
        outs, tuple(pl.BlockSpec(a.shape, lambda i, s: (0, 0)) for a in outs), flops=r * sum(widths),
    )


def sinus_angles(time, features, width):
    halfway = width // 2
    rates = jnp.exp(-math.log(10000.0) * (features % halfway).astype(F32) / halfway)
    angles = time[:, None] * rates[None, :]
    return jnp.where((features < halfway)[None, :], jnp.sin(angles), jnp.cos(angles))


def body(
    dp, seq,
    tokens, time_index, lengths, time_weight, time_bias, attend_gain, query_key_value_weight,
    attention_output_weight, attend_bias, dense_gain, feedforward_up_matrix, up_bias,
    feedforward_down_matrix, down_bias, cotangent,
):
    nl, tl, d = tokens.shape
    ff = feedforward_up_matrix.shape[1]
    total = tl * seq
    chips = dp // 2
    nz = dp // 4
    i = lax.axis_index("dp")
    y = lax.axis_index("seq")
    core = i % 2
    x = (i // 2) % 2
    z = i // 4
    h = tl // 2
    half = d // 2
    fb, nb = ff // dp, dp // 2

    entry = lax.broadcasted_iota(jnp.int32, (16,), 0)
    places = {CORE: core, OFFSET: y * tl, NEAR: core == y // nl, FAR: core == 0, X: x, Z: z, HALF: core != y // nl, Y: y}
    info = jnp.zeros((16,), jnp.int32)
    for n, v in places.items():
        info = jnp.where(entry == n, jnp.asarray(v, jnp.int32), info)
    order = Order(info)
    run = order.run


    core_swap = lambda a: lax.ppermute(a, "dp", [(n, n ^ 1) for n in range(dp)])
    x_swap = lambda a: lax.ppermute(a, "dp", [(n, n ^ 2) for n in range(dp)])

    def y_shift(a, k):
        return lax.ppermute(a, "seq", [(n, (n + k) % seq) for n in range(seq)])

    def travel(k):
        pairs = []
        for chip in range(chips):
            for s in range(seq):
                target = (s + k) % seq
                pairs.append(((chip * 2 + target // nl) * seq + s, chip * 2 * seq + target))
        return pairs


    def take(a, axis, n):
        return lax.dynamic_index_in_dim(a, n, axis, keepdims=False)

    def pick(a, index):
        return lax.dynamic_index_in_dim(a, index, 0, keepdims=False)

    def in_core_order(mine, other):
        return jnp.where(core == 0, mine, other), jnp.where(core == 0, other, mine)

    def fetch_near(a):
        mine = pick(a, y % nl)
        return mine, core_swap(mine)

    def fetch_far(a):
        got = [lax.ppermute(pick(a, (y + k) % seq % nl), ("dp", "seq"), travel(k)) for k in range(1, seq)]
        return got[0] if len(got) == 1 else jnp.concatenate(got, axis=0)

    def give_back(a):
        got = [a[0]]
        for k in range(1, seq):
            pairs = []
            for chip in range(chips):
                for s in range(seq):
                    owner = s // nl
                    source = owner if k < seq // 2 else 1 - owner
                    pairs.append(((chip * 2 + source) * seq + s, (chip * 2 + owner) * seq + (s - k) % seq))
            got.append(lax.ppermute(a[k % (seq // 2)], ("dp", "seq"), pairs))
        if nl == 1 and seq == 2:
            return lambda: jnp.where(core == y, *order.after(got))[None]
        return lambda: jnp.stack([pick(jnp.stack(got), (core * nl + j - y) % seq) for j in range(nl)])

    steps = nz.bit_length() - 1

    def z_swap(a, j):
        return lax.ppermute(a, "dp", [(n, n ^ (4 << j)) for n in range(dp)])

    def two_way(own, weight, swap):
        return (2, weight, own, [lambda s: 1 - own(s)], [swap])

    def z_way(j):
        return two_way(lambda s: (s[Z] >> j) & 1, 2 << j, functools.partial(z_swap, j=j))

    def z_shift(a, k):
        return lax.ppermute(a, "dp", [(n, (n // 4 + k) % nz * 4 + n % 4) for n in range(dp)])

    x_way = two_way(lambda s: s[X], 1, x_swap)
    z_all = (
        nz, 2, lambda s: s[Z],
        [lambda s, k=k: lax.rem(s[Z] + k, nz) for k in range(1, nz)],
        [functools.partial(z_shift, k=k) for k in range(1, nz)],
    )

    class Chain:
        def __init__(self, parts, mb, name, ways, along=False):
            free = ways if along else ways[1:]
            n = math.prod(way[0] for way in free)

            def row(k, group, s):
                place = 0
                for count, weight, _, _, _ in reversed(free):
                    place = place + k % count * weight
                    k = k // count
                if not along:
                    _, weight, own, _, _ = ways[0]
                    bit = own(s)
                    place = place + (bit + (1 - group) * (1 - 2 * bit)) * weight
                return place

            if along:
                parts = [(l, r, lambda s, f=f: f(s) * seq, w // seq) for l, r, f, w in parts]
                col = lambda group, s: lax.rem(s[Y] + group + 1, seq)
                out = run(weight_gradient, parts, n, mb, row, col, seq, True, name)
                self.came = [y_shift(a, k + 1) for k, a in enumerate(out[:-1])]
            else:
                out = run(weight_gradient, parts, n, mb, row, lambda group, s: 0, 2, False, name)
                self.came = [ways[0][4][0](out[0])]
            self.kept = out[-1]
            self.ways = list(free)

        def hop(self):
            count, _, own, away, sends = self.ways.pop(0)
            out = run(add_pick, [self.kept, *self.came], count, [*away, own])
            self.came = [send(a) for send, a in zip(sends, out, strict=False)]
            self.kept = out[-1]

        def hop_y(self):
            picks = [lambda s, k=k: lax.rem(s[Y] + k, seq) for k in range(1, seq)] + [lambda s: s[Y]]
            out = run(add_pick, [self.kept, *self.came], seq, picks, True)
            self.came = [y_shift(a, k + 1) for k, a in enumerate(out[:-1])]
            self.kept = out[-1]

        def last(self):
            return run(add_pick, [self.kept, *self.came], 2, [lambda s: 1 - s[CORE], lambda s: s[CORE]])


    far = fetch_far(tokens)
    mine = jnp.stack([pick(time_index, y % nl), pick(lengths, y % nl)])
    time, length = jnp.where(core == y // nl, mine, core_swap(mine))
    near = fetch_near(tokens)
    own_up_bias = take(up_bias.reshape(nb, 2, fb), 1, core).reshape(1, nb * fb)
    order.info = jnp.where(entry == LENGTH, length, order.info)
    time = time.astype(F32)[None]
    table = sinus_angles(order.after(time), jnp.arange(d), d).astype(BF)
    cond = order.after((jnp.dot(table, time_weight, preferred_element_type=F32) + time_bias).reshape(4, d))
    gain1, gain2 = attend_gain[None, :], dense_gain[None, :]

    weight_up, weight_down = run(own_units, feedforward_up_matrix, feedforward_down_matrix, fb)
    far = order.after(far)
    far_other = core_swap(far)
    cotangent = order.after(cotangent)
    near_cot = fetch_near(cotangent)
    far_cot = fetch_far(cotangent)
    full, act1, qkv = run(project, near, (far, far_other), gain1, cond, query_key_value_weight)
    pairs = half // (2 * HD)
    share = pairs // 2
    attended, swapped = [], []
    for n in range(2):
        attended.append(run(attend_forward, qkv, tl, n * share, share))
        swapped.append(core_swap(attended[n][0]))
        far_cot = order.after(far_cot) if n == 0 else far_cot
    cot, g_dense, g_down_bias = run(assemble, near_cot, (far_cot, core_swap(far_cot)), tl)
    mixture, residual, act2 = run(
        mix_out, [a[0] for a in attended], swapped, attention_output_weight, attend_bias[None, :],
        full, gain2, cond, tl,
    )
    hidden, slope = run(raise_up, act2, weight_up, own_up_bias, 2 * fb)

    rows_of = d // chips
    zero = lambda s: 0
    zs = [z_way(j) for j in range(steps)]
    down = Chain([(hidden, g_dense, zero, d)], fb, "down_gradient", [x_way, *zs], along=True)
    g_raised, g_up_bias = run(raise_back, g_dense, weight_down, slope, 2 * fb)
    quarters = max(2, total // 256)
    g_act2, g_act2_other = [], []
    for n in range(2):
        place = lambda i, s, n=n: n * (quarters // 2) + i
        g_act2.append(run(rows_product, g_raised, weight_up, quarters // 2, total // quarters, place, True, "raise_input_back"))
        g_act2_other.append(core_swap(g_act2[n]))
    up = Chain([(act2, g_raised, zero, fb * nb)], rows_of, "up_gradient", [x_way, *zs])
    g_residual, g_attend, g_mixture, sums2 = run(
        dense_norm_back, g_act2, g_act2_other, residual, cot, gain2, cond, attention_output_weight, tl
    )

    def input_gradients(n):
        back = run(attend_backward, qkv, g_mixture, *attended[n], tl, n * share, share)
        return back, [(act1, a, zero, a.shape[1]) for a in back]

    back1, in1 = input_gradients(0)
    in1 = Chain(in1 + [(mixture, g_attend, lambda s: s[CORE], half)], rows_of, "in_gradient", [zs[0], x_way, *zs[1:]])
    down.hop()
    back2, in2 = input_gradients(1)
    g_act1_theirs, g_act1 = run(project_back, [back1, back2], query_key_value_weight)
    g_act1_theirs = core_swap(g_act1_theirs)
    in2 = Chain(in2, rows_of, "in_gradient", [x_way, z_all])
    up.hop_y()
    down.hop()
    in1.hop()
    g_tokens, sums1 = run(attend_norm_back, g_act1, g_act1_theirs, full, g_residual, gain1, cond)
    gradient_tokens = give_back(g_tokens.reshape(-1, tl, d))

    once = jnp.where(core == 0, 1.0, 0.0)
    scales = 1.0 + cond
    up_sum = g_up_bias.reshape(nb, 1, fb)
    up_sum = jnp.concatenate(in_core_order(up_sum, jnp.zeros_like(up_sum)), axis=1).reshape(ff // d, d)
    level = jnp.where(lax.broadcasted_iota(jnp.int32, (1, d), 1) == 0, time // 256.0, time % 256.0)
    pack = jnp.concatenate(
        [
            sums1[0:1] * gain1,
            sums1[1:2],
            once * sums2[0:1] * gain2,
            once * sums2[1:2],
            once * level,
            sums1[0:1] * scales[0:1],
            once * sums2[0:1] * scales[2:3],
            once * sums2[2:3],
            once * g_down_bias[0:1],
            up_sum,
        ]
    )
    n = max(1, total // 2 // 256)
    n = 1
    own_half = (n, total // 2 // n, lambda i, s: s[HALF] * n + i)
    their_half = (n, total // 2 // n, lambda i, s: (1 - s[HALF]) * n + i)
    pack = order.after(pack)
    swapped = core_swap(pack)

    def pack_hop(rows_each, sums, swaps):
        packs = [swap(jnp.concatenate([rows_each, sums])) for swap in swaps]
        count = rows_each.shape[0]

        def arrive():
            came = order.after(packs)
            rows = jnp.concatenate([rows_each] + [p[:count] for p in came])
            return order.after((rows, sum([p[count:].astype(F32) for p in came], sums.astype(F32)).astype(BF)))

        return arrive

    y_ways = [functools.partial(y_shift, k=k) for k in range(1, seq)]
    pack = pack + order.after(swapped)
    packed = pack_hop(*order.after((pack[:5].astype(BF), pack[5:].astype(BF))), [x_swap])
    in2.hop()
    up.hop()
    branch_theirs = core_swap(run(rows_product, hidden, weight_down, *their_half, False, "lower"))
    packed = pack_hop(*packed(), y_ways)
    for _ in range(steps - 1):
        down.hop()
        in1.hop()
    for _ in range(steps - 1):
        up.hop()
    branch = run(rows_product, hidden, weight_down, *own_half, False, "lower")
    packed = pack_hop(*packed(), [functools.partial(z_swap, j=0)])
    result = give_back(run(add_branch, branch, branch_theirs, residual, down_bias[None, :], tl).reshape(-1, tl, d))
    for j in range(1, steps):
        packed = pack_hop(*packed(), [functools.partial(z_swap, j=j)])
    gradient_tokens = order.after(gradient_tokens())

    def core_shared(chain):
        theirs, mine = chain.last()
        return mine, core_swap(theirs)

    def shared(mine, other):
        both = order.after(jnp.stack([mine, order.after(other)]))
        return [both] + [y_shift(both, k) for k in range(1, seq)]

    in2_all = core_shared(in2)
    up_all = core_shared(up)
    in1_all = core_shared(in1)
    in2_all = shared(*in2_all)
    up_all = shared(*up_all)
    down_parts = order.after([down.kept, *down.came])
    down_mine = order.after(sum(a.astype(F32) for a in down_parts).astype(BF))
    down_all = [down_mine] + [y_shift(down_mine, k) for k in range(1, seq)]
    in1_all = shared(*in1_all)
    rows_each, sums = packed()
    sums = sums.astype(F32)
    result = order.after(result())
    order.open = True
    down_all = jnp.stack(down_all)
    gradient_down = jnp.concatenate([pick(down_all, (y - n) % seq) for n in range(seq)], axis=1).astype(F32)
    up_all = [pick(jnp.stack(up_all), (y - n) % seq) for n in range(seq)]
    up_all = [jnp.concatenate(up_all, axis=2)]
    (gradient_up,) = run(finish, [up_all], [(0, 0, n * fb, fb, 2 * n * fb, fb) for n in range(nb)], [ff])
    w = share * 2 * HD
    spots = [(0, n, t * w, w, (2 * t * 2 + n) * w, 2 * w) for t in range(3) for n in range(2)]
    gradient_in, gradient_out = run(
        finish, [in1_all, in2_all], spots + [(1, 0, 3 * w, half, 0, half)], [3 * d, d]
    )
    gathered = rows_each.reshape(-1, 5, d).astype(F32)
    g_cond = gathered[:, 0:4].reshape(-1, 4 * d)
    own_features = i * (d // dp) + jnp.arange(d // dp)
    times = gathered[:, 4, 0] * 256.0 + gathered[:, 4, 1]
    features = sinus_angles(times, own_features, d).astype(BF)
    gradient_time = lax.dot_general(
        features.astype(F32), g_cond, (((0,), (0,)), ((), ())), precision=lax.Precision.HIGHEST
    )
    g_time_bias = jnp.sum(g_cond, axis=0)
    part = lambda v: lax.dynamic_index_in_dim(v.reshape(dp, -1), i, 0, keepdims=False)
    return (
        result,
        gradient_tokens,
        gradient_time,
        part(g_time_bias),
        part(sums[0]),
        gradient_in,
        gradient_out,
        part(sums[2]),
        part(sums[1]),
        gradient_up,
        part(sums[4:]),
        gradient_down,
        part(sums[3]),
    )


def solution(mesh):
    whole = P()
    rows = P("dp", "seq", None)
    return jax.shard_map(
        functools.partial(body, mesh.shape["dp"], mesh.shape["seq"]),
        mesh=mesh,
        in_specs=(rows, P("dp"), P("dp"), *(whole,) * 11, rows),
        out_specs=(
            rows, rows, P("dp", None), P("dp"), P("dp"), P("dp", None), P("dp", None),
            P("dp"), P("dp"), P("dp", None), P("dp"), P("dp", None), P("dp"),
        ),
        check_vma=False,
    )
```

```python
import functools
import math

import jax
import jax.numpy as jnp
from jax import lax
from jax.experimental import pallas as pl
from jax.experimental.pallas import tpu as pltpu
from jax.sharding import PartitionSpec as P

HD = 64
CORE, OFFSET, LENGTH, NEAR, FAR, X, Z, HALF, Y, FIRST = range(10)
EPS = 1e-05
COST = 8 * 10**8
MASKED = -1e30
EXP2_SCALE = math.log2(math.e) * HD ** (-0.5)
BF = jnp.bfloat16
F32 = jnp.float32
VMEM = 20 * 1024 * 1024
ROOM = 56 * 1024 * 1024


class Order:
    def __init__(self, info):
        self.info = info
        self.open = False

    def run(self, kernel, *args):
        return self.after(kernel(self.info, *args))

    def after(self, values):
        if not self.open:
            values, self.info = lax.optimization_barrier((values, self.info))
        return values


def sds(shape, dtype):
    return jax.ShapeDtypeStruct(shape, dtype)


def nt(a, b):
    return lax.dot_general(a, b, (((1,), (1,)), ((), ())), preferred_element_type=F32)


def nn(a, b):
    return jnp.dot(a, b, preferred_element_type=F32)


def tn_dot(a, b):
    return lax.dot_general(a, b, (((0,), (0,)), ((), ())), preferred_element_type=F32)


def call(kernel, name, scalars, grid, ins, in_specs, outs, out_specs, scratch=(), flops=0, aliases=None, room=VMEM):
    return pl.pallas_call(
        kernel,
        name=name,
        grid_spec=pltpu.PrefetchScalarGridSpec(
            num_scalar_prefetch=len(scalars),
            grid=grid,
            in_specs=in_specs,
            out_specs=out_specs,
            scratch_shapes=list(scratch),
        ),
        out_shape=outs,
        input_output_aliases=aliases or {},
        compiler_params=pltpu.CompilerParams(
            vmem_limit_bytes=room, dimension_semantics=("arbitrary",) * len(grid)
        ),
        cost_estimate=pl.CostEstimate(flops=COST, bytes_accessed=1, transcendentals=0),
    )(*scalars, *ins)


def norm_rows(v):
    centre = v - jnp.mean(v, axis=-1, keepdims=True)
    inverse = lax.rsqrt(jnp.mean(centre * centre, axis=-1, keepdims=True) + EPS)
    return centre * inverse, inverse


def live_column(rows, first, info_ref, local, total):
    r = first + lax.broadcasted_iota(jnp.int32, (rows, 1), 0)
    low = lax.rem(r, local)
    start = info_ref[OFFSET] - (r - low)
    slot = jnp.where(start < 0, start + total, start) + low
    return slot < info_ref[LENGTH]


def own_units_kernel(fb, info_ref, *refs):
    up, down, (up_out, down_out) = refs[:-2:2], refs[1:-2:2], refs[-2:]
    for n, (u, w) in enumerate(zip(up, down, strict=True)):
        up_out[:, n * fb : (n + 1) * fb] = u[...]
        down_out[n * fb : (n + 1) * fb, :] = w[...]


def own_units(info, up, down, fb):
    d, ff = up.shape
    each = 2
    specs = []
    for n in range(each):
        specs.append(pl.BlockSpec((d, fb), lambda i, s, n=n: (0, 2 * (each * i + n) + s[CORE])))
        specs.append(pl.BlockSpec((fb, d), lambda i, s, n=n: (2 * (each * i + n) + s[CORE], 0)))
    return call(
        functools.partial(own_units_kernel, fb), "own_units", (info,), (ff // (2 * fb * each),), [up, down] * each, specs,
        (sds((d, ff // 2), BF), sds((ff // 2, d), BF)),
        (pl.BlockSpec((d, each * fb), lambda i, s: (0, i)), pl.BlockSpec((each * fb, d), lambda i, s: (i, 0))),
        flops=d * ff, room=ROOM,
    )


def choose(flag, a, b):
    return jnp.where(flag == 1, a, b)


def project_kernel(info_ref, n1_ref, n2_ref, f1_ref, f2_ref, gain_ref, cond_ref, wq_ref, wk_ref, wv_ref, full_ref, act_ref, qkv_ref):
    near = choose(info_ref[NEAR], n1_ref[...].astype(F32), n2_ref[...].astype(F32))
    far = choose(info_ref[FAR], f1_ref[...].astype(F32), f2_ref[...].astype(F32))
    x = jnp.where(pl.program_id(0) < info_ref[FIRST], near, far)
    full_ref[...] = x.astype(BF)
    normal, _ = norm_rows(x)
    act = (normal * (gain_ref[...] * (1.0 + cond_ref[0:1, :])) + cond_ref[1:2, :]).astype(BF)
    act_ref[...] = act
    w = wq_ref.shape[1]
    for n, ref in enumerate((wq_ref, wk_ref, wv_ref)):
        qkv_ref[:, n * w : (n + 1) * w] = nn(act, ref[...]).astype(BF)


def project(info, near, far, gain, cond, weight):
    width = near[0].shape[1]
    total = near[0].shape[0] + far[0].shape[0]
    half = weight.shape[1] // 6
    block = min(256, near[0].shape[0])
    n = near[0].shape[0] // block
    head = pl.BlockSpec((block, width), lambda i, s: (jnp.minimum(i, n - 1), 0))
    tail = pl.BlockSpec((block, width), lambda i, s: (jnp.maximum(i - n, 0), 0))
    row = lambda w: pl.BlockSpec((block, w), lambda i, s: (i, 0))
    return call(
        project_kernel, "project", (jnp.where(jnp.arange(16) == FIRST, n, info),), (total // block,),
        [*near, *far, gain, cond, weight, weight, weight],
        [
            head, head, tail, tail,
            pl.BlockSpec((1, width), lambda i, s: (0, 0)),
            pl.BlockSpec(cond.shape, lambda i, s: (0, 0)),
            *[pl.BlockSpec((width, half), lambda i, s, n=n: (0, 2 * n + s[CORE])) for n in range(3)],
        ],
        (sds((total, width), BF), sds((total, width), BF), sds((total, 3 * half), BF)),
        (row(width), row(width), row(3 * half)),
        flops=6 * total * width * half, room=ROOM,
    )


def assemble_kernel(local, total, info_ref, n1_ref, n2_ref, f1_ref, f2_ref, cot_ref, g_ref, sum_ref):
    near = choose(info_ref[NEAR], n1_ref[...].astype(F32), n2_ref[...].astype(F32))
    far = choose(info_ref[FAR], f1_ref[...].astype(F32), f2_ref[...].astype(F32))
    sums = jnp.zeros((1, near.shape[1]), F32)
    for first, piece in ((0, near), (near.shape[0], far)):
        rows = slice(first, first + piece.shape[0])
        live = live_column(piece.shape[0], first, info_ref, local, total)
        masked = jnp.where(live, piece, 0.0)
        cot_ref[rows, :] = piece.astype(BF)
        g_ref[rows, :] = masked.astype(BF)
        sums += jnp.sum(masked, axis=0, keepdims=True)
    sum_ref[...] = jnp.broadcast_to(sums, sum_ref.shape)


def assemble(info, near, far, local):
    total, width = near[0].shape[0] + far[0].shape[0], near[0].shape[1]
    whole = lambda a: pl.BlockSpec(a.shape, lambda i, s: (0, 0))
    ins = [*near, *far]
    outs = (sds((total, width), BF), sds((total, width), BF), sds((8, width), F32))
    return call(
        functools.partial(assemble_kernel, local, total), "assemble", (info,), (1,),
        ins, [whole(a) for a in ins], outs, tuple(whole(a) for a in outs), flops=total * width,
    )


def augment(main, rows, values):
    lane = lax.broadcasted_iota(jnp.int32, (1, 2 * HD), 1)
    extra = jnp.zeros((rows, 2 * HD), F32)
    for n, value in enumerate(values):
        extra = jnp.where(lane == n, value, extra)
    return jnp.concatenate([main.astype(BF), extra.astype(BF)], axis=1)


def stack_heads(pair):
    first = lax.broadcasted_iota(jnp.int32, (1, 2 * HD), 1) < HD
    zero = jnp.zeros_like(pair)
    return jnp.concatenate([jnp.where(first, pair, zero), jnp.where(first, zero, pair)], axis=0)


def merge_heads(stacked):
    rows = stacked.shape[0] // 2
    first = lax.broadcasted_iota(jnp.int32, (1, 2 * HD), 1) < HD
    return jnp.where(first, stacked[:rows], stacked[rows:])


TILE = 256


def attend_forward_kernel(local, info_ref, q_ref, k_ref, v_ref, o_ref, l_ref, ka, va):
    total = k_ref.shape[0]
    pair = pl.program_id(0)
    live = live_column(total, 0, info_ref, local, total)
    ka[...] = augment(k_ref[...], total, (jnp.where(live, 0.0, MASKED),))
    va[...] = augment(v_ref[...], total, (1.0,))

    def scores_of(start):
        return nt(augment(stack_heads(q_ref[start : start + TILE, :]), 2 * TILE, (1.0,)), ka[...])

    def mix(start, top, weights):
        rows = slice(start, start + TILE)
        mixed = nn(weights, va[...])
        sums = mixed[:, 2 * HD : 2 * HD + 1]
        o_ref[rows, :] = merge_heads(mixed[:, : 2 * HD] / sums).astype(BF)
        logs = top + jnp.log(sums) * HD**0.5
        column = lax.broadcasted_iota(jnp.int32, (1, 2 * HD), 1) - 2 * pair
        held = jnp.where(pair == 0, 0.0, l_ref[rows, :])
        l_ref[rows, :] = jnp.where(column == 0, logs[:TILE], jnp.where(column == 1, logs[TILE:], held))

    scores, waiting = scores_of(0), None
    for start in range(0, total, TILE):
        ahead = scores_of(start + TILE) if start + TILE < total else None
        top = jnp.max(scores, axis=-1, keepdims=True)
        weights = jnp.exp2((scores - top) * EXP2_SCALE).astype(BF)
        if waiting is not None:
            mix(*waiting)
        scores, waiting = ahead, (start, top, weights)
    mix(*waiting)


def attend_forward(info, qkv, local, first, count):
    total = qkv.shape[0]
    pairs = qkv.shape[1] // (6 * HD)
    out = pl.BlockSpec((total, 2 * HD), lambda j, s: (0, j))
    return call(
        functools.partial(attend_forward_kernel, local), "attend_forward", (info,), (count,),
        [qkv, qkv, qkv],
        [pl.BlockSpec((total, 2 * HD), lambda j, s, m=m: (0, m * pairs + first + j)) for m in range(3)],
        (sds((total, count * 2 * HD), BF), sds((total, 2 * HD), F32)),
        (out, pl.BlockSpec((total, 2 * HD), lambda j, s: (0, 0))),
        scratch=[pltpu.VMEM((total, 4 * HD), BF), pltpu.VMEM((total, 4 * HD), BF)],
        flops=32 * total * total * count * HD,
    )


def attend_backward_kernel(
    local, info_ref, q_ref, g_ref, o_ref, l_ref, k_ref, v_ref, gq_ref, gk_ref, gv_ref, ka, va, acck, accv
):
    total = k_ref.shape[0]

    @pl.when(pl.program_id(1) == 0)
    def _():
        live = live_column(total, 0, info_ref, local, total)
        ka[...] = augment(k_ref[...], total, (jnp.where(live, 0.0, MASKED), 1.0, 1.0, 1.0))
        va[...] = augment(v_ref[...], total, (1.0, 1.0))
        acck[...] = jnp.zeros_like(acck)
        accv[...] = jnp.zeros_like(accv)

    for start in range(0, q_ref.shape[0], TILE):
        rows = slice(start, start + TILE)
        q = stack_heads(q_ref[rows, :])
        g = stack_heads(g_ref[rows, :])
        o = o_ref[rows, :].astype(F32)
        inner = jnp.sum(g.astype(F32) * jnp.concatenate([o, o], axis=0), axis=-1, keepdims=True)
        column = lax.broadcasted_iota(jnp.int32, (1, 2 * HD), 1) - 2 * pl.program_id(0)
        logs = [jnp.sum(jnp.where(column == k, l_ref[rows, :], 0.0), axis=-1, keepdims=True) for k in range(2)]
        logs = jnp.concatenate(logs, axis=0)
        high = logs.astype(BF).astype(F32)
        middle = (logs - high).astype(BF).astype(F32)
        inner_high = inner.astype(BF).astype(F32)
        qa = augment(q, 2 * TILE, (1.0, -high, -middle, high + middle - logs))
        ga = augment(g, 2 * TILE, (-inner_high, inner_high - inner))
        probability = jnp.exp2(nt(ka[...], qa) * EXP2_SCALE)
        g_scores = (probability * nt(va[...], ga)).astype(BF)
        acck[...] += nn(g_scores, q)
        accv[...] += nn(probability.astype(BF), g)
        gq_ref[rows, :] = merge_heads(tn_dot(g_scores, k_ref[...]) * HD**-0.5).astype(BF)

    @pl.when(pl.program_id(1) == pl.num_programs(1) - 1)
    def _():
        gk_ref[...] = (acck[...] * HD**-0.5).astype(BF)
        gv_ref[...] = accv[...].astype(BF)


def attend_backward(info, qkv, g, o, logs, local, first, count):
    total = qkv.shape[0]
    pairs = qkv.shape[1] // (6 * HD)
    block = total
    part = pl.BlockSpec((block, 2 * HD), lambda j, i, s: (i, first + j))
    own = pl.BlockSpec((block, 2 * HD), lambda j, i, s: (i, j))
    return call(
        functools.partial(attend_backward_kernel, local), "attend_backward", (info,), (count, total // block),
        [qkv, g, o, logs, qkv, qkv],
        [
            part, part, own, pl.BlockSpec((total, 2 * HD), lambda j, i, s: (i, 0)),
            pl.BlockSpec((total, 2 * HD), lambda j, i, s: (0, pairs + first + j)),
            pl.BlockSpec((total, 2 * HD), lambda j, i, s: (0, 2 * pairs + first + j)),
        ],
        (sds((total, count * 2 * HD), BF),) * 3,
        (
            own,
            pl.BlockSpec((total, 2 * HD), lambda j, i, s: (0, j)),
            pl.BlockSpec((total, 2 * HD), lambda j, i, s: (0, j)),
        ),
        scratch=[
            pltpu.VMEM((total, 4 * HD), BF),
            pltpu.VMEM((total, 4 * HD), BF),
            pltpu.VMEM((total, 2 * HD), F32),
            pltpu.VMEM((total, 2 * HD), F32),
        ],
        flops=80 * total * total * count * HD,
    )


def mix_out_kernel(local, total, info_ref, *refs):
    mine, other = refs[:2], refs[2:4]
    w_ref, bias_ref, x_ref, gain_ref, cond_ref, mix_ref, res_ref, act_ref = refs[4:]
    rows = x_ref.shape[0]
    live = live_column(rows, pl.program_id(0) * rows, info_ref, local, total).astype(F32)
    mine, other = [jnp.concatenate([r[...] for r in side], axis=1) for side in (mine, other)]
    first = info_ref[CORE] == 0
    mixture = jnp.concatenate([jnp.where(first, mine, other), jnp.where(first, other, mine)], axis=1)
    mix_ref[...] = mixture
    residual = x_ref[...].astype(F32) + live * (nn(mixture, w_ref[...]) + bias_ref[...])
    res_ref[...] = residual.astype(BF)
    normal, _ = norm_rows(residual)
    act_ref[...] = (normal * (gain_ref[...] * (1.0 + cond_ref[2:3, :])) + cond_ref[3:4, :]).astype(BF)


def mix_out(info, mine, other, weight, bias, x, gain, cond, local):
    total, width = x.shape
    block = 256
    row = lambda w: pl.BlockSpec((block, w), lambda i, s: (i, 0))
    vec = pl.BlockSpec((1, width), lambda i, s: (0, 0))
    parts = [*mine, *other]
    return call(
        functools.partial(mix_out_kernel, local, total), "mix_out", (info,), (total // block,),
        [*parts, weight, bias, x, gain, cond],
        [row(a.shape[1]) for a in parts]
        + [
            pl.BlockSpec(weight.shape, lambda i, s: (0, 0)),
            vec, row(width), vec, pl.BlockSpec(cond.shape, lambda i, s: (0, 0)),
        ],
        (sds((total, width), BF),) * 3, (row(width),) * 3,
        flops=2 * total * width * width,
    )


def raise_kernel(info_ref, act_ref, w_ref, bias_ref, hid_ref, der_ref):
    raised = nn(act_ref[...], w_ref[...]) + bias_ref[...]
    scaled = raised * 0.5**0.5
    half = 0.5 * lax.erf(scaled) + 0.5
    hid_ref[...] = (raised * half).astype(BF)
    slope = half + (raised * (2.0 * math.pi) ** -0.5) * jnp.exp2(scaled * scaled * -math.log2(math.e))
    der_ref[...] = slope.astype(BF)


def raise_up(info, act, weight, bias, block):
    total, width = act.shape
    units = weight.shape[1]
    col = pl.BlockSpec((total, block), lambda j, s: (0, j))
    return call(
        raise_kernel, "raise_up", (info,), (units // block,),
        [act, weight, bias],
        [
            pl.BlockSpec((total, width), lambda j, s: (0, 0)),
            pl.BlockSpec((width, block), lambda j, s: (0, j)),
            pl.BlockSpec((1, block), lambda j, s: (0, j)),
        ],
        (sds((total, units), BF),) * 2, (col, col),
        flops=2 * total * width * units,
    )


def weight_gradient_kernel(which, per, n, wide, info_ref, *refs):
    count = max(which) + 1
    lhs, refs = refs[: count * per], refs[count * per :]
    rhs, outs = refs[: len(which) * wide], refs[len(which) * wide :]

    def left(k):
        blocks = [ref[...] for ref in lhs[k * per : (k + 1) * per]]
        return blocks[0] if per == 1 else jnp.concatenate(blocks, axis=1)

    def write(out, rhs):
        first = 0
        for k, ref in zip(which, rhs, strict=True):
            w = ref.shape[1]
            out[:, first : first + w] = tn_dot(left(k), ref[...]).astype(BF)
            first += w

    for group, out in enumerate(outs):
        if wide > 1:
            write(out, rhs[group::wide])
        else:
            pl.when(pl.program_id(0) // n == group)(lambda out=out: write(out, rhs))


def weight_gradient(info, parts, n, mb, row, col, groups, wide, name):
    total, height = parts[0][0].shape
    width = sum(part[3] for part in parts)
    if mb % 128 or any(part[3] % 128 for part in parts):
        results = []
        for g in range(groups):
            sliced = [
                (l, lax.dynamic_slice_in_dim(r, (f(info) + col(g, info)) * w, w, 1), lambda s: 0, w)
                for l, r, f, w in parts
            ]
            every = height // 128
            (whole,) = weight_gradient(info, sliced, every, 128, lambda k, g, s: k, lambda g, s: 0, 1, False, name)
            rows = jnp.stack([jnp.asarray(row(k, g, info), jnp.int32) for k in range(n)])
            results.append(whole.reshape(height // mb, mb, width)[rows].reshape(n * mb, width))
        return results
    lhs = []
    for part in parts:
        if not any(part[0] is a for a in lhs):
            lhs.append(part[0])
    which = [next(k for k, a in enumerate(lhs) if a is part[0]) for part in parts]
    per = 2 if mb < 256 and n % 2 == 0 else 1
    steps = n // per
    together = groups if wide else 1
    group = (lambda i: 0) if wide else (lambda i: i // steps)
    return call(
        functools.partial(weight_gradient_kernel, which, per, steps, together), name, (info,),
        (steps * groups // together,),
        [a for a in lhs for _ in range(per)] + [part[1] for part in parts for _ in range(together)],
        [
            pl.BlockSpec((total, mb), lambda i, s, p=p: (0, row(i % steps * per + p, group(i), s)))
            for _ in lhs
            for p in range(per)
        ]
        + [
            pl.BlockSpec(
                (total, part[3]), lambda i, s, f=part[2], g=g: (0, f(s) + col(g if wide else group(i), s))
            )
            for part in parts
            for g in range(together)
        ],
        (sds((n * mb, width), BF),) * groups,
        tuple(
            pl.BlockSpec((per * mb, width), lambda i, s, g=g: (i if wide else jnp.clip(i - g * steps, 0, steps - 1), 0))
            for g in range(groups)
        ),
        flops=2 * total * n * mb * width * groups,
    )


def add_pick_kernel(count, info_ref, *refs):
    outs = refs[-(len(refs) // (count + 1)) :]
    for k, out in enumerate(outs):
        out[...] = sum(ref[...].astype(F32) for ref in refs[k * count : (k + 1) * count]).astype(BF)


def add_pick(info, arrays, parts, picks, columns=False):
    rows, width = arrays[0].shape
    rows, width = (rows, width // parts) if columns else (rows // parts, width)
    place = (lambda k: (0, k)) if columns else (lambda k: (k, 0))
    out = pl.BlockSpec((rows, width), lambda i, s: (0, 0))
    return call(
        functools.partial(add_pick_kernel, len(arrays)), "add_pick", (info,), (1,), [*arrays] * len(picks),
        [pl.BlockSpec((rows, width), lambda i, s, f=f: place(f(s))) for f in picks for _ in arrays],
        (sds((rows, width), BF),) * len(picks), (out,) * len(picks), flops=rows * width,
    )


def raise_back_kernel(info_ref, g_ref, w_ref, der_ref, out_ref, sum_ref):
    back = (nt(g_ref[...], w_ref[...]) * der_ref[...].astype(F32)).astype(BF)
    out_ref[...] = back
    sum_ref[...] = jnp.sum(back.astype(F32), axis=0, keepdims=True)


def raise_back(info, g, weight, der, block):
    total, width = g.shape
    units = weight.shape[0]
    col = pl.BlockSpec((total, block), lambda j, s: (0, j))
    return call(
        raise_back_kernel, "raise_back", (info,), (units // block,),
        [g, weight, der],
        [pl.BlockSpec((total, width), lambda j, s: (0, 0)), pl.BlockSpec((block, width), lambda j, s: (j, 0)), col],
        (sds((total, units), BF), sds((1, units), F32)),
        (col, pl.BlockSpec((1, block), lambda j, s: (0, j))),
        flops=2 * total * width * units,
    )


def rows_product_kernel(transposed, index_ref, lhs_ref, w_ref, out_ref):
    out_ref[...] = (nt if transposed else nn)(lhs_ref[...], w_ref[...]).astype(BF)


def rows_product(info, lhs, weight, n, block, row, transposed, name):
    depth = lhs.shape[1]
    width = weight.shape[0] if transposed else weight.shape[1]
    return call(
        functools.partial(rows_product_kernel, transposed), name, (info,), (n,),
        [lhs, weight],
        [pl.BlockSpec((block, depth), lambda i, s: (row(i, s), 0)), pl.BlockSpec(weight.shape, lambda i, s: (0, 0))],
        sds((n * block, width), BF),
        pl.BlockSpec((block, width), lambda i, s: (i, 0)),
        flops=2 * n * block * depth * width,
    )


def lower_kernel(local, total, info_ref, a_ref, b_ref, res_ref, bias_ref, out_ref):
    rows = out_ref.shape[0]
    first = (info_ref[HALF] * pl.num_programs(0) + pl.program_id(0)) * rows
    live = live_column(rows, first, info_ref, local, total)
    branch = a_ref[...].astype(F32) + b_ref[...].astype(F32) + bias_ref[...]
    out_ref[...] = (res_ref[...].astype(F32) + jnp.where(live, branch, 0.0)).astype(BF)


def add_branch(info, a, b, residual, bias, local):
    total, width = residual.shape
    block = 256
    n = total // 2 // block
    row = pl.BlockSpec((block, width), lambda i, s: (i, 0))
    return call(
        functools.partial(lower_kernel, local, total), "add_branch", (info,), (n,),
        [a, b, residual, bias],
        [row, row, pl.BlockSpec((block, width), lambda i, s: (s[HALF] * n + i, 0)), pl.BlockSpec((1, width), lambda i, s: (0, 0))],
        sds((total // 2, width), BF), row, flops=total * width, room=ROOM,
    )


def norm_back(g, v, gain, scale):
    normal, inverse = norm_rows(v)
    e = g * (gain * (1.0 + scale))
    grad = inverse * (
        e - jnp.mean(e, axis=-1, keepdims=True) - normal * jnp.mean(e * normal, axis=-1, keepdims=True)
    )
    return grad, jnp.sum(g * normal, axis=0, keepdims=True), jnp.sum(g, axis=0, keepdims=True)


def accumulate(sum_ref, parts):
    block = jnp.concatenate(parts, axis=0)

    @pl.when(pl.program_id(0) == 0)
    def _():
        sum_ref[...] = block

    @pl.when(pl.program_id(0) > 0)
    def _():
        sum_ref[...] += block


def dense_norm_back_kernel(local, total, info_ref, a1_ref, a2_ref, b1_ref, b2_ref, res_ref, cot_ref, gain_ref, cond_ref, w_ref, gres_ref, gatt_ref, gmix_ref, sum_ref):
    rows = res_ref.shape[0]
    live = live_column(rows, pl.program_id(0) * rows, info_ref, local, total).astype(F32)
    early = pl.program_id(0) < pl.num_programs(0) // 2
    g = jnp.where(early, a1_ref[...].astype(F32) + b1_ref[...].astype(F32), a2_ref[...].astype(F32) + b2_ref[...].astype(F32))
    grad, by_normal, plain = norm_back(g, res_ref[...].astype(F32), gain_ref[...], cond_ref[2:3, :])
    g_residual = cot_ref[...].astype(F32) + grad
    gres_ref[...] = g_residual.astype(BF)
    g_attend = (live * g_residual).astype(BF)
    gatt_ref[...] = g_attend
    gmix_ref[...] = nt(g_attend, w_ref[...]).astype(BF)
    bias = jnp.sum(g_attend.astype(F32), axis=0, keepdims=True)
    accumulate(sum_ref, [by_normal, plain, bias, jnp.zeros((5, bias.shape[1]), F32)])


def dense_norm_back(info, a, b, residual, cot, gain, cond, weight, local):
    total, width = residual.shape
    half = weight.shape[0] // 2
    block = 256
    row = lambda w: pl.BlockSpec((block, w), lambda i, s: (i, 0))
    n = total // block // 2
    first = pl.BlockSpec((block, width), lambda i, s: (jnp.minimum(i, n - 1), 0))
    second = pl.BlockSpec((block, width), lambda i, s: (jnp.maximum(i - n, 0), 0))
    return call(
        functools.partial(dense_norm_back_kernel, local, total), "dense_norm_back", (info,), (total // block,),
        [*a, *b, residual, cot, gain, cond, weight],
        [
            first, second, first, second, row(width), row(width),
            pl.BlockSpec((1, width), lambda i, s: (0, 0)),
            pl.BlockSpec(cond.shape, lambda i, s: (0, 0)),
            pl.BlockSpec((half, width), lambda i, s: (s[CORE], 0)),
        ],
        (sds((total, width), BF), sds((total, width), BF), sds((total, half), BF), sds((8, width), F32)),
        (row(width), row(width), row(half), pl.BlockSpec((8, width), lambda i, s: (0, 0))),
        flops=2 * total * width * half, room=ROOM,
    )


def project_back_kernel(count, n, info_ref, *refs):
    lhs, weights, outs = refs[:-5], refs[-5:-2], refs[-2:]
    total = None
    for k in range(3):
        first = 0
        for m in range(count):
            ref = lhs[k * count + m]
            w = ref.shape[1]
            term = nt(ref[...], weights[k][:, first : first + w])
            total = term if total is None else total + term
            first += w
    for half, out in enumerate(outs):

        @pl.when(pl.program_id(0) // n == half)
        def _():
            out[...] = total.astype(BF)


def project_back(info, parts, weight):
    width, half = weight.shape[0], weight.shape[1] // 6
    total = parts[0][0].shape[0]
    block = 256
    n = total // block // 2
    lhs = [part[m] for m in range(3) for part in parts]
    return call(
        functools.partial(project_back_kernel, len(parts), n), "project_back", (info,), (2 * n,),
        lhs + [weight] * 3,
        [
            pl.BlockSpec((block, a.shape[1]), lambda i, s: (lax.rem(s[HALF] + 1 + i // n, 2) * n + i % n, 0))
            for a in lhs
        ]
        + [pl.BlockSpec((width, half), lambda i, s, m=m: (0, 2 * m + s[CORE])) for m in range(3)],
        (sds((n * block, width), BF),) * 2,
        tuple(pl.BlockSpec((block, width), lambda i, s, g=g: (jnp.clip(i - g * n, 0, n - 1), 0)) for g in range(2)),
        flops=6 * total * half * width, room=ROOM,
    )


def attend_norm_back_kernel(info_ref, a_ref, b_ref, x_ref, gres_ref, gain_ref, cond_ref, out_ref, sum_ref):
    g = a_ref[...].astype(F32) + b_ref[...].astype(F32)
    grad, by_normal, plain = norm_back(g, x_ref[...].astype(F32), gain_ref[...], cond_ref[0:1, :])
    out_ref[...] = (gres_ref[...].astype(F32) + grad).astype(BF)
    accumulate(sum_ref, [by_normal, plain, jnp.zeros((6, plain.shape[1]), F32)])


def attend_norm_back(info, a, b, x, g_residual, gain, cond):
    width = x.shape[1]
    block = 256
    n = a.shape[0] // block
    plain = pl.BlockSpec((block, width), lambda i, s: (i, 0))
    picked = pl.BlockSpec((block, width), lambda i, s: (s[HALF] * n + i, 0))
    return call(
        attend_norm_back_kernel, "attend_norm_back", (info,), (n,),
        [a, b, x, g_residual, gain, cond],
        [
            plain, plain, picked, picked,
            pl.BlockSpec((1, width), lambda i, s: (0, 0)),
            pl.BlockSpec(cond.shape, lambda i, s: (0, 0)),
        ],
        (sds((n * block, width), BF), sds((8, width), F32)),
        (plain, pl.BlockSpec((8, width), lambda i, s: (0, 0))),
        flops=n * block * width, room=ROOM,
    )


def finish_kernel(places, counts, info_ref, *refs):
    outs = refs[sum(counts) :]
    groups, at = [], 0
    for count in counts:
        groups.append(refs[at : at + count])
        at += count
    first = info_ref[CORE] == 0
    for out, group, source, width, target, stride in places:
        refs_ = groups[group]
        columns = slice(source, source + width)
        mine, other = [sum(r[side, :, columns].astype(F32) for r in refs_) for side in range(2)]
        outs[out][:, target : target + width] = jnp.where(first, mine, other)
        outs[out][:, target + stride : target + stride + width] = jnp.where(first, other, mine)


def finish(info, groups, places, widths):
    r = groups[0][0].shape[1]
    ins = [a for group in groups for a in group]
    outs = tuple(sds((r, w), F32) for w in widths)
    return call(
        functools.partial(finish_kernel, places, [len(g) for g in groups]), "finish", (info,), (1,),
        ins, [pl.BlockSpec(a.shape, lambda i, s: (0, 0, 0)) for a in ins],
        outs, tuple(pl.BlockSpec(a.shape, lambda i, s: (0, 0)) for a in outs), flops=r * sum(widths),
    )


def sinus_angles(time, features, width):
    halfway = width // 2
    rates = jnp.exp(-math.log(10000.0) * (features % halfway).astype(F32) / halfway)
    angles = time[:, None] * rates[None, :]
    return jnp.where((features < halfway)[None, :], jnp.sin(angles), jnp.cos(angles))


def body(
    dp, seq,
    tokens, time_index, lengths, time_weight, time_bias, attend_gain, query_key_value_weight,
    attention_output_weight, attend_bias, dense_gain, feedforward_up_matrix, up_bias,
    feedforward_down_matrix, down_bias, cotangent,
):
    nl, tl, d = tokens.shape
    ff = feedforward_up_matrix.shape[1]
    total = tl * seq
    chips = dp // 2
    nz = dp // 4
    i = lax.axis_index("dp")
    y = lax.axis_index("seq")
    core = i % 2
    x = (i // 2) % 2
    z = i // 4
    h = tl // 2
    half = d // 2
    fb, nb = ff // dp, dp // 2

    entry = lax.broadcasted_iota(jnp.int32, (16,), 0)
    places = {CORE: core, OFFSET: y * tl, NEAR: core == y // nl, FAR: core == 0, X: x, Z: z, HALF: core != y // nl, Y: y}
    info = jnp.zeros((16,), jnp.int32)
    for n, v in places.items():
        info = jnp.where(entry == n, jnp.asarray(v, jnp.int32), info)
    order = Order(info)
    run = order.run


    core_swap = lambda a: lax.ppermute(a, "dp", [(n, n ^ 1) for n in range(dp)])
    x_swap = lambda a: lax.ppermute(a, "dp", [(n, n ^ 2) for n in range(dp)])

    def y_shift(a, k):
        return lax.ppermute(a, "seq", [(n, (n + k) % seq) for n in range(seq)])

    def travel(k):
        pairs = []
        for chip in range(chips):
            for s in range(seq):
                target = (s + k) % seq
                pairs.append(((chip * 2 + target // nl) * seq + s, chip * 2 * seq + target))
        return pairs


    def take(a, axis, n):
        return lax.dynamic_index_in_dim(a, n, axis, keepdims=False)

    def pick(a, index):
        return lax.dynamic_index_in_dim(a, index, 0, keepdims=False)

    def in_core_order(mine, other):
        return jnp.where(core == 0, mine, other), jnp.where(core == 0, other, mine)

    def fetch_near(a):
        mine = pick(a, y % nl)
        return mine, core_swap(mine)

    def fetch_far(a):
        got = [lax.ppermute(pick(a, (y + k) % seq % nl), ("dp", "seq"), travel(k)) for k in range(1, seq)]
        return got[0] if len(got) == 1 else jnp.concatenate(got, axis=0)

    def give_back(a):
        got = [a[0]]
        for k in range(1, seq):
            pairs = []
            for chip in range(chips):
                for s in range(seq):
                    owner = s // nl
                    source = owner if k < seq // 2 else 1 - owner
                    pairs.append(((chip * 2 + source) * seq + s, (chip * 2 + owner) * seq + (s - k) % seq))
            got.append(lax.ppermute(a[k % (seq // 2)], ("dp", "seq"), pairs))
        if nl == 1 and seq == 2:
            return lambda: jnp.where(core == y, *order.after(got))[None]
        return lambda: jnp.stack([pick(jnp.stack(got), (core * nl + j - y) % seq) for j in range(nl)])

    steps = nz.bit_length() - 1

    def z_swap(a, j):
        return lax.ppermute(a, "dp", [(n, n ^ (4 << j)) for n in range(dp)])

    def two_way(own, weight, swap):
        return (2, weight, own, [lambda s: 1 - own(s)], [swap])

    def z_way(j):
        return two_way(lambda s: (s[Z] >> j) & 1, 2 << j, functools.partial(z_swap, j=j))

    def z_shift(a, k):
        return lax.ppermute(a, "dp", [(n, (n // 4 + k) % nz * 4 + n % 4) for n in range(dp)])

    x_way = two_way(lambda s: s[X], 1, x_swap)
    z_all = (
        nz, 2, lambda s: s[Z],
        [lambda s, k=k: lax.rem(s[Z] + k, nz) for k in range(1, nz)],
        [functools.partial(z_shift, k=k) for k in range(1, nz)],
    )

    class Chain:
        def __init__(self, parts, mb, name, ways, along=False):
            free = ways if along else ways[1:]
            n = math.prod(way[0] for way in free)

            def row(k, group, s):
                place = 0
                for count, weight, _, _, _ in reversed(free):
                    place = place + k % count * weight
                    k = k // count
                if not along:
                    _, weight, own, _, _ = ways[0]
                    bit = own(s)
                    place = place + (bit + (1 - group) * (1 - 2 * bit)) * weight
                return place

            if along:
                parts = [(l, r, lambda s, f=f: f(s) * seq, w // seq) for l, r, f, w in parts]
                col = lambda group, s: lax.rem(s[Y] + group + 1, seq)
                out = run(weight_gradient, parts, n, mb, row, col, seq, True, name)
                self.came = [y_shift(a, k + 1) for k, a in enumerate(out[:-1])]
            else:
                out = run(weight_gradient, parts, n, mb, row, lambda group, s: 0, 2, False, name)
                self.came = [ways[0][4][0](out[0])]
            self.kept = out[-1]
            self.ways = list(free)

        def hop(self):
            count, _, own, away, sends = self.ways.pop(0)
            out = run(add_pick, [self.kept, *self.came], count, [*away, own])
            self.came = [send(a) for send, a in zip(sends, out, strict=False)]
            self.kept = out[-1]

        def hop_y(self):
            picks = [lambda s, k=k: lax.rem(s[Y] + k, seq) for k in range(1, seq)] + [lambda s: s[Y]]
            out = run(add_pick, [self.kept, *self.came], seq, picks, True)
            self.came = [y_shift(a, k + 1) for k, a in enumerate(out[:-1])]
            self.kept = out[-1]

        def last(self):
            return run(add_pick, [self.kept, *self.came], 2, [lambda s: 1 - s[CORE], lambda s: s[CORE]])


    far = fetch_far(tokens)
    mine = jnp.stack([pick(time_index, y % nl), pick(lengths, y % nl)])
    time, length = jnp.where(core == y // nl, mine, core_swap(mine))
    near = fetch_near(tokens)
    own_up_bias = take(up_bias.reshape(nb, 2, fb), 1, core).reshape(1, nb * fb)
    order.info = jnp.where(entry == LENGTH, length, order.info)
    time = time.astype(F32)[None]
    table = sinus_angles(order.after(time), jnp.arange(d), d).astype(BF)
    cond = order.after((jnp.dot(table, time_weight, preferred_element_type=F32) + time_bias).reshape(4, d))
    gain1, gain2 = attend_gain[None, :], dense_gain[None, :]

    weight_up, weight_down = run(own_units, feedforward_up_matrix, feedforward_down_matrix, fb)
    far = order.after(far)
    far_other = core_swap(far)
    cotangent = order.after(cotangent)
    near_cot = fetch_near(cotangent)
    far_cot = fetch_far(cotangent)
    full, act1, qkv = run(project, near, (far, far_other), gain1, cond, query_key_value_weight)
    pairs = half // (2 * HD)
    share = pairs // 2
    attended, swapped = [], []
    for n in range(2):
        attended.append(run(attend_forward, qkv, tl, n * share, share))
        swapped.append(core_swap(attended[n][0]))
        far_cot = order.after(far_cot) if n == 0 else far_cot
    cot, g_dense, g_down_bias = run(assemble, near_cot, (far_cot, core_swap(far_cot)), tl)
    mixture, residual, act2 = run(
        mix_out, [a[0] for a in attended], swapped, attention_output_weight, attend_bias[None, :],
        full, gain2, cond, tl,
    )
    hidden, slope = run(raise_up, act2, weight_up, own_up_bias, 2 * fb)

    rows_of = d // chips
    zero = lambda s: 0
    zs = [z_way(j) for j in range(steps)]
    down = Chain([(hidden, g_dense, zero, d)], fb, "down_gradient", [x_way, *zs], along=True)
    g_raised, g_up_bias = run(raise_back, g_dense, weight_down, slope, 2 * fb)
    quarters = max(2, total // 256)
    g_act2, g_act2_other = [], []
    for n in range(2):
        place = lambda i, s, n=n: n * (quarters // 2) + i
        g_act2.append(run(rows_product, g_raised, weight_up, quarters // 2, total // quarters, place, True, "raise_input_back"))
        g_act2_other.append(core_swap(g_act2[n]))
    up = Chain([(act2, g_raised, zero, fb * nb)], rows_of, "up_gradient", [x_way, *zs])
    g_residual, g_attend, g_mixture, sums2 = run(
        dense_norm_back, g_act2, g_act2_other, residual, cot, gain2, cond, attention_output_weight, tl
    )

    def input_gradients(n):
        back = run(attend_backward, qkv, g_mixture, *attended[n], tl, n * share, share)
        return back, [(act1, a, zero, a.shape[1]) for a in back]

    back1, in1 = input_gradients(0)
    in1 = Chain(in1 + [(mixture, g_attend, lambda s: s[CORE], half)], rows_of, "in_gradient", [zs[0], x_way, *zs[1:]])
    down.hop()
    back2, in2 = input_gradients(1)
    g_act1_theirs, g_act1 = run(project_back, [back1, back2], query_key_value_weight)
    g_act1_theirs = core_swap(g_act1_theirs)
    in2 = Chain(in2, rows_of, "in_gradient", [x_way, z_all])
    up.hop_y()
    down.hop()
    in1.hop()
    g_tokens, sums1 = run(attend_norm_back, g_act1, g_act1_theirs, full, g_residual, gain1, cond)
    gradient_tokens = give_back(g_tokens.reshape(-1, tl, d))

    once = jnp.where(core == 0, 1.0, 0.0)
    scales = 1.0 + cond
    up_sum = g_up_bias.reshape(nb, 1, fb)
    up_sum = jnp.concatenate(in_core_order(up_sum, jnp.zeros_like(up_sum)), axis=1).reshape(ff // d, d)
    level = jnp.where(lax.broadcasted_iota(jnp.int32, (1, d), 1) == 0, time // 256.0, time % 256.0)
    pack = jnp.concatenate(
        [
            sums1[0:1] * gain1,
            sums1[1:2],
            once * sums2[0:1] * gain2,
            once * sums2[1:2],
            once * level,
            sums1[0:1] * scales[0:1],
            once * sums2[0:1] * scales[2:3],
            once * sums2[2:3],
            once * g_down_bias[0:1],
            up_sum,
        ]
    )
    n = max(1, total // 2 // 256)
    n = 1
    own_half = (n, total // 2 // n, lambda i, s: s[HALF] * n + i)
    their_half = (n, total // 2 // n, lambda i, s: (1 - s[HALF]) * n + i)
    pack = order.after(pack)
    swapped = core_swap(pack)

    def pack_hop(rows_each, sums, swaps):
        packs = [swap(jnp.concatenate([rows_each, sums])) for swap in swaps]
        count = rows_each.shape[0]

        def arrive():
            came = order.after(packs)
            rows = jnp.concatenate([rows_each] + [p[:count] for p in came])
            return order.after((rows, sum([p[count:].astype(F32) for p in came], sums.astype(F32)).astype(BF)))

        return arrive

    y_ways = [functools.partial(y_shift, k=k) for k in range(1, seq)]
    pack = pack + order.after(swapped)
    packed = pack_hop(*order.after((pack[:5].astype(BF), pack[5:].astype(BF))), [x_swap])
    in2.hop()
    up.hop()
    branch_theirs = core_swap(run(rows_product, hidden, weight_down, *their_half, False, "lower"))
    packed = pack_hop(*packed(), y_ways)
    branch = run(rows_product, hidden, weight_down, *own_half, False, "lower")
    for _ in range(steps - 1):
        down.hop()
        in1.hop()
    for _ in range(steps - 1):
        up.hop()
    packed = pack_hop(*packed(), [functools.partial(z_swap, j=0)])
    result = give_back(run(add_branch, branch, branch_theirs, residual, down_bias[None, :], tl).reshape(-1, tl, d))
    for j in range(1, steps):
        packed = pack_hop(*packed(), [functools.partial(z_swap, j=j)])
    gradient_tokens = order.after(gradient_tokens())

    def core_shared(chain):
        theirs, mine = chain.last()
        return mine, core_swap(theirs)

    def shared(mine, other):
        both = order.after(jnp.stack([mine, order.after(other)]))
        return [both] + [y_shift(both, k) for k in range(1, seq)]

    in2_all = core_shared(in2)
    up_all = core_shared(up)
    in1_all = core_shared(in1)
    in2_all = shared(*in2_all)
    up_all = shared(*up_all)
    down_parts = order.after([down.kept, *down.came])
    down_mine = order.after(sum(a.astype(F32) for a in down_parts).astype(BF))
    down_all = [down_mine] + [y_shift(down_mine, k) for k in range(1, seq)]
    in1_all = shared(*in1_all)
    rows_each, sums = packed()
    sums = sums.astype(F32)
    result = order.after(result())
    order.open = True
    down_all = jnp.stack(down_all)
    gradient_down = jnp.concatenate([pick(down_all, (y - n) % seq) for n in range(seq)], axis=1).astype(F32)
    up_all = [pick(jnp.stack(up_all), (y - n) % seq) for n in range(seq)]
    up_all = [jnp.concatenate(up_all, axis=2)]
    (gradient_up,) = run(finish, [up_all], [(0, 0, n * fb, fb, 2 * n * fb, fb) for n in range(nb)], [ff])
    w = share * 2 * HD
    spots = [(0, n, t * w, w, (2 * t * 2 + n) * w, 2 * w) for t in range(3) for n in range(2)]
    gradient_in, gradient_out = run(
        finish, [in1_all, in2_all], spots + [(1, 0, 3 * w, half, 0, half)], [3 * d, d]
    )
    gathered = rows_each.reshape(-1, 5, d).astype(F32)
    g_cond = gathered[:, 0:4].reshape(-1, 4 * d)
    own_features = i * (d // dp) + jnp.arange(d // dp)
    times = gathered[:, 4, 0] * 256.0 + gathered[:, 4, 1]
    features = sinus_angles(times, own_features, d).astype(BF)
    gradient_time = lax.dot_general(
        features.astype(F32), g_cond, (((0,), (0,)), ((), ())), precision=lax.Precision.HIGHEST
    )
    g_time_bias = jnp.sum(g_cond, axis=0)
    part = lambda v: lax.dynamic_index_in_dim(v.reshape(dp, -1), i, 0, keepdims=False)
    return (
        result,
        gradient_tokens,
        gradient_time,
        part(g_time_bias),
        part(sums[0]),
        gradient_in,
        gradient_out,
        part(sums[2]),
        part(sums[1]),
        gradient_up,
        part(sums[4:]),
        gradient_down,
        part(sums[3]),
    )


def solution(mesh):
    whole = P()
    rows = P("dp", "seq", None)
    return jax.shard_map(
        functools.partial(body, mesh.shape["dp"], mesh.shape["seq"]),
        mesh=mesh,
        in_specs=(rows, P("dp"), P("dp"), *(whole,) * 11, rows),
        out_specs=(
            rows, rows, P("dp", None), P("dp"), P("dp"), P("dp", None), P("dp", None),
            P("dp"), P("dp"), P("dp", None), P("dp"), P("dp", None), P("dp"),
        ),
        check_vma=False,
    )
```
